128 devices in a mesh: lon: 8 (over x, y_hi), lat: 16 (over z, y_lo, core).
Axes of the slice: x: 4, y: 4 (y_hi: 2, y_lo: 2; y = y_hi * 2 + y_lo), z: 4, core: 2. Of those that a mesh axis runs over, the one named last changes fastest.
Arguments:
- atmos: float32 [4, 16, 1024, 2048], P(None, None, 'lat', 'lon'), may hold values from -6 to 6
- previous_surface_heat: float32 [1024, 2048], P('lat', 'lon'), may hold values from -4 to 4
- insolation: float32 [1024, 2048], P('lat', 'lon'), may hold values from 0 to 2
- regrid_weight: bfloat16 [16384, 3, 128, 128], P(('lon', 'lat')), may hold values from -0.3125 to 0.3125
- destination_device: int32 [16384, 3], P(('lon', 'lat')), may hold values from 0 to 127, as said below
- destination_tile: int32 [16384, 3], P(('lon', 'lat')), may hold values from 0 to 95
- atmosphere_mixer: float32 [16, 16], replicated, may hold values from -1.5 to 1.5
- ocean: float32 [4, 16, 768, 2048], P(None, None, 'lat', 'lon'), may hold values from -6 to 6
- water_mask: int32 [768, 2048], P('lat', 'lon'), may hold values 0 or 1
- seam_column_index: int32 [2048], P('lon'), may hold values from 0 to 2047, as said below
- marine_mixer: float32 [16, 16], replicated, may hold values from -1.5 to 1.5
Outputs:
- atmosphere_final: float32 [4, 16, 1024, 2048], P(None, None, 'lat', 'lon')
- exchanged_surface_heat: float32 [1024, 2048], P('lat', 'lon')
- marine_final: float32 [4, 16, 768, 2048], P(None, None, 'lat', 'lon')
- marine_surface_flux: float32 [8, 768, 2048], P(None, 'lat', 'lon')
The draws below stay inside these ranges and needn't reach their ends.
Inputs may be any that keep to these rules, and one draw needn't show every extreme that they name: `destination_device`: each row names 3 different owners; each owner's lon index is within one of the lon index of the tile's own block (cyclically over 8) and its lat index within one of the block's lat index. seam_column_index[c] = (p - c) mod 2048 for one p of the draw, so the map is its own inverse.
All inputs are finite; a program needn't handle non-finite values. No bound on the sum of `water_mask` on one device may be relied on, other than what follows from the above.
Results may differ from the reference program's by a relative error of at most 0.003.
Values may be sent and summed in bfloat16 or wider, within the bound.
A program may use at most 192 MiB of HBM per device.

```python
import jax
import jax.numpy as jnp
from jax import lax

LEV = 16
TILE_CELLS = 128
K = 3
NFLUX = 8
LATITUDE_ROWS = 64
LONGITUDE_COLUMNS = 256
OCEAN_ROW_NUM = 48
OCEAN_COLUMN_NUM = 256
ATILES = 128
OCEAN_TILE_COUNT = 96
GLOBAL_LAT_ROWS = 1024
GLOBAL_LON_COLS = 2048
NY = 768
NX = 2048
NTA = 16384
N_LON = 8
N_LAT = 16
DEVICES = 128


def draw_seam_column_index(key, part):
    key = jax.random.fold_in(key, 11)
    pole = jax.random.randint(key, (), 0, NX)
    return jnp.mod(pole - jnp.arange(NX, dtype=jnp.int32), NX).astype(jnp.int32)


def draw_destination_device(key, part):
    key = jax.random.fold_in(key, 5)
    key_order, key_start = jax.random.split(key)
    device_ids = jnp.arange(DEVICES, dtype=jnp.int32)
    lon_ids = device_ids // N_LAT
    lat_ids = device_ids % N_LAT
    candidate = jnp.arange(9, dtype=jnp.int32)
    lon_step = candidate // 3 - 1
    lat_step = candidate % 3 - 1
    lat_target = lat_ids[:, None] + lat_step[None, :]
    valid = jnp.logical_and(lat_target >= 0, lat_target < N_LAT)
    owners = jnp.mod(lon_ids[:, None] + lon_step[None, :], N_LON) * N_LAT + jnp.clip(lat_target, 0, N_LAT - 1)
    noise = jax.random.randint(key_order, (DEVICES, 9), 0, 50)
    score = jnp.where(valid, 0, 1000) + noise * 9 + candidate[None, :]
    order = jnp.argsort(score, axis=1)
    ordered = jnp.take_along_axis(owners, order, axis=1)
    count = jnp.sum(valid.astype(jnp.int32), axis=1)
    start = jnp.mod(jax.random.randint(key_start, (DEVICES,), 0, 9), count)
    rows = jnp.arange(ATILES, dtype=jnp.int32)[None, :, None] * K
    cols = jnp.arange(K, dtype=jnp.int32)[None, None, :]
    position = jnp.mod(start[:, None, None] + rows + cols, count[:, None, None])
    selected_entries = jnp.take_along_axis(ordered, position.reshape(DEVICES, ATILES * K), axis=1)
    return selected_entries.reshape(NTA, K).astype(jnp.int32)


def set_ends(values, rng, low, top_value):
    spot = [jax.random.randint(jax.random.fold_in(rng, axis), (), 0, length) for axis, length in enumerate(values.shape)]
    main_axis = values.shape.index(max(values.shape))
    neighbour = spot[:main_axis] + [(spot[main_axis] + 1) % values.shape[main_axis]] + spot[main_axis + 1:]
    return values.at[tuple(spot)].set(low).at[tuple(neighbour)].set(top_value)


def levels(rng, dims, cuts, smallest, high):
    level, own = 1.0, jax.random.fold_in(rng, 6)
    for dim, blocks in cuts:
        heights = jnp.exp(jax.random.uniform(jax.random.fold_in(own, dim), (blocks,), jnp.float32, smallest / len(cuts), high / len(cuts)))
        level = level * jnp.repeat(heights, dims[dim] // blocks).reshape([-1 if axis == dim else 1 for axis in range(len(dims))])
    return level


def gaussian(rng, shape, deviation, most, cuts=(), kind=jnp.bfloat16):
    drawn = deviation * jax.random.normal(rng, shape, jnp.float32)
    if cuts:
        drawn = drawn * levels(rng, shape, cuts, -0.22, 0.18)
    return jnp.clip(drawn, -most, most).astype(kind)


def setup_inputs(seed: int = 0) -> dict:
    keys = jax.random.split(jax.random.key(seed), 12)
    return {
        "atmos": gaussian(keys[0], (4, LEV, GLOBAL_LAT_ROWS, GLOBAL_LON_COLS), 1.0, 6.0, ((2, 16), (3, 8)), jnp.float32),
        "previous_surface_heat": gaussian(keys[1], (GLOBAL_LAT_ROWS, GLOBAL_LON_COLS), 1.0, 4.0, ((0, 16), (1, 8)), jnp.float32),
        "insolation": jnp.clip(2.0 * jax.random.uniform(keys[2], (GLOBAL_LAT_ROWS, GLOBAL_LON_COLS), jnp.float32) ** levels(keys[2], (GLOBAL_LAT_ROWS, GLOBAL_LON_COLS), ((0, 16), (1, 8)), -0.2, 0.2), 0.0, 2.0),
        "regrid_weight": gaussian(keys[3], (NTA, K, TILE_CELLS, TILE_CELLS), (TILE_CELLS * K) ** -0.5, 0.3125, ((0, 128),)),
        "destination_device": draw_destination_device(jax.random.fold_in(keys[11], 71), 0),
        "destination_tile": set_ends(jax.random.randint(keys[5], (NTA, K), 0, OCEAN_TILE_COUNT), jax.random.fold_in(keys[5], 1), 0, OCEAN_TILE_COUNT - 1).astype(jnp.int32),
        "atmosphere_mixer": gaussian(keys[6], (LEV, LEV), LEV ** -0.5, 1.5, (), jnp.float32),
        "ocean": gaussian(keys[7], (4, LEV, NY, NX), 1.0, 6.0, ((2, 16), (3, 8)), jnp.float32),
        "water_mask": set_ends((jax.random.randint(keys[8], (NY, NX), 0, 10) < 7).astype(jnp.int32), jax.random.fold_in(keys[8], 1), 0, 1),
        "seam_column_index": draw_seam_column_index(jax.random.fold_in(keys[11], 71), 0),
        "marine_mixer": gaussian(keys[10], (LEV, LEV), LEV ** -0.5, 1.5, (), jnp.float32),
    }


HIGH = lax.Precision.HIGHEST

def boundary_flux_terms(atmos, previous_surface_heat, insolation):
    zonal_wind = atmos[0, -1]
    meridional_wind = atmos[1, -1]
    air_heat_level = atmos[2, -1]
    moisture_level = atmos[3, -1]
    wind_magnitude = jnp.sqrt(zonal_wind * zonal_wind + meridional_wind * meridional_wind + 1.0)
    return jnp.stack([0.8 * wind_magnitude * zonal_wind, 0.8 * wind_magnitude * meridional_wind, 0.6 * wind_magnitude * (previous_surface_heat - air_heat_level), 0.5 * wind_magnitude * (0.4 * jnp.exp(0.5 * previous_surface_heat) - moisture_level), 0.3 * (air_heat_level - previous_surface_heat) * (2.0 + jnp.tanh(air_heat_level)), insolation * (0.9 - 0.1 * jnp.tanh(moisture_level)), jax.nn.softplus(moisture_level), 0.3 * wind_magnitude * wind_magnitude])

def force_ocean(ocean, flux_terms_list, sea_fraction):
    temp = ocean[0, 0] + 0.2 * sea_fraction * (flux_terms_list[5] - flux_terms_list[2] - flux_terms_list[3] - flux_terms_list[4])
    salt = ocean[1, 0] + 0.2 * sea_fraction * (flux_terms_list[3] - flux_terms_list[6])
    vel_u = ocean[2, 0] + sea_fraction * (0.3 * flux_terms_list[0] - 0.1 * flux_terms_list[7] * ocean[2, 0])
    vel_v = ocean[3, 0] + sea_fraction * (0.3 * flux_terms_list[1] - 0.1 * flux_terms_list[7] * ocean[3, 0])
    return ocean.at[:, 0].set(jnp.stack([temp, salt, vel_u, vel_v]))

def atmos_field_step(field, mixing):
    padded = jnp.pad(field, ((0, 0), (1, 1), (0, 0)))
    lap = padded[:, :-2] + padded[:, 2:] + jnp.roll(field, 1, 2) + jnp.roll(field, -1, 2) - 4.0 * field
    advanced_state = field + 0.15 * lap
    return jnp.einsum('lm,myx->lyx', mixing, advanced_state, precision=HIGH)

def reference(atmos, previous_surface_heat, insolation, regrid_weight, destination_device, destination_tile, atmosphere_mixer, ocean, water_mask, seam_column_index, marine_mixer):
    flux_terms_list = boundary_flux_terms(atmos, previous_surface_heat, insolation).astype(jnp.bfloat16)
    shaped = flux_terms_list.reshape(NFLUX, N_LAT, LATITUDE_ROWS, N_LON, LONGITUDE_COLUMNS).transpose(3, 1, 0, 2, 4)
    flux_tiles = shaped.reshape(DEVICES, NFLUX, ATILES, TILE_CELLS).transpose(0, 2, 1, 3)
    weight_blocks = regrid_weight.reshape(DEVICES, ATILES, K, TILE_CELLS, TILE_CELLS)
    global_target = (destination_device * OCEAN_TILE_COUNT + destination_tile).astype(jnp.int32).reshape(DEVICES, ATILES, K)

    def forward(total, block):
        tiles_block, weight_block, destination_block = block
        terms = jnp.einsum('tfr,tkrc->tkfc', tiles_block.astype(jnp.float32), weight_block.astype(jnp.float32), precision=HIGH)
        return (total.at[destination_block.reshape(-1)].add(terms.reshape(-1, NFLUX, TILE_CELLS)), None)
    summed, _ = lax.scan(forward, jnp.zeros((DEVICES * OCEAN_TILE_COUNT, NFLUX, TILE_CELLS), jnp.float32), (flux_tiles, weight_blocks, global_target))
    summed = summed.reshape(N_LON, N_LAT, OCEAN_TILE_COUNT, NFLUX, TILE_CELLS).transpose(0, 1, 3, 2, 4)
    summed = summed.reshape(N_LON, N_LAT, NFLUX, OCEAN_ROW_NUM, OCEAN_COLUMN_NUM).transpose(2, 1, 3, 0, 4).reshape(NFLUX, NY, NX)
    sea_fraction = water_mask.astype(jnp.float32)
    marine_surface_flux = summed * sea_fraction
    model_state = force_ocean(ocean, marine_surface_flux, sea_fraction)
    signs = jnp.array([1.0, 1.0, -1.0, -1.0], jnp.float32)

    def ocean_field_step(args):
        field, sign = args
        north = sign * jnp.take(field[:, -1, :], seam_column_index, axis=1)
        above = jnp.concatenate([field[:, 1:], north[:, None]], axis=1)
        below = jnp.concatenate([jnp.zeros_like(field[:, :1]), field[:, :-1]], axis=1)
        lap = above + below + jnp.roll(field, 1, 2) + jnp.roll(field, -1, 2) - 4.0 * field
        advanced_state = field + 0.2 * lap
        mixed = jnp.einsum('lm,myx->lyx', marine_mixer, advanced_state, precision=HIGH)
        return jnp.where(water_mask > 0, mixed, field)
    for step in range(2):
        model_state = lax.map(ocean_field_step, (model_state, signs))
    marine_final = model_state
    marine_surface_heat = (marine_final[0, 0] * sea_fraction).astype(jnp.bfloat16)
    surface_heat_tiles = marine_surface_heat.reshape(N_LAT, OCEAN_ROW_NUM, N_LON, OCEAN_COLUMN_NUM).transpose(2, 0, 1, 3).reshape(DEVICES * OCEAN_TILE_COUNT, TILE_CELLS)

    def backward(carry, block):
        weight_block, destination_block = block
        selected_entries = jnp.take(surface_heat_tiles, destination_block, axis=0).astype(jnp.float32)
        return (carry, jnp.einsum('tkrc,tkc->tr', weight_block.astype(jnp.float32), selected_entries, precision=HIGH))
    _, sent_back = lax.scan(backward, jnp.zeros((), jnp.float32), (weight_blocks, global_target))
    exchanged_surface_heat = sent_back.reshape(N_LON, N_LAT, LATITUDE_ROWS, LONGITUDE_COLUMNS).transpose(1, 2, 0, 3).reshape(GLOBAL_LAT_ROWS, GLOBAL_LON_COLS)
    advanced_state = atmos
    for step in range(2):
        advanced_state = lax.map(lambda field: atmos_field_step(field, atmosphere_mixer), advanced_state)
    cold_heat_level = advanced_state[2, -1]
    atmosphere_final = advanced_state.at[2, -1].set(cold_heat_level + 0.5 * (exchanged_surface_heat - cold_heat_level))
    return (atmosphere_final, exchanged_surface_heat, marine_final, marine_surface_flux)
```

```python
import functools

import jax
import jax.numpy as jnp
from jax import lax
from jax.experimental import pallas as pl
from jax.experimental.pallas import tpu as pltpu
from jax.sharding import PartitionSpec as P

F32 = jnp.float32
BF = jnp.bfloat16
MESH = pl.DeviceIdType.MESH
HIGHEST = lax.Precision.HIGHEST
NT = (((1,), (1,)), ((), ()))
TN = (((0,), (0,)), ((), ()))
N_LON = 8
N_LAT = 16
STEPS = 4
MIB = 2**20


def flux_fields(u, v, ta, qa, ts, sw):
    speed = jnp.sqrt(u * u + v * v + 1.0)
    soft = jnp.maximum(qa, 0.0) + jnp.log1p(jnp.exp(-jnp.abs(qa)))
    return [
        0.8 * speed * u,
        0.8 * speed * v,
        0.6 * speed * (ts - ta),
        0.5 * speed * (0.4 * jnp.exp(0.5 * ts) - qa),
        0.3 * (ta - ts) * (2.0 + jnp.tanh(ta)),
        sw * (0.9 - 0.1 * jnp.tanh(qa)),
        soft,
        0.3 * speed * speed,
    ]


def slot_rows(owner, tile):
    lon = lax.axis_index("lon")
    lat = lax.axis_index("lat")
    lon_offset = ((owner >> 4) - lon + 1) & 7
    lat_offset = (owner & 15) - lat + 1
    return (lon_offset * 3 + lat_offset) * 96 + tile


def one_hot_slots(dd, dt, k):
    slot = slot_rows(dd[k : k + 1, :], dt[k : k + 1, :])
    rows = lax.broadcasted_iota(jnp.int32, (864, 128), 0)
    return jnp.where(slot == rows, 1.0, 0.0).astype(BF)


def out_kernel(surf, ts, sw, dd, dt, atm, oce, mask, w, send, rows, cols, corn, ft, terms, oh, tb, rbuf, cbuf):
    i = pl.program_id(0)
    tiles = w.shape[0]
    fields = atm.shape[0]

    @pl.when(i == 0)
    def _():
        vals = flux_fields(surf[0, 0], surf[1, 0], surf[2, 0], surf[3, 0], ts[...], sw[...])
        for f, val in enumerate(vals):
            val = val.astype(BF).astype(F32)
            ft[pl.ds(f, 64, stride=16), :] = val[:, :128]
            ft[pl.ds(8 + f, 64, stride=16), :] = val[:, 128:]
        for k in range(3):
            oh[:, k * 128 : (k + 1) * 128] = one_hot_slots(dd, dt, k)
        cbuf[...] = jnp.zeros_like(cbuf)
        rbuf[...] = jnp.zeros_like(rbuf)

    group = lax.broadcasted_iota(jnp.int32, (32, 128), 0)
    even = (group & 8) == 0
    for j in range(0, tiles, 4):
        t = i * tiles + j
        a = ft[pl.ds(pl.multiple_of(t * 8, 32), 32), :]
        lhs = jnp.concatenate([jnp.where(even, a, 0.0), jnp.where(even, 0.0, a)], axis=1).astype(BF)
        for h in range(2):
            q = j + 2 * h
            block = jnp.concatenate(
                [jnp.concatenate([w[q, 0], w[q, 1]], axis=1), jnp.concatenate([w[q + 1, 0], w[q + 1, 1]], axis=1)], axis=0
            )
            r = jnp.dot(lhs[16 * h : 16 * h + 16], block, preferred_element_type=F32)
            for k in range(2):
                terms[pl.ds(pl.multiple_of((k * 128 + t + 2 * h) * 8, 16), 16), :] = r[:, k * 128 : (k + 1) * 128]
        block = jnp.concatenate(
            [jnp.concatenate([w[j, 2], w[j + 2, 2]], axis=1), jnp.concatenate([w[j + 1, 2], w[j + 3, 2]], axis=1)], axis=0
        )
        r = jnp.dot(lhs, block, preferred_element_type=F32)
        at = pl.multiple_of((256 + t) * 8, 32)
        terms[pl.ds(at, 16), :] = r[:16, :128]
        terms[pl.ds(at + 16, 16), :] = r[16:, 128:]

    lane_a = lax.broadcasted_iota(jnp.int32, (64, 128), 1) >> 1
    lane_o = lax.broadcasted_iota(jnp.int32, (48, 128), 1) >> 1
    left_a, right_a = cbuf[0, 0:64, :], cbuf[1, 0:64, :]
    left_o, right_o = cbuf[0, 64:112, :], cbuf[1, 64:112, :]
    for j in range(fields):
        n = i * fields + j
        back = (2 * n + 2) & 127
        left_a = jnp.where(lane_a == n, pltpu.roll(atm[j, :, 0:128], 2 * n, 1), left_a)
        right_a = jnp.where(lane_a == n, pltpu.roll(atm[j, :, 128:256], back, 1), right_a)
        left_o = jnp.where(lane_o == n, pltpu.roll(oce[j, :, 0:128], 2 * n, 1), left_o)
        right_o = jnp.where(lane_o == n, pltpu.roll(oce[j, :, 128:256], back, 1), right_o)
        for e in range(2):
            rbuf[e, pl.ds(n, 1), :] = atm[j, e : e + 1, :]
            rbuf[2 + e, pl.ds(n, 1), :] = atm[j, 62 + e : 63 + e, :]
            rbuf[e, pl.ds(64 + n, 1), :] = oce[j, e : e + 1, :]
            rbuf[2 + e, pl.ds(64 + n, 1), :] = oce[j, 46 + e : 47 + e, :]
    cbuf[0, 0:64, :], cbuf[1, 0:64, :] = left_a, right_a
    cbuf[0, 64:112, :], cbuf[1, 64:112, :] = left_o, right_o

    @pl.when(i == pl.num_programs(0) - 1)
    def _():
        sea = mask[...].astype(F32)
        cbuf[0, 112:160, :] = sea[:, 0:128]
        cbuf[1, 112:160, :] = sea[:, 128:256]
        for e in range(2):
            rbuf[e, 128:129, :] = sea[e : e + 1, :]
            rbuf[2 + e, 128:129, :] = sea[46 + e : 47 + e, :]
        rows[...] = rbuf[...].astype(BF)
        cols[...] = cbuf[...].astype(BF)
        for side in range(2):
            corn[2 * side, 0:16, :] = cbuf[side, 0:16, :].astype(BF)
            corn[2 * side, 16:32, :] = cbuf[side, 64:80, :].astype(BF)
            corn[2 * side + 1, 0:16, :] = cbuf[side, 48:64, :].astype(BF)
            corn[2 * side + 1, 16:32, :] = cbuf[side, 96:112, :].astype(BF)
        for f in range(8):
            tb[:, f * 128 : (f + 1) * 128] = terms[pl.ds(f, 384, stride=8), :].astype(BF)
        for g in range(4):
            res = jnp.dot(oh[...], tb[:, g * 256 : (g + 1) * 256], preferred_element_type=F32)
            for o in range(9):
                for b in range(2):
                    send[o, 2 * g + b] = res[o * 96 : (o + 1) * 96, b * 128 : (b + 1) * 128].astype(BF)


def remap_out(atm, oce, ts, sw, w, dd, dt, mask):
    tiles = 128 // STEPS
    fields = 64 // STEPS
    whole = lambda *shape: pl.BlockSpec(shape, lambda i: (0,) * len(shape))
    return pl.pallas_call(
        out_kernel,
        grid=(STEPS,),
        in_specs=[
            pl.BlockSpec((4, 1, 64, 256), lambda i: (0, 15, 0, 0)),
            whole(64, 256),
            whole(64, 256),
            whole(3, 128),
            whole(3, 128),
            pl.BlockSpec((fields, 64, 256), lambda i: (i, 0, 0)),
            pl.BlockSpec((fields, 48, 256), lambda i: (i, 0, 0)),
            whole(48, 256),
            pl.BlockSpec((tiles, 3, 128, 128), lambda i: (i, 0, 0, 0)),
        ],
        out_specs=[whole(9, 8, 96, 128), whole(4, 144, 256), whole(2, 160, 128), whole(4, 32, 128)],
        out_shape=[
            jax.ShapeDtypeStruct((9, 8, 96, 128), BF),
            jax.ShapeDtypeStruct((4, 144, 256), BF),
            jax.ShapeDtypeStruct((2, 160, 128), BF),
            jax.ShapeDtypeStruct((4, 32, 128), BF),
        ],
        scratch_shapes=[
            pltpu.VMEM((1024, 128), F32),
            pltpu.VMEM((3072, 128), F32),
            pltpu.VMEM((864, 384), BF),
            pltpu.VMEM((384, 1024), BF),
            pltpu.VMEM((4, 144, 256), F32),
            pltpu.VMEM((2, 160, 128), F32),
        ],
        compiler_params=pltpu.CompilerParams(vmem_limit_bytes=40 * MIB),
        name="remap_out",
    )(atm, ts, sw, dd, dt, atm.reshape(64, 64, 256), oce.reshape(64, 48, 256), mask, w)


def step(x, rate):
    rows, lanes = x.shape
    around = pltpu.roll(x, 1, 0) + pltpu.roll(x, rows - 1, 0) + pltpu.roll(x, 1, 1) + pltpu.roll(x, lanes - 1, 1)
    return (1.0 - 4.0 * rate) * x + rate * around


def unpacked(from_left, from_right, n):
    lane = lax.broadcasted_iota(jnp.int32, from_left.shape, 1)
    right = pltpu.roll(from_right, (128 - 2 * n) & 127, 1)
    left = pltpu.roll(from_left, 126 - 2 * n, 1)
    return jnp.where(lane < 2, right, jnp.where(lane >= 126, left, 0.0))


def two_rows(at, first, second):
    rows = lax.broadcasted_iota(jnp.int32, (8, first.shape[1]), 0)
    return jnp.where(rows == at, first, jnp.where(rows == at + 1, second, 0.0))


def framed(x, south, north, third):
    return jnp.concatenate([jnp.concatenate([south, x, north], axis=0), third], axis=1)


def spread(mixer, cells):
    size = 16 * cells
    pick = lambda dim: jnp.where(
        lax.broadcasted_iota(jnp.int32, (size, 16) if dim == 0 else (16, size), dim) // cells
        == lax.broadcasted_iota(jnp.int32, (size, 16) if dim == 0 else (16, size), 1 - dim),
        1.0,
        0.0,
    )
    dot = functools.partial(jnp.dot, precision=HIGHEST, preferred_element_type=F32)
    full = dot(dot(pick(0), mixer), pick(1))
    r = lax.broadcasted_iota(jnp.int32, (size, size), 0) % cells
    c = lax.broadcasted_iota(jnp.int32, (size, size), 1) % cells
    return jnp.where(r == c, full, 0.0)


def halves(x):
    high = x.astype(BF)
    return high, (x - high.astype(F32)).astype(BF)


def dot3(lhs_high, lhs_low, x):
    high, low = halves(x)
    dot = functools.partial(jnp.dot, preferred_element_type=F32)
    return dot(lhs_high, high) + dot(lhs_high, low) + dot(lhs_low, high)


def middle_kernel(
    send, rows, cols, corn, atm, oce, mask, seam, mix_a, mix_o,
    stepped, ss, q_out, f_out, sst_out, coef_out,
    xa, xo, lla, bc, own, pr, ro, rl, sl, rr, cc, kk, fr, rrf, cea, ceo, gfc, mext, fold, uv,
    ka, ko, fs, dr_s, dr_r, dc_s, dc_r, dk_r, fd, drf, ced, gd, sst_s, sst_r,
    lsem, ssem, rsem,
):
    lon = lax.axis_index("lon")
    lat = lax.axis_index("lat")
    side = lax.rem(lat, 2)
    partner = lat + 1 - 2 * side
    outer = lat - 1 + 2 * side
    has_outer = jnp.logical_and(outer >= 0, outer < N_LAT)
    has_south = lat > 0
    has_north = lat < N_LAT - 1
    top = lat == N_LAT - 1
    always = lat >= 0
    lon_at = lambda d: lax.rem(lon + d + N_LON, N_LON)

    def lat_ok(d):
        return always if d == 0 else (has_south if d < 0 else has_north)

    def send_to(cond, src, dst, n, m, dev_lon, dev_lat):
        copy = pltpu.make_async_remote_copy(
            src_ref=src, dst_ref=dst, send_sem=ssem.at[n], recv_sem=rsem.at[m],
            device_id=(dev_lon, dev_lat), device_id_type=MESH,
        )

        @pl.when(cond)
        def _():
            copy.start()

        def finish():
            @pl.when(cond)
            def _():
                copy.wait_send()

        pending.append(finish)

    def arrive(cond, dst, m):
        @pl.when(cond)
        def _():
            pltpu.make_async_remote_copy(
                src_ref=dst, dst_ref=dst, send_sem=ssem.at[0], recv_sem=rsem.at[m],
                device_id=(lon, partner), device_id_type=MESH,
            ).wait_recv()

    pending = []
    loads = [
        pltpu.make_async_copy(oce, xo, lsem.at[0]),
        pltpu.make_async_copy(atm, xa, lsem.at[1]),
    ] + [pltpu.make_async_copy(send.at[dl * 3 + 1], own.at[dl], lsem.at[2 + dl]) for dl in range(3)]
    for load in loads:
        load.start()

    barrier = pltpu.get_barrier_semaphore()
    around = [(dl, dn) for dl in (-1, 0, 1) for dn in (-1, 0, 1) if (dl, dn) != (0, 0)]
    for dl, dn in around:

        @pl.when(lat_ok(dn))
        def _(dl=dl, dn=dn):
            pl.semaphore_signal(barrier, inc=1, device_id=(lon_at(dl), lat + dn), device_id_type=MESH)

    @pl.when(top)
    def _():
        for d in range(2, N_LON - 1):
            pl.semaphore_signal(barrier, inc=1, device_id=(lon_at(d), lat), device_id_type=MESH)
        pl.semaphore_wait(barrier, 5 + 5)

    @pl.when(lat == 0)
    def _():
        pl.semaphore_wait(barrier, 5)

    @pl.when(jnp.logical_and(has_south, has_north))
    def _():
        pl.semaphore_wait(barrier, 8)

    direction = {pair: n for n, pair in enumerate(around)}

    def halo(first, rows_s, rows_r, cols_s, cols_r, corn_s, corn_r):
        for dl, dn in around:
            n = first + direction[(dl, dn)]
            back = first + direction[(-dl, -dn)]
            if dl == 0:
                src, dst = rows_s(max(dn, 0)), rows_r(max(-dn, 0))
            elif dn == 0:
                src, dst = cols_s(max(dl, 0)), cols_r(max(-dl, 0))
            else:
                src, dst = corn_s(max(dl, 0), max(dn, 0)), corn_r(max(-dl, 0), max(-dn, 0))
            send_to(lat_ok(dn), src, dst, n, back, lon_at(dl), lat + dn)

    def halo_arrive(first, rows_r, cols_r, corn_r):
        for dl, dn in around:
            n = first + direction[(dl, dn)]
            if dl == 0:
                dst = rows_r(max(dn, 0))
            elif dn == 0:
                dst = cols_r(max(dl, 0))
            else:
                dst = corn_r(max(dl, 0), max(dn, 0))
            arrive(lat_ok(dn), dst, n)

    def ring(first, src, landing):
        for d in range(1, N_LON):
            send_to(top, src, landing.at[lon], first + d, first + lon, lon_at(d), lat)

    def ring_arrive(first, landing):
        for d in range(1, N_LON):
            arrive(top, landing.at[lon_at(d)], first + lon_at(d))

    rows_r = lambda b: rr.at[b]
    cols_r = lambda a: cc.at[a]
    corn_r = lambda a, b: kk.at[2 * a + b]
    halo(0, lambda b: rows.at[pl.ds(2 * b, 2)], rows_r, lambda a: cols.at[a], cols_r, lambda a, b: corn.at[2 * a + b], corn_r)
    fold_src = rows.at[pl.ds(2, 2), pl.ds(64, 80)]
    ring(8, fold_src, fr)
    own_fold = pltpu.make_async_copy(fold_src, fr.at[lon], lsem.at[5])

    @pl.when(top)
    def _():
        own_fold.start()

    for dl in (0, 2, 1):
        send_to(always, send.at[dl * 3 + 2 - 2 * side], pr.at[dl], 16 + dl, 16 + dl, lon, partner)
    for dl in range(3):
        send_to(has_outer, send.at[dl * 3 + 2 * side], ro.at[dl], 19 + dl, 19 + dl, lon_at(dl - 1), outer)

    @pl.when(jnp.logical_not(has_outer))
    def _():
        ro[...] = jnp.zeros_like(ro)

    for b, cond in ((0, has_south), (1, has_north)):

        @pl.when(jnp.logical_not(cond))
        def _(b=b):
            rr[b] = jnp.zeros(rr.shape[1:], BF)
            dr_r[b] = jnp.zeros(dr_r.shape[1:], BF)
            for a in range(2):
                kk[2 * a + b] = jnp.zeros(kk.shape[1:], BF)
                dk_r[2 * a + b] = jnp.zeros(dk_r.shape[1:], BF)
            for dl in range(3):
                sst_r[dl * 3 + 2 * b] = jnp.zeros(sst_r.shape[1:], BF)

    for load in loads[2:]:
        load.wait()
    for dl in (0, 2, 1):
        arrive(always, pr.at[dl], 16 + dl)
    for n, dl in enumerate((0, 2)):

        @pl.loop(0, 8)
        def _(f, n=n, dl=dl):
            sl[n, f] = (own[dl, f].astype(F32) + pr[dl, f].astype(F32)).astype(BF)

        send_to(always, sl.at[n], rl.at[n], 22 + n, 22 + n, lon_at(dl - 1), lat)

    ma = mix_a[...]
    mo = mix_o[...]
    dot = functools.partial(jnp.dot, precision=HIGHEST, preferred_element_type=F32)
    ma2 = dot(ma, ma)
    mo2 = dot(mo, mo)
    ka[0], ka[1] = halves(spread(ma2, 16))
    ko[0, :, 0:128], ko[1, :, 0:128] = halves(spread(mo2, 8))
    ko[0, :, 128:256], ko[1, :, 128:256] = halves(spread(mo, 8))
    coef = jnp.broadcast_to(mo2[:, 0:1], (16, 128))
    coef_out[...] = coef

    @pl.when(top)
    def _():
        lane = lax.broadcasted_iota(jnp.int32, (1, 384), 1)
        column = lon * 256 + jnp.where(lane < 320, lane, lane - 384)
        pole = seam[0:1, 0:1] + lon * 256
        source = (pole - column) & 2047
        for j in range(8):
            fold[j * 256 : (j + 1) * 256, :] = jnp.where(
                lax.broadcasted_iota(jnp.int32, (256, 384), 0) + j * 256 == source, 1.0, 0.0
            ).astype(BF)

    loads[0].wait()
    loads[1].wait()
    uv[0] = xo[2, 0]
    uv[1] = xo[3, 0]

    halo_arrive(0, rows_r, cols_r, corn_r)
    for b in range(2):
        for e in range(2):
            rrf[b, e] = rr[b, e].astype(F32)
    for a in range(2):
        side_cols = cc[a].astype(F32)
        ks = kk[2 * a].astype(F32)
        kn = kk[2 * a + 1].astype(F32)
        cea[a, 0:8, :] = ks[8:16]
        cea[a, 8:72, :] = side_cols[0:64]
        cea[a, 72:80, :] = kn[0:8]
        ceo[a, 0:8, :] = ks[24:32]
        ceo[a, 8:56, :] = side_cols[64:112]
        ceo[a, 56:64, :] = kn[16:24]

    @pl.when(top)
    def _():
        own_fold.wait()
        ring_arrive(8, fr)
        total = jnp.zeros((160, 384), F32)
        for j in range(8):
            total += jnp.dot(fr[j].reshape(160, 256), fold[j * 256 : (j + 1) * 256, :], preferred_element_type=F32)
        n = lax.broadcasted_iota(jnp.int32, (80, 384), 0)
        sign = jnp.where(jnp.logical_and(n >= 32, n < 64), -1.0, 1.0)
        for e in range(2):
            ghost = total[80 * (1 - e) : 80 * (2 - e)] * sign
            gfc[e] = ghost[:, 256:384]
            rrf[1, e, 64:144, :] = ghost[:, 0:256]

    @pl.when(jnp.logical_not(top))
    def _():
        gfc[...] = jnp.zeros_like(gfc)

    lane_m = lax.broadcasted_iota(jnp.int32, (48, 128), 1)
    sea = mask[...].astype(F32)
    third = jnp.where(
        lane_m < 2, cc[1, 112:160, :].astype(F32), jnp.where(lane_m >= 126, cc[0, 112:160, :].astype(F32), 0.0)
    )
    none = jnp.zeros((8, 128), F32)
    mext[...] = framed(
        sea,
        two_rows(6, rrf[0, 0, 128:129, :], rrf[0, 1, 128:129, :]),
        two_rows(0, rrf[1, 0, 128:129, :], rrf[1, 1, 128:129, :]),
        jnp.concatenate([none, third, none], axis=0),
    )

    @pl.loop(0, 64)
    def _(n):
        v = n // 16
        l = lax.rem(n, 16)
        third = unpacked(ceo[0], ceo[1], n)
        north = jnp.where(top, two_rows(0, gfc[0, pl.ds(n, 1), :], gfc[1, pl.ds(n, 1), :]), third[56:64])
        x = framed(
            xo[v, l],
            two_rows(6, rrf[0, 0, pl.ds(64 + n, 1), :], rrf[0, 1, pl.ds(64 + n, 1), :]),
            two_rows(0, rrf[1, 0, pl.ds(64 + n, 1), :], rrf[1, 1, pl.ds(64 + n, 1), :]),
            jnp.concatenate([third[0:56], north], axis=0),
        )
        m = mext[...]
        b = step(m * step(x, 0.2), 0.2)
        c = step(x - m * x, 0.2)
        bc[v, l] = b[8:56, 0:256]
        bc[v, 16 + l] = c[8:56, 0:256]

    @pl.loop(0, 24)
    def _(n):
        v = n // 6
        at = pl.multiple_of(lax.rem(n, 6) * 8, 8)
        mixed = dot3(ko[0], ko[1], bc[v, :, pl.ds(at, 8), :].reshape(256, 256)).reshape(16, 8, 256)
        wet = mask[pl.ds(at, 8), :] > 0
        xo[v, :, pl.ds(at, 8), :] = jnp.where(wet[None], mixed, xo[v, :, pl.ds(at, 8), :])

    ocean_out = pltpu.make_async_copy(xo, ss, lsem.at[0])
    ocean_out.start()

    row_a = lax.broadcasted_iota(jnp.int32, (80, 1), 0)
    inside = jnp.where(
        jnp.logical_and(jnp.logical_or(row_a >= 8, has_south), jnp.logical_or(row_a < 72, has_north)), 1.0, 0.0
    )

    @pl.loop(0, 64)
    def _(n):
        x = framed(
            xa[n // 16, lax.rem(n, 16)],
            two_rows(6, rrf[0, 0, pl.ds(n, 1), :], rrf[0, 1, pl.ds(n, 1), :]),
            two_rows(0, rrf[1, 0, pl.ds(n, 1), :], rrf[1, 1, pl.ds(n, 1), :]),
            unpacked(cea[0], cea[1], n),
        )
        y = step(inside * step(x, 0.15), 0.15)
        lla[n // 16, lax.rem(n, 16)] = y[8:72, 0:256]

    @pl.loop(0, 16)
    def _(n):
        v = n // 4
        at = pl.multiple_of(lax.rem(n, 4) * 16, 16)
        mixed = dot3(ka[0], ka[1], lla[v, :, pl.ds(at, 16), :].reshape(256, 256))
        xa[v, :, pl.ds(at, 16), :] = mixed.reshape(16, 16, 256)

    atm_out = pltpu.make_async_copy(xa, stepped, lsem.at[1])
    atm_out.start()

    for dl in range(3):
        arrive(has_outer, ro.at[dl], 19 + dl)
    for n in range(2):
        arrive(always, rl.at[n], 22 + n)

    @pl.loop(0, 8)
    def _(f):
        parts = [own[1, f], pr[1, f], rl[0, f], rl[1, f], ro[0, f], ro[1, f], ro[2, f]]
        total = functools.reduce(lambda x, y: x + y, [p.astype(F32) for p in parts])
        fs[pl.ds(pl.multiple_of(f * 96, 8), 96), :] = total

    flux = []
    for f in range(8):
        value = sea * jnp.concatenate([fs[pl.ds(f * 96 + h, 48, stride=2), :] for h in range(2)], axis=1)
        f_out[f] = value
        flux.append(value)
    forcing = [
        0.2 * sea * (flux[5] - flux[2] - flux[3] - flux[4]),
        0.2 * sea * (flux[3] - flux[6]),
        sea * (0.3 * flux[0] - 0.1 * flux[7] * uv[0]),
        sea * (0.3 * flux[1] - 0.1 * flux[7] * uv[1]),
    ]

    left = jnp.zeros((48, 128), F32)
    right = jnp.zeros((48, 128), F32)
    edge = [[jnp.zeros((16, 256), F32) for _ in range(2)] for _ in range(2)]
    row_16 = lax.broadcasted_iota(jnp.int32, (16, 256), 0)
    for f, d in enumerate(forcing):
        left = jnp.where((lane_m >> 1) == f, pltpu.roll(d[:, 0:128], 2 * f, 1) if f else d[:, 0:128], left)
        right = jnp.where((lane_m >> 1) == f, pltpu.roll(d[:, 128:256], 2 * f + 2, 1), right)
        for b in range(2):
            for e in range(2):
                r = 46 * b + e
                edge[b][e] = jnp.where(row_16 == f, d[r : r + 1, :], edge[b][e])
    dc_s[0] = left.astype(BF)
    dc_s[1] = right.astype(BF)
    for b in range(2):
        for e in range(2):
            dr_s[b, 16 * e : 16 * e + 16, :] = edge[b][e].astype(BF)
    rows_r = lambda b: dr_r.at[b]
    cols_r = lambda a: dc_r.at[a]
    corn_r = lambda a, b: dk_r.at[2 * a + b]
    halo(24, lambda b: dr_s.at[b], rows_r, lambda a: dc_s.at[a], cols_r,
         lambda a, b: dc_s.at[a, pl.ds(32 * b, 16)], corn_r)
    ring(32, dr_s.at[1], fd)

    @pl.when(top)
    def _():
        fd[lon] = dr_s[1]

    halo_arrive(24, rows_r, cols_r, corn_r)
    for b in range(2):
        drf[b] = dr_r[b].astype(F32)
    for a in range(2):
        ced[a, 0:8, :] = dk_r[2 * a].astype(F32)[8:16]
        ced[a, 8:56, :] = dc_r[a].astype(F32)
        ced[a, 56:64, :] = dk_r[2 * a + 1].astype(F32)[0:8]

    @pl.when(top)
    def _():
        ring_arrive(32, fd)
        total = jnp.zeros((32, 384), F32)
        for j in range(8):
            total += jnp.dot(fd[j], fold[j * 256 : (j + 1) * 256, :], preferred_element_type=F32)
        n = lax.broadcasted_iota(jnp.int32, (16, 384), 0)
        sign = jnp.where(n >= 2, -1.0, 1.0)
        for e in range(2):
            gd[e] = total[16 * (1 - e) : 16 * (2 - e)] * sign
            drf[1, 16 * e : 16 * e + 16, :] = gd[e][:, 0:256]

    @pl.when(jnp.logical_not(top))
    def _():
        gd[...] = jnp.zeros_like(gd)

    m = mext[...]
    for f, d in enumerate(forcing):
        third = unpacked(ced[0], ced[1], f)
        north = jnp.where(top, two_rows(0, gd[0, f : f + 1, 256:384], gd[1, f : f + 1, 256:384]), third[56:64])
        x = framed(
            d,
            two_rows(6, drf[0, f : f + 1, :], drf[0, 16 + f : 17 + f, :]),
            two_rows(0, drf[1, f : f + 1, :], drf[1, 16 + f : 17 + f, :]),
            jnp.concatenate([third[0:56], north], axis=0),
        )
        q = sea * step(m * step(x, 0.2), 0.2)[8:56, 0:256]
        q_out[f] = q
        if f == 0:
            c00 = jnp.concatenate([coef[0:1, :], coef[0:1, :]], axis=1)
            heat = sea * (xo[0, 0] + c00 * q)
            for h in range(2):
                fs[pl.ds(h, 48, stride=2), :] = heat[:, 128 * h : 128 * h + 128]
            sst_s[...] = fs[0:96, :].astype(BF)
            for dl, dn in around:
                n = 40 + direction[(dl, dn)]
                back = 40 + direction[(-dl, -dn)]
                slot = (1 - dl) * 3 + 1 - dn
                send_to(lat_ok(dn), sst_s, sst_r.at[slot], n, back, lon_at(dl), lat + dn)
    sst_r[4] = sst_s[...]
    for dl, dn in around:
        arrive(lat_ok(dn), sst_r.at[(1 + dl) * 3 + 1 + dn], 40 + direction[(dl, dn)])
    sst_out[...] = sst_r[...]
    for finish in pending:
        finish()
    ocean_out.wait()
    atm_out.wait()


def exchange(send, rows, cols, corn, atm, oce, mask, seam, mix_a, mix_o):
    here = pl.BlockSpec(memory_space=pltpu.VMEM)
    away = pl.BlockSpec(memory_space=pl.ANY)
    return pl.pallas_call(
        middle_kernel,
        in_specs=[away] * 6 + [here] * 4,
        out_specs=[away] * 2 + [here] * 4,
        out_shape=[
            jax.ShapeDtypeStruct((4, 16, 64, 256), F32),
            jax.ShapeDtypeStruct((4, 16, 48, 256), F32),
            jax.ShapeDtypeStruct((4, 48, 256), F32),
            jax.ShapeDtypeStruct((8, 48, 256), F32),
            jax.ShapeDtypeStruct((9, 96, 128), BF),
            jax.ShapeDtypeStruct((16, 128), F32),
        ],
        scratch_shapes=[
            pltpu.VMEM((4, 16, 64, 256), F32),
            pltpu.VMEM((4, 16, 48, 256), F32),
            pltpu.VMEM((4, 16, 64, 256), F32),
            pltpu.VMEM((4, 32, 48, 256), F32),
            pltpu.VMEM((3, 8, 96, 128), BF),
            pltpu.VMEM((3, 8, 96, 128), BF),
            pltpu.VMEM((3, 8, 96, 128), BF),
            pltpu.VMEM((2, 8, 96, 128), BF),
            pltpu.VMEM((2, 8, 96, 128), BF),
            pltpu.VMEM((2, 2, 144, 256), BF),
            pltpu.VMEM((2, 160, 128), BF),
            pltpu.VMEM((4, 32, 128), BF),
            pltpu.VMEM((8, 2, 80, 256), BF),
            pltpu.VMEM((2, 2, 144, 256), F32),
            pltpu.VMEM((2, 80, 128), F32),
            pltpu.VMEM((2, 64, 128), F32),
            pltpu.VMEM((2, 80, 128), F32),
            pltpu.VMEM((64, 384), F32),
            pltpu.VMEM((2048, 384), BF),
            pltpu.VMEM((2, 48, 256), F32),
            pltpu.VMEM((2, 256, 256), BF),
            pltpu.VMEM((2, 128, 256), BF),
            pltpu.VMEM((768, 128), F32),
            pltpu.VMEM((2, 32, 256), BF),
            pltpu.VMEM((2, 32, 256), BF),
            pltpu.VMEM((2, 48, 128), BF),
            pltpu.VMEM((2, 48, 128), BF),
            pltpu.VMEM((4, 16, 128), BF),
            pltpu.VMEM((8, 32, 256), BF),
            pltpu.VMEM((2, 32, 256), F32),
            pltpu.VMEM((2, 64, 128), F32),
            pltpu.VMEM((2, 16, 384), F32),
            pltpu.VMEM((96, 128), BF),
            pltpu.VMEM((9, 96, 128), BF),
            pltpu.SemaphoreType.DMA((6,)),
            pltpu.SemaphoreType.DMA((48,)),
            pltpu.SemaphoreType.DMA((48,)),
        ],
        compiler_params=pltpu.CompilerParams(collective_id=0, has_side_effects=True, vmem_limit_bytes=40 * MIB),
        name="exchange",
    )(send, rows, cols, corn, atm, oce, mask, seam, mix_a, mix_o)


BACK_STEPS = 8


def back_kernel(sst, dd, dt, q, coef, w, atm, oce, f_in, atm_out, ex, oce_out, f_out, sel, exs):
    i = pl.program_id(0)
    tiles = w.shape[0]
    fields = atm.shape[0]

    @pl.when(i == 0)
    def _():
        heat = sst[...].reshape(864, 128)
        for k in range(3):
            picked = lax.dot_general(one_hot_slots(dd, dt, k), heat, TN, preferred_element_type=F32)
            sel[k * 128 : (k + 1) * 128, :] = picked.astype(BF)

    row = lax.broadcasted_iota(jnp.int32, (16, 128), 0)
    even = (row & 1) == 0
    for g in range(tiles // 16):
        acc = jnp.zeros((16, 128), F32)
        t0 = pl.multiple_of(i * tiles + g * 16, 16)
        part = [sel[pl.ds(pl.multiple_of(k * 128 + t0, 16), 16), :] for k in range(3)]
        lhs = jnp.concatenate(part[:2], axis=1)
        last = part[2].astype(F32)
        split = jnp.concatenate([jnp.where(even, last, 0.0), jnp.where(even, 0.0, last)], axis=1).astype(BF)
        for j in range(0, 16, 4):
            n = g * 16 + j
            for h in range(2):
                p = n + 2 * h
                block = jnp.concatenate(
                    [jnp.concatenate([w[p, 0], w[p, 1]], axis=1), jnp.concatenate([w[p + 1, 0], w[p + 1, 1]], axis=1)],
                    axis=0,
                )
                r = lax.dot_general(lhs, block, NT, preferred_element_type=F32)
                acc += jnp.where(row == j + 2 * h, r[:, :128], 0.0) + jnp.where(row == j + 2 * h + 1, r[:, 128:], 0.0)
            block = jnp.concatenate(
                [jnp.concatenate([w[n, 2], w[n + 1, 2]], axis=1), jnp.concatenate([w[n + 2, 2], w[n + 3, 2]], axis=1)],
                axis=0,
            )
            r = lax.dot_general(split, block, NT, preferred_element_type=F32)
            acc += jnp.where((row == j) | (row == j + 1), r[:, :128], 0.0)
            acc += jnp.where((row == j + 2) | (row == j + 3), r[:, 128:], 0.0)
        exs[pl.ds(t0, 16), :] = acc

    atm_out[...] = atm[...]
    place = jnp.where(i < 5, i, jnp.where(i == 7, 5, i + 1))
    v = place // 2
    for j in range(fields):
        c = coef[pl.ds(lax.rem(place, 2) * fields + j, 1), :]
        oce_out[j] = oce[j] + jnp.concatenate([c, c], axis=1) * q[v]

    @pl.when(i == 0)
    def _():
        f_out[...] = f_in[...]

    @pl.when(i == pl.num_programs(0) - 1)
    def _():
        for h in range(2):
            at = slice(128 * h, 128 * h + 128)
            heat = exs[pl.ds(h, 64, stride=2), :]
            ex[:, at] = heat
            cold = atm[fields - 1, :, at]
            atm_out[fields - 1, :, at] = cold + 0.5 * (heat - cold)


def remap_back(sst, dd, dt, q, coef, w, atm, oce, flux):
    tiles = 128 // BACK_STEPS
    fields = 64 // BACK_STEPS
    whole = lambda *shape: pl.BlockSpec(shape, lambda i: (0,) * len(shape))
    place = lambda i: (jnp.where(i < 5, i, jnp.where(i == 7, 5, i + 1)), 0, 0)
    return pl.pallas_call(
        back_kernel,
        grid=(BACK_STEPS,),
        in_specs=[
            whole(9, 96, 128),
            whole(3, 128),
            whole(3, 128),
            whole(4, 48, 256),
            whole(16, 128),
            pl.BlockSpec((tiles, 3, 128, 128), lambda i: (i, 0, 0, 0)),
            pl.BlockSpec((fields, 64, 256), place),
            pl.BlockSpec((fields, 48, 256), place),
            whole(8, 48, 256),
        ],
        out_specs=[
            pl.BlockSpec((fields, 64, 256), place),
            whole(64, 256),
            pl.BlockSpec((fields, 48, 256), place),
            whole(8, 48, 256),
        ],
        out_shape=[
            jax.ShapeDtypeStruct((64, 64, 256), F32),
            jax.ShapeDtypeStruct((64, 256), F32),
            jax.ShapeDtypeStruct((64, 48, 256), F32),
            jax.ShapeDtypeStruct((8, 48, 256), F32),
        ],
        scratch_shapes=[pltpu.VMEM((384, 128), BF), pltpu.VMEM((128, 128), F32)],
        compiler_params=pltpu.CompilerParams(vmem_limit_bytes=40 * MIB),
        name="remap_back",
    )(sst, dd, dt, q, coef, w, atm.reshape(64, 64, 256), oce.reshape(64, 48, 256), flux)


def per_device(atmos, ts, sw, w, dd, dt, mix_a, ocean, mask, seam, mix_o):
    dd, dt = dd.T, dt.T
    send, rows, cols, corn = remap_out(atmos, ocean, ts, sw, w, dd, dt, mask)
    stepped, ss, q, flux, sst, coef = exchange(
        send, rows, cols, corn, atmos, ocean, mask, seam.reshape(1, 256), mix_a, mix_o
    )
    atm, ex, oce, flux = remap_back(sst, dd, dt, q, coef, w, stepped, ss, flux)
    return atm.reshape(atmos.shape), ex, oce.reshape(ocean.shape), flux


def solution(mesh):
    field = P(None, None, "lat", "lon")
    plane = P("lat", "lon")
    tiles = P(("lon", "lat"), None)
    return jax.shard_map(
        per_device,
        mesh=mesh,
        in_specs=(field, plane, plane, P(("lon", "lat"), None, None, None), tiles, tiles, P(), field, plane, P("lon"), P()),
        out_specs=(field, plane, field, P(None, "lat", "lon")),
        check_vma=False,
    )
```

```python
import functools

import jax
import jax.numpy as jnp
from jax import lax
from jax.experimental import pallas as pl
from jax.experimental.pallas import tpu as pltpu
from jax.sharding import PartitionSpec as P

F32 = jnp.float32
BF = jnp.bfloat16
MESH = pl.DeviceIdType.MESH
HIGHEST = lax.Precision.HIGHEST
NT = (((1,), (1,)), ((), ()))
TN = (((0,), (0,)), ((), ()))
N_LON = 8
N_LAT = 16
CHUNKS = 8
MIB = 2**20


def flux_fields(u, v, ta, qa, ts, sw):
    speed = jnp.sqrt(u * u + v * v + 1.0)
    soft = jnp.maximum(qa, 0.0) + jnp.log1p(jnp.exp(-jnp.abs(qa)))
    return [
        0.8 * speed * u,
        0.8 * speed * v,
        0.6 * speed * (ts - ta),
        0.5 * speed * (0.4 * jnp.exp(0.5 * ts) - qa),
        0.3 * (ta - ts) * (2.0 + jnp.tanh(ta)),
        sw * (0.9 - 0.1 * jnp.tanh(qa)),
        soft,
        0.3 * speed * speed,
    ]


def slot_rows(owner, tile):
    lon = lax.axis_index("lon")
    lat = lax.axis_index("lat")
    lon_offset = ((owner >> 4) - lon + 1) & 7
    lat_offset = (owner & 15) - lat + 1
    return (lon_offset * 3 + lat_offset) * 96 + tile


def one_hot_slots(dd, dt, k):
    slot = slot_rows(dd[k : k + 1, :], dt[k : k + 1, :])
    rows = lax.broadcasted_iota(jnp.int32, (864, 128), 0)
    return jnp.where(slot == rows, 1.0, 0.0).astype(BF)


def out_kernel(
    atm, oce, ts, sw, dd_far, dt_far, mask_far, w,
    send, rows, cols, corn, atm_here, oce_here, w_here,
    surf, heat, sun, dd, dt, mask, ft, terms, oh, tb, rbuf, sem,
):
    chunk = 128 // CHUNKS
    copies = [
        pltpu.make_async_copy(atm.at[:, 15], surf, sem.at[0]),
        pltpu.make_async_copy(ts, heat, sem.at[1]),
        pltpu.make_async_copy(sw, sun, sem.at[2]),
        pltpu.make_async_copy(mask_far, mask, sem.at[5 + CHUNKS]),
    ]
    targets = [
        pltpu.make_async_copy(dd_far, dd, sem.at[6 + CHUNKS]),
        pltpu.make_async_copy(dt_far, dt, sem.at[7 + CHUNKS]),
    ]
    for copy in targets:
        copy.start()
    weights = lambda i: pltpu.make_async_copy(
        w.at[pl.ds(i * chunk, chunk)], w_here.at[pl.ds(i * chunk, chunk)], sem.at[3 + i]
    )
    fields = [
        pltpu.make_async_copy(atm, atm_here, sem.at[3 + CHUNKS]),
        pltpu.make_async_copy(oce, oce_here, sem.at[4 + CHUNKS]),
    ]
    for copy in copies:
        copy.start()
    for i in range(CHUNKS):
        weights(i).start()
    for copy in fields:
        copy.start()

    for copy in targets:
        copy.wait()
    for k in range(3):
        oh[:, k * 128 : (k + 1) * 128] = one_hot_slots(dd, dt, k)
    for copy in copies:
        copy.wait()
    for f, val in enumerate(flux_fields(surf[0], surf[1], surf[2], surf[3], heat[...], sun[...])):
        val = val.astype(BF).astype(F32)
        ft[pl.ds(f, 64, stride=16), :] = val[:, :128]
        ft[pl.ds(8 + f, 64, stride=16), :] = val[:, 128:]

    group = lax.broadcasted_iota(jnp.int32, (32, 128), 0)
    even = (group & 8) == 0

    @pl.loop(0, CHUNKS)
    def _(i):
        weights(i).wait()
        for j in range(0, chunk, 4):
            t = i * chunk + j
            a = ft[pl.ds(pl.multiple_of(t * 8, 32), 32), :]
            lhs = jnp.concatenate([jnp.where(even, a, 0.0), jnp.where(even, 0.0, a)], axis=1).astype(BF)
            quad = [[w_here[t + q, k] for k in range(3)] for q in range(4)]
            for h in range(2):
                p, q = quad[2 * h], quad[2 * h + 1]
                block = jnp.concatenate([jnp.concatenate(p[:2], axis=1), jnp.concatenate(q[:2], axis=1)], axis=0)
                r = jnp.dot(lhs[16 * h : 16 * h + 16], block, preferred_element_type=F32)
                for k in range(2):
                    terms[pl.ds(pl.multiple_of((k * 128 + t + 2 * h) * 8, 16), 16), :] = r[:, k * 128 : (k + 1) * 128]
            block = jnp.concatenate(
                [
                    jnp.concatenate([quad[0][2], quad[2][2]], axis=1),
                    jnp.concatenate([quad[1][2], quad[3][2]], axis=1),
                ],
                axis=0,
            )
            r = jnp.dot(lhs, block, preferred_element_type=F32)
            at = pl.multiple_of((256 + t) * 8, 32)
            terms[pl.ds(at, 16), :] = r[:16, :128]
            terms[pl.ds(at + 16, 16), :] = r[16:, 128:]

    for copy in fields:
        copy.wait()
    lane_a = lax.broadcasted_iota(jnp.int32, (64, 128), 1) >> 1
    lane_o = lax.broadcasted_iota(jnp.int32, (48, 128), 1) >> 1
    za = jnp.zeros((64, 128), F32)
    zo = jnp.zeros((48, 128), F32)

    @pl.loop(0, 16, init_carry=(za, za, zo, zo))
    def packed(l, carry):
        left_a, right_a, left_o, right_o = carry
        for v in range(4):
            n = v * 16 + l
            ahead = 2 * n
            back = (2 * n + 2) & 127
            left_a = jnp.where(lane_a == n, pltpu.roll(atm_here[v, l, :, 0:128], ahead, 1), left_a)
            right_a = jnp.where(lane_a == n, pltpu.roll(atm_here[v, l, :, 128:256], back, 1), right_a)
            left_o = jnp.where(lane_o == n, pltpu.roll(oce_here[v, l, :, 0:128], ahead, 1), left_o)
            right_o = jnp.where(lane_o == n, pltpu.roll(oce_here[v, l, :, 128:256], back, 1), right_o)
            for e in range(2):
                rbuf[e, pl.ds(n, 1), :] = atm_here[v, l, e : e + 1, :]
                rbuf[2 + e, pl.ds(n, 1), :] = atm_here[v, l, 62 + e : 63 + e, :]
                rbuf[e, pl.ds(64 + n, 1), :] = oce_here[v, l, e : e + 1, :]
                rbuf[2 + e, pl.ds(64 + n, 1), :] = oce_here[v, l, 46 + e : 47 + e, :]
        return left_a, right_a, left_o, right_o

    sea = mask[...].astype(F32)
    for side in range(2):
        cols_a, cols_o = packed[side], packed[2 + side]
        cols[side, 0:64, :] = cols_a.astype(BF)
        cols[side, 64:112, :] = cols_o.astype(BF)
        cols[side, 112:160, :] = sea[:, 128 * side : 128 * side + 128].astype(BF)
        corn[2 * side, 0:16, :] = cols_a[0:16].astype(BF)
        corn[2 * side, 16:32, :] = cols_o[0:16].astype(BF)
        corn[2 * side + 1, 0:16, :] = cols_a[48:64].astype(BF)
        corn[2 * side + 1, 16:32, :] = cols_o[32:48].astype(BF)
    for e in range(2):
        for b in range(2):
            r = 46 * b + e
            rbuf[2 * b + e, 128:144, :] = jnp.broadcast_to(sea[r : r + 1, :], (16, 256))
    rows[...] = rbuf[...].astype(BF)

    for f in range(8):
        tb[:, f * 128 : (f + 1) * 128] = terms[pl.ds(f, 384, stride=8), :].astype(BF)
    for g in range(4):
        res = jnp.dot(oh[...], tb[:, g * 256 : (g + 1) * 256], preferred_element_type=F32)
        for o in range(9):
            for b in range(2):
                send[o, 2 * g + b] = res[o * 96 : (o + 1) * 96, b * 128 : (b + 1) * 128].astype(BF)


HERE = pl.BlockSpec(memory_space=pltpu.VMEM)
AWAY = pl.BlockSpec(memory_space=pltpu.HBM)


def remap_out(atm, oce, ts, sw, w, dd, dt, mask):
    return pl.pallas_call(
        out_kernel,
        in_specs=[AWAY] * 8,
        out_specs=[HERE] * 7,
        out_shape=[
            pltpu.VMEM((9, 8, 96, 128), BF),
            pltpu.VMEM((4, 144, 256), BF),
            pltpu.VMEM((2, 160, 128), BF),
            pltpu.VMEM((4, 32, 128), BF),
            pltpu.VMEM((4, 16, 64, 256), F32),
            pltpu.VMEM((4, 16, 48, 256), F32),
            pltpu.VMEM((128, 3, 128, 128), BF),
        ],
        scratch_shapes=[
            pltpu.VMEM((4, 64, 256), F32),
            pltpu.VMEM((64, 256), F32),
            pltpu.VMEM((64, 256), F32),
            pltpu.VMEM((3, 128), jnp.int32),
            pltpu.VMEM((3, 128), jnp.int32),
            pltpu.VMEM((48, 256), jnp.int32),
            pltpu.VMEM((1024, 128), F32),
            pltpu.VMEM((3072, 128), F32),
            pltpu.VMEM((864, 384), BF),
            pltpu.VMEM((384, 1024), BF),
            pltpu.VMEM((4, 144, 256), F32),
            pltpu.SemaphoreType.DMA((8 + CHUNKS,)),
        ],
        compiler_params=pltpu.CompilerParams(vmem_limit_bytes=16 * MIB),
        name="remap_out",
    )(*[pltpu.with_memory_space_constraint(x, pltpu.HBM) for x in (atm, oce, ts, sw, dd, dt, mask, w)])


def step(x, rate):
    rows, lanes = x.shape
    around = pltpu.roll(x, 1, 0) + pltpu.roll(x, rows - 1, 0) + pltpu.roll(x, 1, 1) + pltpu.roll(x, lanes - 1, 1)
    return (1.0 - 4.0 * rate) * x + rate * around


def step_from(x, around, rate):
    return (1.0 - 4.0 * rate) * x + rate * around


def unpacked(from_left, from_right, n):
    lane = lax.broadcasted_iota(jnp.int32, from_left.shape, 1)
    right = pltpu.roll(from_right, (128 - 2 * n) & 127, 1)
    left = pltpu.roll(from_left, 126 - 2 * n, 1)
    return jnp.where(lane < 2, right, jnp.where(lane >= 126, left, 0.0))


def two_rows(at, first, second):
    rows = lax.broadcasted_iota(jnp.int32, (8, first.shape[1]), 0)
    return jnp.where(rows == at, first, jnp.where(rows == at + 1, second, 0.0))


def framed(x, south, north, third):
    return jnp.concatenate([jnp.concatenate([south, x, north], axis=0), third], axis=1)


def lateral(parts, tri):
    rows = parts[0].shape[0]
    total = jnp.dot(jnp.concatenate(parts, axis=0).astype(BF), tri, preferred_element_type=F32)
    return [total[n * rows : (n + 1) * rows] for n in range(len(parts))]


def near(x, inner, above, below, ghost):
    rows = x.shape[0]
    lane = lax.broadcasted_iota(jnp.int32, (rows, 128), 1)
    row = lax.broadcasted_iota(jnp.int32, (8, 256), 0)
    up = pltpu.roll(x, 1, 0)
    down = pltpu.roll(x, rows - 1, 0)
    up = jnp.concatenate([jnp.where(row == 0, above, up[0:8]), up[8:]], axis=0)
    down = jnp.concatenate([down[: rows - 8], jnp.where(row == 7, below, down[rows - 8 :])], axis=0)
    edges = jnp.concatenate([jnp.where(lane == 0, ghost, 0.0), jnp.where(lane == 127, ghost, 0.0)], axis=1)
    return up + down + inner + edges


def beside(x, ghost, lane):
    t0, t1 = x[:, 0:128], x[:, 128:256]
    r0, r1 = pltpu.roll(t0, 1, 1), pltpu.roll(t1, 1, 1)
    l0, l1 = pltpu.roll(t0, 127, 1), pltpu.roll(t1, 127, 1)
    first, last = lane == 0, lane == 127
    s0 = jnp.where(first, ghost, r0) + jnp.where(last, l1, l0)
    s1 = jnp.where(first, r0, r1) + jnp.where(last, ghost, l1)
    return jnp.concatenate([s0, s1], axis=1)


def beside_packed(left, right, own_left, own_right, odd):
    centre = jnp.where(odd, left, right)
    outer = jnp.where(odd, pltpu.roll(left, 1, 1), pltpu.roll(right, 127, 1))
    inner = jnp.where(odd, pltpu.roll(own_left, 1, 1), pltpu.roll(own_right, 127, 1))
    return centre, outer + inner


def corner_lanes(centre, row):
    lane = lax.broadcasted_iota(jnp.int32, (64, 128), 1)
    field = lax.broadcasted_iota(jnp.int32, (64, 128), 0)
    line = jnp.broadcast_to(centre[row : row + 1, :], (64, 128))
    left = jnp.sum(jnp.where(lane == 2 * field + 1, line, 0.0), axis=1, keepdims=True)
    right = jnp.sum(jnp.where(lane == 2 * field, line, 0.0), axis=1, keepdims=True)
    return jnp.where(lane == 0, left, jnp.where(lane == 127, right, 0.0))


def spread(mixer, cells):
    size = 16 * cells
    pick = lambda dim: jnp.where(
        lax.broadcasted_iota(jnp.int32, (size, 16) if dim == 0 else (16, size), dim) // cells
        == lax.broadcasted_iota(jnp.int32, (size, 16) if dim == 0 else (16, size), 1 - dim),
        1.0,
        0.0,
    )
    dot = functools.partial(jnp.dot, precision=HIGHEST, preferred_element_type=F32)
    full = dot(dot(pick(0), mixer), pick(1))
    r = lax.broadcasted_iota(jnp.int32, (size, size), 0) % cells
    c = lax.broadcasted_iota(jnp.int32, (size, size), 1) % cells
    return jnp.where(r == c, full, 0.0)


def halves(x):
    high = x.astype(BF)
    return high, (x - high.astype(F32)).astype(BF)


def dot3(lhs_high, lhs_low, x):
    high, low = halves(x)
    dot = functools.partial(jnp.dot, preferred_element_type=F32)
    return dot(lhs_high, high) + dot(lhs_high, low) + dot(lhs_low, high)


def middle_kernel(
    send, rows, cols, corn, atm, oce, mask, seam, mix_a, mix_o,
    stepped, ss, q_out, f_out, sst_out, coef_out,
    lla, bc, pr, ro, rl, sl, rr, cc, kk, fr, rrf, cea, ceo, mext, fold, gsa, gso, gea, geo, tri,
    ka, ko, fs, dr_s, dr_r, dc_s, dc_r, dk_r, fd, drf, ced, gd, sst_s, sst_r,
    lsem, ssem, rsem,
):
    lon = lax.axis_index("lon")
    lat = lax.axis_index("lat")
    side = lax.rem(lat, 2)
    partner = lat + 1 - 2 * side
    outer = lat - 1 + 2 * side
    has_outer = jnp.logical_and(outer >= 0, outer < N_LAT)
    has_south = lat > 0
    has_north = lat < N_LAT - 1
    top = lat == N_LAT - 1
    always = lat >= 0
    lon_at = lambda d: lax.rem(lon + d + N_LON, N_LON)

    def lat_ok(d):
        return always if d == 0 else (has_south if d < 0 else has_north)

    def send_to(cond, src, dst, n, m, dev_lon, dev_lat):
        copy = pltpu.make_async_remote_copy(
            src_ref=src, dst_ref=dst, send_sem=ssem.at[n], recv_sem=rsem.at[m],
            device_id=(dev_lon, dev_lat), device_id_type=MESH,
        )

        @pl.when(cond)
        def _():
            copy.start()

        def finish():
            @pl.when(cond)
            def _():
                copy.wait_send()

        pending.append(finish)

    def arrive(cond, dst, m):
        @pl.when(cond)
        def _():
            pltpu.make_async_remote_copy(
                src_ref=dst, dst_ref=dst, send_sem=ssem.at[0], recv_sem=rsem.at[m],
                device_id=(lon, partner), device_id_type=MESH,
            ).wait_recv()

    pending = []
    barrier = pltpu.get_barrier_semaphore()
    around = [(dl, dn) for dl in (-1, 0, 1) for dn in (-1, 0, 1) if (dl, dn) != (0, 0)]
    for dl, dn in around:

        @pl.when(lat_ok(dn))
        def _(dl=dl, dn=dn):
            pl.semaphore_signal(barrier, inc=1, device_id=(lon_at(dl), lat + dn), device_id_type=MESH)

    @pl.when(top)
    def _():
        for d in range(2, N_LON - 1):
            pl.semaphore_signal(barrier, inc=1, device_id=(lon_at(d), lat), device_id_type=MESH)
        pl.semaphore_wait(barrier, 5 + 5)

    @pl.when(lat == 0)
    def _():
        pl.semaphore_wait(barrier, 5)

    @pl.when(jnp.logical_and(has_south, has_north))
    def _():
        pl.semaphore_wait(barrier, 8)

    direction = {pair: n for n, pair in enumerate(around)}

    def halo(first, rows_s, rows_r, cols_s, cols_r, corn_s, corn_r):
        for dl, dn in around:
            n = first + direction[(dl, dn)]
            back = first + direction[(-dl, -dn)]
            if dl == 0:
                src, dst = rows_s(max(dn, 0)), rows_r(max(-dn, 0))
            elif dn == 0:
                src, dst = cols_s(max(dl, 0)), cols_r(max(-dl, 0))
            else:
                src, dst = corn_s(max(dl, 0), max(dn, 0)), corn_r(max(-dl, 0), max(-dn, 0))
            send_to(lat_ok(dn), src, dst, n, back, lon_at(dl), lat + dn)

    def halo_arrive(first, rows_r, cols_r, corn_r):
        for dl, dn in around:
            n = first + direction[(dl, dn)]
            if dl == 0:
                dst = rows_r(max(dn, 0))
            elif dn == 0:
                dst = cols_r(max(dl, 0))
            else:
                dst = corn_r(max(dl, 0), max(dn, 0))
            arrive(lat_ok(dn), dst, n)

    def ring(first, src, landing):
        for d in range(1, N_LON):
            send_to(top, src, landing.at[lon], first + d, first + lon, lon_at(d), lat)

    def ring_arrive(first, landing):
        for d in range(1, N_LON):
            arrive(top, landing.at[lon_at(d)], first + lon_at(d))

    rows_r = lambda b: rr.at[b]
    cols_r = lambda a: cc.at[a]
    corn_r = lambda a, b: kk.at[2 * a + b]
    halo(0, lambda b: rows.at[pl.ds(2 * b, 2)], rows_r, lambda a: cols.at[a], cols_r, lambda a, b: corn.at[2 * a + b], corn_r)
    fold_src = rows.at[pl.ds(2, 2), pl.ds(64, 80)]
    ring(8, fold_src, fr)
    own_fold = pltpu.make_async_copy(fold_src, fr.at[lon], lsem.at[0])

    @pl.when(top)
    def _():
        own_fold.start()

    for dl in (0, 2, 1):
        send_to(always, send.at[dl * 3 + 2 - 2 * side], pr.at[dl], 16 + dl, 16 + dl, lon, partner)
    for dl in range(3):
        send_to(has_outer, send.at[dl * 3 + 2 * side], ro.at[dl], 19 + dl, 19 + dl, lon_at(dl - 1), outer)

    @pl.when(jnp.logical_not(has_outer))
    def _():
        ro[...] = jnp.zeros_like(ro)

    for b, cond in ((0, has_south), (1, has_north)):

        @pl.when(jnp.logical_not(cond))
        def _(b=b):
            rr[b] = jnp.zeros(rr.shape[1:], BF)
            dr_r[b] = jnp.zeros(dr_r.shape[1:], BF)
            for a in range(2):
                kk[2 * a + b] = jnp.zeros(kk.shape[1:], BF)
                dk_r[2 * a + b] = jnp.zeros(dk_r.shape[1:], BF)
            for dl in range(3):
                sst_r[dl * 3 + 2 * b] = jnp.zeros(sst_r.shape[1:], BF)

    for dl in (0, 2, 1):
        arrive(always, pr.at[dl], 16 + dl)
    for n, dl in enumerate((0, 2)):

        @pl.loop(0, 8)
        def _(f, n=n, dl=dl):
            sl[n, f] = (send[3 * dl + 1, f].astype(F32) + pr[dl, f].astype(F32)).astype(BF)

        send_to(always, sl.at[n], rl.at[n], 22 + n, 22 + n, lon_at(dl - 1), lat)

    ma = mix_a[...]
    mo = mix_o[...]
    dot = functools.partial(jnp.dot, precision=HIGHEST, preferred_element_type=F32)
    ma2 = dot(ma, ma)
    mo2 = dot(mo, mo)
    ka[0], ka[1] = halves(spread(ma2, 16))
    ko[0, :, 0:128], ko[1, :, 0:128] = halves(spread(mo2, 8))
    ko[0, :, 128:256], ko[1, :, 128:256] = halves(spread(mo, 8))
    coef = jnp.broadcast_to(mo2[:, 0:1], (16, 128))
    coef_out[...] = coef

    @pl.when(top)
    def _():
        lane = lax.broadcasted_iota(jnp.int32, (1, 384), 1)
        column = lon * 256 + jnp.where(lane < 320, lane, lane - 384)
        pole = seam[0:1, 0:1] + lon * 256
        source = (pole - column) & 2047
        for j in range(8):
            fold[j * 256 : (j + 1) * 256, :] = jnp.where(
                lax.broadcasted_iota(jnp.int32, (256, 384), 0) + j * 256 == source, 1.0, 0.0
            ).astype(BF)

    halo_arrive(0, rows_r, cols_r, corn_r)
    for b in range(2):
        for e in range(2):
            rrf[b, e] = rr[b, e].astype(F32)
    for a in range(2):
        side_cols = cc[a].astype(F32)
        ks = kk[2 * a].astype(F32)
        kn = kk[2 * a + 1].astype(F32)
        cea[a, 0:8, :] = ks[8:16]
        cea[a, 8:72, :] = side_cols[0:64]
        cea[a, 72:80, :] = kn[0:8]
        ceo[a, 0:8, :] = ks[24:32]
        ceo[a, 8:56, :] = side_cols[64:112]
        ceo[a, 56:64, :] = kn[16:24]

    @pl.when(top)
    def _():
        own_fold.wait()
        ring_arrive(8, fr)
        total = jnp.zeros((160, 384), F32)
        for j in range(8):
            total += jnp.dot(fr[j].reshape(160, 256), fold[j * 256 : (j + 1) * 256, :], preferred_element_type=F32)
        n = lax.broadcasted_iota(jnp.int32, (80, 384), 0)
        sign = jnp.where(jnp.logical_and(n >= 32, n < 64), -1.0, 1.0)
        for e in range(2):
            ghost = total[80 * (1 - e) : 80 * (2 - e)] * sign
            if e == 0:
                beyond = ghost[0:64, 256:384]
            rrf[1, e, 64:144, :] = ghost[:, 0:256]
        lane = lax.broadcasted_iota(jnp.int32, (64, 128), 1)
        field = lax.broadcasted_iota(jnp.int32, (64, 128), 0)
        both = jnp.where(lane == 2 * field + 1, beyond[:, 127:128], jnp.where(lane == 2 * field, beyond[:, 0:1], 0.0))
        both = jnp.sum(both, axis=0, keepdims=True)
        ceo[0, 56:57, :] = both
        ceo[1, 56:57, :] = both

    lane_m = lax.broadcasted_iota(jnp.int32, (48, 128), 1)
    sea = mask[...].astype(F32)
    sea_left = cc[0, 112:160, :].astype(F32)
    sea_right = cc[1, 112:160, :].astype(F32)
    third = jnp.where(lane_m < 2, sea_right, jnp.where(lane_m >= 126, sea_left, 0.0))
    none = jnp.zeros((8, 128), F32)
    mext[...] = framed(
        sea,
        two_rows(6, rrf[0, 0, 128:129, :], rrf[0, 1, 128:129, :]),
        two_rows(0, rrf[1, 0, 128:129, :], rrf[1, 1, 128:129, :]),
        jnp.concatenate([none, third, none], axis=0),
    )
    lane_f = lax.broadcasted_iota(jnp.int32, (64, 128), 1)

    def outside(ce, own_at, rows, at, rate, sea_side, sea_rows):
        odd = (lax.broadcasted_iota(jnp.int32, (rows + 16, 128), 1) & 1) == 1
        own = [
            jnp.concatenate([none, cols[a, own_at : own_at + rows, :].astype(F32), none], axis=0)
            for a in range(2)
        ]
        centre, lateral = beside_packed(ce[0], ce[1], own[0], own[1], odd)
        y = step_from(centre, pltpu.roll(centre, 1, 0) + pltpu.roll(centre, rows + 15, 0) + lateral, rate)
        x_side, y_side = centre[8 : 8 + rows], y[8 : 8 + rows]
        pack = lambda x: pltpu.roll(x, 127, 1)
        sides = [pack(x_side), pack(y_side if sea_side is None else y_side * sea_side)]
        if sea_side is not None:
            sides.append(pack(x_side - x_side * sea_side))
        ends = []
        for b in range(2):
            near_row = rrf[b, 1 - b, at : at + 64, :]
            far_row = rrf[b, b, at : at + 64, :]
            own_row = rows_in[2 * b + b, at : at + 64, :].astype(F32)
            ghost = corner_lanes(centre, 7 if b == 0 else rows + 8)
            z = step_from(near_row, far_row + own_row + beside(near_row, ghost, lane_f), rate)
            if sea_side is None:
                ends.append([jnp.where(has_south if b == 0 else has_north, z, 0.0)])
            else:
                ends.append([z * sea_rows[b], near_row - near_row * sea_rows[b]])
        return sides, ends

    rows_in = rows
    odd_m = (lane_m & 1) == 1
    sea_side = jnp.where(odd_m, jnp.broadcast_to(sea_left[:, 127:128], (48, 128)), jnp.broadcast_to(sea_right[:, 0:1], (48, 128)))
    sides, ends = outside(ceo, 64, 48, 64, 0.2, sea_side, [rrf[0, 1, 128:129, :], rrf[1, 0, 128:129, :]])
    for n in range(3):
        gso[n] = sides[n]
    for b in range(2):
        for n in range(2):
            geo[b, n] = ends[b][n]
    sides, ends = outside(cea, 0, 64, 0, 0.15, None, None)
    for n in range(2):
        gsa[n] = sides[n]
    for b in range(2):
        gea[b] = ends[b][0]

    r256 = lax.broadcasted_iota(jnp.int32, (256, 256), 0)
    c256 = lax.broadcasted_iota(jnp.int32, (256, 256), 1)
    tri[...] = jnp.where(jnp.logical_or(r256 == c256 + 1, r256 + 1 == c256), 1.0, 0.0).astype(BF)

    @pl.loop(0, 8)
    def _(i):
        v = i // 2
        first = pl.multiple_of(lax.rem(i, 2) * 8, 8)
        lines = pl.ds(pl.multiple_of(i * 8, 8), 8)
        far = pl.ds(pl.multiple_of(64 + i * 8, 8), 8)
        turned = lambda k, j: pltpu.roll(gso[k], (128 - 2 * (i * 8 + j)) & 127, 1)
        wet_here = mext[8:56, 0:256]
        south, north = rrf[0, 1, far, :], rrf[1, 0, far, :]
        xs = [oce[v, first + j] for j in range(8)]
        inner = lateral(xs, tri[...])
        a, c = [], []
        for j, x in enumerate(xs):
            around = near(x, inner[j], south[j : j + 1], north[j : j + 1], turned(0, j))
            a.append(wet_here * step_from(x, around, 0.2))
            c.append(x - wet_here * x)
        for k, parts in enumerate((a, c)):
            inner = lateral(parts, tri[...])
            south, north = geo[0, k, lines, :], geo[1, k, lines, :]
            for j, x in enumerate(parts):
                around = near(x, inner[j], south[j : j + 1], north[j : j + 1], turned(1 + k, j))
                bc[v, 16 * k + first + j] = step_from(x, around, 0.2)

    @pl.loop(0, 24, unroll=3)
    def _(n):
        v = n // 6
        at = pl.multiple_of(lax.rem(n, 6) * 8, 8)
        mixed = dot3(ko[0], ko[1], bc[v, :, pl.ds(at, 8), :].reshape(256, 256)).reshape(16, 8, 256)
        wet = mask[pl.ds(at, 8), :] > 0
        ss[v, :, pl.ds(at, 8), :] = jnp.where(wet[None], mixed, oce[v, :, pl.ds(at, 8), :])

    @pl.loop(0, 8)
    def _(i):
        v = i // 2
        first = pl.multiple_of(lax.rem(i, 2) * 8, 8)
        lines = pl.ds(pl.multiple_of(i * 8, 8), 8)
        turned = lambda k, j: pltpu.roll(gsa[k], (128 - 2 * (i * 8 + j)) & 127, 1)
        parts = [atm[v, first + j] for j in range(8)]
        ends = ((rrf[0, 1, lines, :], rrf[1, 0, lines, :]), (gea[0, lines, :], gea[1, lines, :]))
        for k in range(2):
            inner = lateral(parts, tri[...])
            south, north = ends[k]
            parts = [
                step_from(x, near(x, inner[j], south[j : j + 1], north[j : j + 1], turned(k, j)), 0.15)
                for j, x in enumerate(parts)
            ]
        for j, y in enumerate(parts):
            lla[v, first + j] = y

    @pl.loop(0, 16, unroll=4)
    def _(n):
        v = n // 4
        at = pl.multiple_of(lax.rem(n, 4) * 16, 16)
        mixed = dot3(ka[0], ka[1], lla[v, :, pl.ds(at, 16), :].reshape(256, 256))
        stepped[v, :, pl.ds(at, 16), :] = mixed.reshape(16, 16, 256)

    for dl in range(3):
        arrive(has_outer, ro.at[dl], 19 + dl)
    for n in range(2):
        arrive(always, rl.at[n], 22 + n)

    @pl.loop(0, 8)
    def _(f):
        parts = [send[4, f], pr[1, f], rl[0, f], rl[1, f], ro[0, f], ro[1, f], ro[2, f]]
        total = functools.reduce(lambda x, y: x + y, [p.astype(F32) for p in parts])
        fs[pl.ds(pl.multiple_of(f * 96, 8), 96), :] = total

    flux = []
    for f in range(8):
        value = sea * jnp.concatenate([fs[pl.ds(f * 96 + h, 48, stride=2), :] for h in range(2)], axis=1)
        f_out[f] = value
        flux.append(value)
    forcing = [
        0.2 * sea * (flux[5] - flux[2] - flux[3] - flux[4]),
        0.2 * sea * (flux[3] - flux[6]),
        sea * (0.3 * flux[0] - 0.1 * flux[7] * oce[2, 0]),
        sea * (0.3 * flux[1] - 0.1 * flux[7] * oce[3, 0]),
    ]

    left = jnp.zeros((48, 128), F32)
    right = jnp.zeros((48, 128), F32)
    edge = [[jnp.zeros((16, 256), F32) for _ in range(2)] for _ in range(2)]
    row_16 = lax.broadcasted_iota(jnp.int32, (16, 256), 0)
    for f, d in enumerate(forcing):
        left = jnp.where((lane_m >> 1) == f, pltpu.roll(d[:, 0:128], 2 * f, 1) if f else d[:, 0:128], left)
        right = jnp.where((lane_m >> 1) == f, pltpu.roll(d[:, 128:256], 2 * f + 2, 1), right)
        for b in range(2):
            for e in range(2):
                r = 46 * b + e
                edge[b][e] = jnp.where(row_16 == f, d[r : r + 1, :], edge[b][e])
    dc_s[0] = left.astype(BF)
    dc_s[1] = right.astype(BF)
    for b in range(2):
        for e in range(2):
            dr_s[b, 16 * e : 16 * e + 16, :] = edge[b][e].astype(BF)
    rows_r = lambda b: dr_r.at[b]
    cols_r = lambda a: dc_r.at[a]
    corn_r = lambda a, b: dk_r.at[2 * a + b]
    halo(24, lambda b: dr_s.at[b], rows_r, lambda a: dc_s.at[a], cols_r,
         lambda a, b: dc_s.at[a, pl.ds(32 * b, 16)], corn_r)
    ring(32, dr_s.at[1], fd)

    @pl.when(top)
    def _():
        fd[lon] = dr_s[1]

    halo_arrive(24, rows_r, cols_r, corn_r)
    for b in range(2):
        drf[b] = dr_r[b].astype(F32)
    for a in range(2):
        ced[a, 0:8, :] = dk_r[2 * a].astype(F32)[8:16]
        ced[a, 8:56, :] = dc_r[a].astype(F32)
        ced[a, 56:64, :] = dk_r[2 * a + 1].astype(F32)[0:8]

    @pl.when(top)
    def _():
        ring_arrive(32, fd)
        total = jnp.zeros((32, 384), F32)
        for j in range(8):
            total += jnp.dot(fd[j], fold[j * 256 : (j + 1) * 256, :], preferred_element_type=F32)
        n = lax.broadcasted_iota(jnp.int32, (16, 384), 0)
        sign = jnp.where(n >= 2, -1.0, 1.0)
        for e in range(2):
            gd[e] = total[16 * (1 - e) : 16 * (2 - e)] * sign
            drf[1, 16 * e : 16 * e + 16, :] = gd[e][:, 0:256]

    @pl.when(jnp.logical_not(top))
    def _():
        gd[...] = jnp.zeros_like(gd)

    m = mext[...]
    for f, d in enumerate(forcing):
        third = unpacked(ced[0], ced[1], f)
        north = jnp.where(top, two_rows(0, gd[0, f : f + 1, 256:384], gd[1, f : f + 1, 256:384]), third[56:64])
        x = framed(
            d,
            two_rows(6, drf[0, f : f + 1, :], drf[0, 16 + f : 17 + f, :]),
            two_rows(0, drf[1, f : f + 1, :], drf[1, 16 + f : 17 + f, :]),
            jnp.concatenate([third[0:56], north], axis=0),
        )
        q = sea * step(m * step(x, 0.2), 0.2)[8:56, 0:256]
        q_out[f] = q
        if f == 0:
            c00 = jnp.concatenate([coef[0:1, :], coef[0:1, :]], axis=1)
            heat = sea * (ss[0, 0] + c00 * q)
            for h in range(2):
                fs[pl.ds(h, 48, stride=2), :] = heat[:, 128 * h : 128 * h + 128]
            sst_s[...] = fs[0:96, :].astype(BF)
            for dl, dn in around:
                n = 40 + direction[(dl, dn)]
                back = 40 + direction[(-dl, -dn)]
                slot = (1 - dl) * 3 + 1 - dn
                send_to(lat_ok(dn), sst_s, sst_r.at[slot], n, back, lon_at(dl), lat + dn)
    sst_r[4] = sst_s[...]
    for dl, dn in around:
        arrive(lat_ok(dn), sst_r.at[(1 + dl) * 3 + 1 + dn], 40 + direction[(dl, dn)])
    sst_out[...] = sst_r[...]
    for finish in pending:
        finish()


def exchange(send, rows, cols, corn, atm, oce, mask, seam, mix_a, mix_o):
    return pl.pallas_call(
        middle_kernel,
        in_specs=[HERE] * 10,
        out_specs=[HERE] * 6,
        out_shape=[
            pltpu.VMEM((4, 16, 64, 256), F32),
            pltpu.VMEM((4, 16, 48, 256), F32),
            pltpu.VMEM((4, 48, 256), F32),
            pltpu.VMEM((8, 48, 256), F32),
            pltpu.VMEM((9, 96, 128), BF),
            pltpu.VMEM((16, 128), F32),
        ],
        scratch_shapes=[
            pltpu.VMEM((4, 16, 64, 256), F32),
            pltpu.VMEM((4, 32, 48, 256), F32),
            pltpu.VMEM((3, 8, 96, 128), BF),
            pltpu.VMEM((3, 8, 96, 128), BF),
            pltpu.VMEM((2, 8, 96, 128), BF),
            pltpu.VMEM((2, 8, 96, 128), BF),
            pltpu.VMEM((2, 2, 144, 256), BF),
            pltpu.VMEM((2, 160, 128), BF),
            pltpu.VMEM((4, 32, 128), BF),
            pltpu.VMEM((8, 2, 80, 256), BF),
            pltpu.VMEM((2, 2, 144, 256), F32),
            pltpu.VMEM((2, 80, 128), F32),
            pltpu.VMEM((2, 64, 128), F32),
            pltpu.VMEM((64, 384), F32),
            pltpu.VMEM((2048, 384), BF),
            pltpu.VMEM((2, 64, 128), F32),
            pltpu.VMEM((3, 48, 128), F32),
            pltpu.VMEM((2, 64, 256), F32),
            pltpu.VMEM((2, 2, 64, 256), F32),
            pltpu.VMEM((256, 256), BF),
            pltpu.VMEM((2, 256, 256), BF),
            pltpu.VMEM((2, 128, 256), BF),
            pltpu.VMEM((768, 128), F32),
            pltpu.VMEM((2, 32, 256), BF),
            pltpu.VMEM((2, 32, 256), BF),
            pltpu.VMEM((2, 48, 128), BF),
            pltpu.VMEM((2, 48, 128), BF),
            pltpu.VMEM((4, 16, 128), BF),
            pltpu.VMEM((8, 32, 256), BF),
            pltpu.VMEM((2, 32, 256), F32),
            pltpu.VMEM((2, 64, 128), F32),
            pltpu.VMEM((2, 16, 384), F32),
            pltpu.VMEM((96, 128), BF),
            pltpu.VMEM((9, 96, 128), BF),
            pltpu.SemaphoreType.DMA((1,)),
            pltpu.SemaphoreType.DMA((48,)),
            pltpu.SemaphoreType.DMA((48,)),
        ],
        compiler_params=pltpu.CompilerParams(collective_id=0, has_side_effects=True, vmem_limit_bytes=28 * MIB),
        name="exchange",
    )(send, rows, cols, corn, atm, oce, mask, seam, mix_a, mix_o)


def back_kernel(sst, dd, dt, q, coef, w, stepped, ss, flux, atm, ex, oce, f_out, sel, exs, exd, warm, sea, sem):
    plain = [
        pltpu.make_async_copy(flux, f_out, sem.at[0]),
        pltpu.make_async_copy(stepped.at[pl.ds(0, 2)], atm.at[pl.ds(0, 2)], sem.at[1]),
        pltpu.make_async_copy(stepped.at[2, pl.ds(0, 15)], atm.at[2, pl.ds(0, 15)], sem.at[2]),
        pltpu.make_async_copy(stepped.at[3], atm.at[3], sem.at[3]),
    ]
    for copy in plain:
        copy.start()
    heat = sst[...].reshape(864, 128)
    for k in range(3):
        picked = lax.dot_general(one_hot_slots(dd, dt, k), heat, TN, preferred_element_type=F32)
        sel[k * 128 : (k + 1) * 128, :] = picked.astype(BF)

    row = lax.broadcasted_iota(jnp.int32, (16, 128), 0)
    even = (row & 1) == 0
    ocean_out = lambda g: pltpu.make_async_copy(sea.at[pl.ds(g * 8, 8)], oce.at[pl.ds(g * 8, 8)], sem.at[6 + g])

    @pl.loop(0, 8)
    def _(g):
        v = g // 2
        for j in range(8):
            l = lax.rem(g, 2) * 8 + j
            c = coef[pl.ds(l, 1), :]
            sea[g * 8 + j] = ss[v, l] + jnp.concatenate([c, c], axis=1) * q[v]
        ocean_out(g).start()
        acc = jnp.zeros((16, 128), F32)
        t0 = pl.multiple_of(g * 16, 16)
        part = [sel[pl.ds(pl.multiple_of(k * 128 + t0, 16), 16), :] for k in range(3)]
        lhs = jnp.concatenate(part[:2], axis=1)
        last = part[2].astype(F32)
        split = jnp.concatenate([jnp.where(even, last, 0.0), jnp.where(even, 0.0, last)], axis=1).astype(BF)
        for j in range(0, 16, 4):
            quad = [[w[t0 + j + n, k] for k in range(3)] for n in range(4)]
            for h in range(2):
                p0, p1 = quad[2 * h], quad[2 * h + 1]
                block = jnp.concatenate([jnp.concatenate(p0[:2], axis=1), jnp.concatenate(p1[:2], axis=1)], axis=0)
                r = lax.dot_general(lhs, block, NT, preferred_element_type=F32)
                acc += jnp.where(row == j + 2 * h, r[:, :128], 0.0) + jnp.where(row == j + 2 * h + 1, r[:, 128:], 0.0)
            block = jnp.concatenate(
                [
                    jnp.concatenate([quad[0][2], quad[1][2]], axis=1),
                    jnp.concatenate([quad[2][2], quad[3][2]], axis=1),
                ],
                axis=0,
            )
            r = lax.dot_general(split, block, NT, preferred_element_type=F32)
            acc += jnp.where((row == j) | (row == j + 1), r[:, :128], 0.0)
            acc += jnp.where((row == j + 2) | (row == j + 3), r[:, 128:], 0.0)
        exs[pl.ds(t0, 16), :] = acc

    for h in range(2):
        at = slice(128 * h, 128 * h + 128)
        heat = exs[pl.ds(h, 64, stride=2), :]
        exd[:, at] = heat
        cold = stepped[2, 15, :, at]
        warm[:, at] = cold + 0.5 * (heat - cold)
    late = [
        pltpu.make_async_copy(exd, ex, sem.at[4]),
        pltpu.make_async_copy(warm, atm.at[2, 15], sem.at[5]),
    ]
    for copy in late:
        copy.start()
    for copy in plain + late:
        copy.wait()
    for g in range(8):
        ocean_out(g).wait()


def remap_back(sst, dd, dt, q, coef, w, stepped, ss, flux):
    return pl.pallas_call(
        back_kernel,
        in_specs=[HERE] * 9,
        out_specs=[AWAY] * 4,
        out_shape=[
            jax.ShapeDtypeStruct((4, 16, 64, 256), F32),
            jax.ShapeDtypeStruct((64, 256), F32),
            jax.ShapeDtypeStruct((64, 48, 256), F32),
            jax.ShapeDtypeStruct((8, 48, 256), F32),
        ],
        scratch_shapes=[
            pltpu.VMEM((384, 128), BF),
            pltpu.VMEM((128, 128), F32),
            pltpu.VMEM((64, 256), F32),
            pltpu.VMEM((64, 256), F32),
            pltpu.VMEM((64, 48, 256), F32),
            pltpu.SemaphoreType.DMA((14,)),
        ],
        compiler_params=pltpu.CompilerParams(vmem_limit_bytes=16 * MIB),
        name="remap_back",
    )(sst, dd, dt, q, coef, w, stepped, ss, flux)


def per_device(atmos, ts, sw, w, dd, dt, mix_a, ocean, mask, seam, mix_o):
    dd, dt = dd.T, dt.T
    send, rows, cols, corn, atm, oce, w = remap_out(atmos, ocean, ts, sw, w, dd, dt, mask)
    stepped, ss, q, flux, sst, coef = exchange(
        send, rows, cols, corn, atm, oce, mask, seam.reshape(1, 256), mix_a, mix_o
    )
    atm, ex, oce, flux = remap_back(sst, dd, dt, q, coef, w, stepped, ss, flux)
    return atm, ex, oce.reshape(ocean.shape), flux


def solution(mesh):
    field = P(None, None, "lat", "lon")
    plane = P("lat", "lon")
    tiles = P(("lon", "lat"), None)
    return jax.shard_map(
        per_device,
        mesh=mesh,
        in_specs=(field, plane, plane, P(("lon", "lat"), None, None, None), tiles, tiles, P(), field, plane, P("lon"), P()),
        out_specs=(field, plane, field, P(None, "lat", "lon")),
        check_vma=False,
    )
```

```python
import functools

import jax
import jax.numpy as jnp
from jax import lax
from jax.experimental import pallas as pl
from jax.experimental.pallas import tpu as pltpu
from jax.sharding import PartitionSpec as P

F32 = jnp.float32
BF = jnp.bfloat16
MESH = pl.DeviceIdType.MESH
HIGHEST = lax.Precision.HIGHEST
NT = (((1,), (1,)), ((), ()))
TN = (((0,), (0,)), ((), ()))
N_LON = 8
N_LAT = 16
CHUNKS = 8
EARLY = 4
FIRST = 4
MIB = 2**20


def flux_fields(u, v, ta, qa, ts, sw):
    speed = jnp.sqrt(u * u + v * v + 1.0)
    soft = jnp.maximum(qa, 0.0) + jnp.log1p(jnp.exp(-jnp.abs(qa)))
    return [
        0.8 * speed * u,
        0.8 * speed * v,
        0.6 * speed * (ts - ta),
        0.5 * speed * (0.4 * jnp.exp(0.5 * ts) - qa),
        0.3 * (ta - ts) * (2.0 + jnp.tanh(ta)),
        sw * (0.9 - 0.1 * jnp.tanh(qa)),
        soft,
        0.3 * speed * speed,
    ]


def slot_rows(owner, tile):
    lon = lax.axis_index("lon")
    lat = lax.axis_index("lat")
    lon_offset = ((owner >> 4) - lon + 1) & 7
    lat_offset = (owner & 15) - lat + 1
    return (lon_offset * 3 + lat_offset) * 96 + tile


def one_hot_slots(dd, dt, k):
    slot = slot_rows(dd[k : k + 1, :], dt[k : k + 1, :])
    rows = lax.broadcasted_iota(jnp.int32, (864, 128), 0)
    return jnp.where(slot == rows, 1.0, 0.0).astype(BF)


HERE = pl.BlockSpec(memory_space=pltpu.VMEM)
AWAY = pl.BlockSpec(memory_space=pltpu.HBM)


def step(x, rate):
    rows, lanes = x.shape
    around = pltpu.roll(x, 1, 0) + pltpu.roll(x, rows - 1, 0) + pltpu.roll(x, 1, 1) + pltpu.roll(x, lanes - 1, 1)
    return (1.0 - 4.0 * rate) * x + rate * around


def step_from(x, around, rate):
    return (1.0 - 4.0 * rate) * x + rate * around


def unpacked(from_left, from_right, n):
    lane = lax.broadcasted_iota(jnp.int32, from_left.shape, 1)
    right = pltpu.roll(from_right, (128 - 2 * n) & 127, 1)
    left = pltpu.roll(from_left, 126 - 2 * n, 1)
    return jnp.where(lane < 2, right, jnp.where(lane >= 126, left, 0.0))


def two_rows(at, first, second):
    rows = lax.broadcasted_iota(jnp.int32, (8, first.shape[1]), 0)
    return jnp.where(rows == at, first, jnp.where(rows == at + 1, second, 0.0))


def framed(x, south, north, third):
    return jnp.concatenate([jnp.concatenate([south, x, north], axis=0), third], axis=1)


def lateral(parts, tri):
    rows = parts[0].shape[0]
    total = jnp.dot(jnp.concatenate(parts, axis=0).astype(BF), tri, preferred_element_type=F32)
    return [total[n * rows : (n + 1) * rows] for n in range(len(parts))]


def near(x, inner, above, below, ghost):
    rows = x.shape[0]
    lane = lax.broadcasted_iota(jnp.int32, (rows, 128), 1)
    row = lax.broadcasted_iota(jnp.int32, (8, 256), 0)
    up = pltpu.roll(x, 1, 0)
    down = pltpu.roll(x, rows - 1, 0)
    up = jnp.concatenate([jnp.where(row == 0, above, up[0:8]), up[8:]], axis=0)
    down = jnp.concatenate([down[: rows - 8], jnp.where(row == 7, below, down[rows - 8 :])], axis=0)
    edges = jnp.concatenate([jnp.where(lane == 0, ghost, 0.0), jnp.where(lane == 127, ghost, 0.0)], axis=1)
    return up + down + inner + edges


def beside(x, ghost, lane):
    t0, t1 = x[:, 0:128], x[:, 128:256]
    r0, r1 = pltpu.roll(t0, 1, 1), pltpu.roll(t1, 1, 1)
    l0, l1 = pltpu.roll(t0, 127, 1), pltpu.roll(t1, 127, 1)
    first, last = lane == 0, lane == 127
    s0 = jnp.where(first, ghost, r0) + jnp.where(last, l1, l0)
    s1 = jnp.where(first, r0, r1) + jnp.where(last, ghost, l1)
    return jnp.concatenate([s0, s1], axis=1)


def beside_packed(left, right, own_left, own_right, odd):
    centre = jnp.where(odd, left, right)
    outer = jnp.where(odd, pltpu.roll(left, 1, 1), pltpu.roll(right, 127, 1))
    inner = jnp.where(odd, pltpu.roll(own_left, 1, 1), pltpu.roll(own_right, 127, 1))
    return centre, outer + inner


def corner_lanes(centre, row):
    lane = lax.broadcasted_iota(jnp.int32, (64, 128), 1)
    field = lax.broadcasted_iota(jnp.int32, (64, 128), 0)
    line = jnp.broadcast_to(centre[row : row + 1, :], (64, 128))
    left = jnp.sum(jnp.where(lane == 2 * field + 1, line, 0.0), axis=1, keepdims=True)
    right = jnp.sum(jnp.where(lane == 2 * field, line, 0.0), axis=1, keepdims=True)
    return jnp.where(lane == 0, left, jnp.where(lane == 127, right, 0.0))


def spread(mixer, cells):
    size = 16 * cells
    pick = lambda dim: jnp.where(
        lax.broadcasted_iota(jnp.int32, (size, 16) if dim == 0 else (16, size), dim) // cells
        == lax.broadcasted_iota(jnp.int32, (size, 16) if dim == 0 else (16, size), 1 - dim),
        1.0,
        0.0,
    )
    dot = functools.partial(jnp.dot, precision=HIGHEST, preferred_element_type=F32)
    full = dot(dot(pick(0), mixer), pick(1))
    r = lax.broadcasted_iota(jnp.int32, (size, size), 0) % cells
    c = lax.broadcasted_iota(jnp.int32, (size, size), 1) % cells
    return jnp.where(r == c, full, 0.0)


def halves(x):
    high = x.astype(BF)
    return high, (x - high.astype(F32)).astype(BF)


def dot3(lhs_high, lhs_low, x):
    high, low = halves(x)
    dot = functools.partial(jnp.dot, preferred_element_type=F32)
    return dot(lhs_high, high) + dot(lhs_high, low) + dot(lhs_low, high)


def exchange_kernel(
    atm_far, oce_far, ts_far, sw_far, dd_far, dt_far, mask_far, w_far, seam, mix_a, mix_o,
    w_here, stepped, ss, q_out, f_out, sst_out, coef_out,
    atm, oce, surf, heat, sun, dd, dt, mask, ft, terms, oh, tb, rbuf, rows, cols, corn, send,
    bc, pr, ro, rl, sl, rr, cc, kk, fr, rrf, cea, ceo, mext, fold, gsa, gso, gea, geo, tri,
    ka, ko, fs, dr_s, dr_r, dc_s, dc_r, dk_r, fd, drf, ced, gd, sst_s, sst_r,
    sem, lsem, ssem, rsem,
):
    lon = lax.axis_index("lon")
    lat = lax.axis_index("lat")
    side = lax.rem(lat, 2)
    partner = lat + 1 - 2 * side
    outer = lat - 1 + 2 * side
    has_outer = jnp.logical_and(outer >= 0, outer < N_LAT)
    has_south = lat > 0
    has_north = lat < N_LAT - 1
    top = lat == N_LAT - 1
    always = lat >= 0
    lon_at = lambda d: lax.rem(lon + d + N_LON, N_LON)

    def lat_ok(d):
        return always if d == 0 else (has_south if d < 0 else has_north)

    def send_to(cond, src, dst, n, m, dev_lon, dev_lat):
        copy = pltpu.make_async_remote_copy(
            src_ref=src, dst_ref=dst, send_sem=ssem.at[n], recv_sem=rsem.at[m],
            device_id=(dev_lon, dev_lat), device_id_type=MESH,
        )

        @pl.when(cond)
        def _():
            copy.start()

        def finish():
            @pl.when(cond)
            def _():
                copy.wait_send()

        pending.append(finish)

    def arrive(cond, dst, m):
        @pl.when(cond)
        def _():
            pltpu.make_async_remote_copy(
                src_ref=dst, dst_ref=dst, send_sem=ssem.at[0], recv_sem=rsem.at[m],
                device_id=(lon, partner), device_id_type=MESH,
            ).wait_recv()

    pending = []
    barrier = pltpu.get_barrier_semaphore()
    around = [(dl, dn) for dl in (-1, 0, 1) for dn in (-1, 0, 1) if (dl, dn) != (0, 0)]
    for dl, dn in around:

        @pl.when(lat_ok(dn))
        def _(dl=dl, dn=dn):
            pl.semaphore_signal(barrier, inc=1, device_id=(lon_at(dl), lat + dn), device_id_type=MESH)

    @pl.when(top)
    def _():
        for d in range(2, N_LON - 1):
            pl.semaphore_signal(barrier, inc=1, device_id=(lon_at(d), lat), device_id_type=MESH)

    chunk = 128 // CHUNKS
    copies = [
        pltpu.make_async_copy(atm_far.at[:, 15], surf, sem.at[0]),
        pltpu.make_async_copy(ts_far, heat, sem.at[1]),
        pltpu.make_async_copy(sw_far, sun, sem.at[2]),
        pltpu.make_async_copy(mask_far, mask, sem.at[5 + CHUNKS]),
    ]
    targets = [
        pltpu.make_async_copy(dd_far, dd, sem.at[6 + CHUNKS]),
        pltpu.make_async_copy(dt_far, dt, sem.at[7 + CHUNKS]),
    ]
    for copy in targets:
        copy.start()
    weights = lambda i: pltpu.make_async_copy(
        w_far.at[pl.ds(i * chunk, chunk)], w_here.at[pl.ds(i * chunk, chunk)], sem.at[3 + i]
    )
    fields = [
        pltpu.make_async_copy(atm_far, atm, sem.at[3 + CHUNKS]),
        pltpu.make_async_copy(oce_far, oce, sem.at[4 + CHUNKS]),
    ]
    for copy in copies:
        copy.start()
    for i in range(EARLY):
        weights(i).start()
    for copy in fields:
        copy.start()
    for i in range(EARLY, CHUNKS):
        weights(i).start()

    for copy in targets:
        copy.wait()
    for k in range(3):
        oh[:, k * 128 : (k + 1) * 128] = one_hot_slots(dd, dt, k)
    for copy in copies:
        copy.wait()
    for f, val in enumerate(flux_fields(surf[0], surf[1], surf[2], surf[3], heat[...], sun[...])):
        val = val.astype(BF).astype(F32)
        ft[pl.ds(f, 64, stride=16), :] = val[:, :128]
        ft[pl.ds(8 + f, 64, stride=16), :] = val[:, 128:]

    group = lax.broadcasted_iota(jnp.int32, (32, 128), 0)
    even = (group & 8) == 0

    def remap_chunk(i):
        weights(i).wait()
        for j in range(0, chunk, 4):
            t = i * chunk + j
            a = ft[pl.ds(pl.multiple_of(t * 8, 32), 32), :]
            lhs = jnp.concatenate([jnp.where(even, a, 0.0), jnp.where(even, 0.0, a)], axis=1).astype(BF)
            quad = [[w_here[t + q, k] for k in range(3)] for q in range(4)]
            for h in range(2):
                p, q = quad[2 * h], quad[2 * h + 1]
                block = jnp.concatenate([jnp.concatenate(p[:2], axis=1), jnp.concatenate(q[:2], axis=1)], axis=0)
                r = jnp.dot(lhs[16 * h : 16 * h + 16], block, preferred_element_type=F32)
                for k in range(2):
                    terms[pl.ds(pl.multiple_of((k * 128 + t + 2 * h) * 8, 16), 16), :] = r[:, k * 128 : (k + 1) * 128]
            block = jnp.concatenate(
                [
                    jnp.concatenate([quad[0][2], quad[2][2]], axis=1),
                    jnp.concatenate([quad[1][2], quad[3][2]], axis=1),
                ],
                axis=0,
            )
            r = jnp.dot(lhs, block, preferred_element_type=F32)
            at = pl.multiple_of((256 + t) * 8, 32)
            terms[pl.ds(at, 16), :] = r[:16, :128]
            terms[pl.ds(at + 16, 16), :] = r[16:, 128:]

    @pl.loop(0, EARLY)
    def _(i):
        remap_chunk(i)

    for copy in fields:
        copy.wait()
    lane_a = lax.broadcasted_iota(jnp.int32, (64, 128), 1) >> 1
    lane_o = lax.broadcasted_iota(jnp.int32, (48, 128), 1) >> 1
    za = jnp.zeros((64, 128), F32)
    zo = jnp.zeros((48, 128), F32)

    @pl.loop(0, 16, init_carry=(za, za, zo, zo))
    def packed(l, carry):
        left_a, right_a, left_o, right_o = carry
        for v in range(4):
            n = v * 16 + l
            ahead = 2 * n
            back = (2 * n + 2) & 127
            left_a = jnp.where(lane_a == n, pltpu.roll(atm[v, l, :, 0:128], ahead, 1), left_a)
            right_a = jnp.where(lane_a == n, pltpu.roll(atm[v, l, :, 128:256], back, 1), right_a)
            left_o = jnp.where(lane_o == n, pltpu.roll(oce[v, l, :, 0:128], ahead, 1), left_o)
            right_o = jnp.where(lane_o == n, pltpu.roll(oce[v, l, :, 128:256], back, 1), right_o)
            for e in range(2):
                rbuf[e, pl.ds(n, 1), :] = atm[v, l, e : e + 1, :]
                rbuf[2 + e, pl.ds(n, 1), :] = atm[v, l, 62 + e : 63 + e, :]
                rbuf[e, pl.ds(64 + n, 1), :] = oce[v, l, e : e + 1, :]
                rbuf[2 + e, pl.ds(64 + n, 1), :] = oce[v, l, 46 + e : 47 + e, :]
        return left_a, right_a, left_o, right_o

    sea = mask[...].astype(F32)
    for a in range(2):
        cols_a, cols_o = packed[a], packed[2 + a]
        cols[a, 0:64, :] = cols_a.astype(BF)
        cols[a, 64:112, :] = cols_o.astype(BF)
        cols[a, 112:160, :] = sea[:, 128 * a : 128 * a + 128].astype(BF)
        corn[2 * a, 0:16, :] = cols_a[0:16].astype(BF)
        corn[2 * a, 16:32, :] = cols_o[0:16].astype(BF)
        corn[2 * a + 1, 0:16, :] = cols_a[48:64].astype(BF)
        corn[2 * a + 1, 16:32, :] = cols_o[32:48].astype(BF)
    for e in range(2):
        for b in range(2):
            r = 46 * b + e
            rbuf[2 * b + e, 128:144, :] = jnp.broadcast_to(sea[r : r + 1, :], (16, 256))
    rows[...] = rbuf[...].astype(BF)

    @pl.when(top)
    def _():
        pl.semaphore_wait(barrier, 5 + 5)

    @pl.when(lat == 0)
    def _():
        pl.semaphore_wait(barrier, 5)

    @pl.when(jnp.logical_and(has_south, has_north))
    def _():
        pl.semaphore_wait(barrier, 8)

    direction = {pair: n for n, pair in enumerate(around)}

    def halo(first, rows_s, rows_r, cols_s, cols_r, corn_s, corn_r):
        for dl, dn in around:
            n = first + direction[(dl, dn)]
            back = first + direction[(-dl, -dn)]
            if dl == 0:
                src, dst = rows_s(max(dn, 0)), rows_r(max(-dn, 0))
            elif dn == 0:
                src, dst = cols_s(max(dl, 0)), cols_r(max(-dl, 0))
            else:
                src, dst = corn_s(max(dl, 0), max(dn, 0)), corn_r(max(-dl, 0), max(-dn, 0))
            send_to(lat_ok(dn), src, dst, n, back, lon_at(dl), lat + dn)

    def halo_arrive(first, rows_r, cols_r, corn_r):
        for dl, dn in around:
            n = first + direction[(dl, dn)]
            if dl == 0:
                dst = rows_r(max(dn, 0))
            elif dn == 0:
                dst = cols_r(max(dl, 0))
            else:
                dst = corn_r(max(dl, 0), max(dn, 0))
            arrive(lat_ok(dn), dst, n)

    def ring(first, src, landing):
        for d in range(1, N_LON):
            send_to(top, src, landing.at[lon], first + d, first + lon, lon_at(d), lat)

    def ring_arrive(first, landing):
        for d in range(1, N_LON):
            arrive(top, landing.at[lon_at(d)], first + lon_at(d))

    rows_r = lambda b: rr.at[b]
    cols_r = lambda a: cc.at[a]
    corn_r = lambda a, b: kk.at[2 * a + b]
    halo(0, lambda b: rows.at[pl.ds(2 * b, 2)], rows_r, lambda a: cols.at[a], cols_r, lambda a, b: corn.at[2 * a + b], corn_r)
    fold_src = rows.at[pl.ds(2, 2), pl.ds(64, 80)]
    ring(8, fold_src, fr)
    own_fold = pltpu.make_async_copy(fold_src, fr.at[lon], lsem.at[0])

    @pl.when(top)
    def _():
        own_fold.start()

    @pl.loop(EARLY, CHUNKS)
    def _(i):
        remap_chunk(i)

    for f in range(8):
        tb[:, f * 128 : (f + 1) * 128] = terms[pl.ds(f, 384, stride=8), :].astype(BF)
    for g in range(4):
        res = jnp.dot(oh[...], tb[:, g * 256 : (g + 1) * 256], preferred_element_type=F32)
        for o in range(9):
            for b in range(2):
                send[o, 2 * g + b] = res[o * 96 : (o + 1) * 96, b * 128 : (b + 1) * 128].astype(BF)


    for dl in (0, 2, 1):
        send_to(always, send.at[dl * 3 + 2 - 2 * side], pr.at[dl], 16 + dl, 16 + dl, lon, partner)
    for dl in range(3):
        send_to(has_outer, send.at[dl * 3 + 2 * side], ro.at[dl], 19 + dl, 19 + dl, lon_at(dl - 1), outer)

    @pl.when(jnp.logical_not(has_outer))
    def _():
        ro[...] = jnp.zeros_like(ro)

    for b, cond in ((0, has_south), (1, has_north)):

        @pl.when(jnp.logical_not(cond))
        def _(b=b):
            rr[b] = jnp.zeros(rr.shape[1:], BF)
            dr_r[b] = jnp.zeros(dr_r.shape[1:], BF)
            for a in range(2):
                kk[2 * a + b] = jnp.zeros(kk.shape[1:], BF)
                dk_r[2 * a + b] = jnp.zeros(dk_r.shape[1:], BF)
            for dl in range(3):
                sst_r[dl * 3 + 2 * b] = jnp.zeros(sst_r.shape[1:], BF)

    ma = mix_a[...]
    mo = mix_o[...]
    dot = functools.partial(jnp.dot, precision=HIGHEST, preferred_element_type=F32)
    ma2 = dot(ma, ma)
    mo2 = dot(mo, mo)
    ka[0], ka[1] = halves(spread(ma2, 16))
    ko[0, :, 0:128], ko[1, :, 0:128] = halves(spread(mo2, 8))
    ko[0, :, 128:256], ko[1, :, 128:256] = halves(spread(mo, 8))
    coef = jnp.broadcast_to(mo2[:, 0:1], (16, 128))
    coef_out[...] = coef

    @pl.when(top)
    def _():
        lane = lax.broadcasted_iota(jnp.int32, (1, 384), 1)
        column = lon * 256 + jnp.where(lane < 320, lane, lane - 384)
        pole = seam[0:1, 0:1] + lon * 256
        source = (pole - column) & 2047
        for j in range(8):
            fold[j * 256 : (j + 1) * 256, :] = jnp.where(
                lax.broadcasted_iota(jnp.int32, (256, 384), 0) + j * 256 == source, 1.0, 0.0
            ).astype(BF)

    halo_arrive(0, rows_r, cols_r, corn_r)
    for b in range(2):
        for e in range(2):
            rrf[b, e] = rr[b, e].astype(F32)
    for a in range(2):
        side_cols = cc[a].astype(F32)
        ks = kk[2 * a].astype(F32)
        kn = kk[2 * a + 1].astype(F32)
        cea[a, 0:8, :] = ks[8:16]
        cea[a, 8:72, :] = side_cols[0:64]
        cea[a, 72:80, :] = kn[0:8]
        ceo[a, 0:8, :] = ks[24:32]
        ceo[a, 8:56, :] = side_cols[64:112]
        ceo[a, 56:64, :] = kn[16:24]

    @pl.when(top)
    def _():
        own_fold.wait()
        ring_arrive(8, fr)
        total = jnp.zeros((160, 384), F32)
        for j in range(8):
            total += jnp.dot(fr[j].reshape(160, 256), fold[j * 256 : (j + 1) * 256, :], preferred_element_type=F32)
        n = lax.broadcasted_iota(jnp.int32, (80, 384), 0)
        sign = jnp.where(jnp.logical_and(n >= 32, n < 64), -1.0, 1.0)
        for e in range(2):
            ghost = total[80 * (1 - e) : 80 * (2 - e)] * sign
            if e == 0:
                beyond = ghost[0:64, 256:384]
            rrf[1, e, 64:144, :] = ghost[:, 0:256]
        lane = lax.broadcasted_iota(jnp.int32, (64, 128), 1)
        field = lax.broadcasted_iota(jnp.int32, (64, 128), 0)
        both = jnp.where(lane == 2 * field + 1, beyond[:, 127:128], jnp.where(lane == 2 * field, beyond[:, 0:1], 0.0))
        both = jnp.sum(both, axis=0, keepdims=True)
        ceo[0, 56:57, :] = both
        ceo[1, 56:57, :] = both

    lane_m = lax.broadcasted_iota(jnp.int32, (48, 128), 1)
    sea = mask[...].astype(F32)
    sea_left = cc[0, 112:160, :].astype(F32)
    sea_right = cc[1, 112:160, :].astype(F32)
    third = jnp.where(lane_m < 2, sea_right, jnp.where(lane_m >= 126, sea_left, 0.0))
    none = jnp.zeros((8, 128), F32)
    mext[...] = framed(
        sea,
        two_rows(6, rrf[0, 0, 128:129, :], rrf[0, 1, 128:129, :]),
        two_rows(0, rrf[1, 0, 128:129, :], rrf[1, 1, 128:129, :]),
        jnp.concatenate([none, third, none], axis=0),
    )
    lane_f = lax.broadcasted_iota(jnp.int32, (64, 128), 1)

    def outside(ce, own_at, rows, at, rate, sea_side, sea_rows):
        odd = (lax.broadcasted_iota(jnp.int32, (rows + 16, 128), 1) & 1) == 1
        own = [
            jnp.concatenate([none, cols[a, own_at : own_at + rows, :].astype(F32), none], axis=0)
            for a in range(2)
        ]
        centre, lateral = beside_packed(ce[0], ce[1], own[0], own[1], odd)
        y = step_from(centre, pltpu.roll(centre, 1, 0) + pltpu.roll(centre, rows + 15, 0) + lateral, rate)
        x_side, y_side = centre[8 : 8 + rows], y[8 : 8 + rows]
        pack = lambda x: pltpu.roll(x, 127, 1)
        sides = [pack(x_side), pack(y_side if sea_side is None else y_side * sea_side)]
        if sea_side is not None:
            sides.append(pack(x_side - x_side * sea_side))
        ends = []
        for b in range(2):
            near_row = rrf[b, 1 - b, at : at + 64, :]
            far_row = rrf[b, b, at : at + 64, :]
            own_row = rows_in[2 * b + b, at : at + 64, :].astype(F32)
            ghost = corner_lanes(centre, 7 if b == 0 else rows + 8)
            z = step_from(near_row, far_row + own_row + beside(near_row, ghost, lane_f), rate)
            if sea_side is None:
                ends.append([jnp.where(has_south if b == 0 else has_north, z, 0.0)])
            else:
                ends.append([z * sea_rows[b], near_row - near_row * sea_rows[b]])
        return sides, ends

    rows_in = rows
    odd_m = (lane_m & 1) == 1
    sea_side = jnp.where(odd_m, jnp.broadcast_to(sea_left[:, 127:128], (48, 128)), jnp.broadcast_to(sea_right[:, 0:1], (48, 128)))
    sides, ends = outside(ceo, 64, 48, 64, 0.2, sea_side, [rrf[0, 1, 128:129, :], rrf[1, 0, 128:129, :]])
    for n in range(3):
        gso[n] = sides[n]
    for b in range(2):
        for n in range(2):
            geo[b, n] = ends[b][n]
    sides, ends = outside(cea, 0, 64, 0, 0.15, None, None)
    for n in range(2):
        gsa[n] = sides[n]
    for b in range(2):
        gea[b] = ends[b][0]

    r256 = lax.broadcasted_iota(jnp.int32, (256, 256), 0)
    c256 = lax.broadcasted_iota(jnp.int32, (256, 256), 1)
    tri[...] = jnp.where(jnp.logical_or(r256 == c256 + 1, r256 + 1 == c256), 1.0, 0.0).astype(BF)

    for dl in (0, 2, 1):
        arrive(always, pr.at[dl], 16 + dl)
    for n, dl in enumerate((0, 2)):

        @pl.loop(0, 8)
        def _(f, n=n, dl=dl):
            sl[n, f] = (send[3 * dl + 1, f].astype(F32) + pr[dl, f].astype(F32)).astype(BF)

        send_to(always, sl.at[n], rl.at[n], 22 + n, 22 + n, lon_at(dl - 1), lat)

    @pl.loop(0, 8)
    def _(i):
        v = i // 2
        first = pl.multiple_of(lax.rem(i, 2) * 8, 8)
        lines = pl.ds(pl.multiple_of(i * 8, 8), 8)
        far = pl.ds(pl.multiple_of(64 + i * 8, 8), 8)
        turned = lambda k, j: pltpu.roll(gso[k], (128 - 2 * (i * 8 + j)) & 127, 1)
        wet_here = mext[8:56, 0:256]
        south, north = rrf[0, 1, far, :], rrf[1, 0, far, :]
        xs = [oce[v, first + j] for j in range(8)]
        inner = lateral(xs, tri[...])
        a, c = [], []
        for j, x in enumerate(xs):
            around = near(x, inner[j], south[j : j + 1], north[j : j + 1], turned(0, j))
            a.append(wet_here * step_from(x, around, 0.2))
            c.append(x - wet_here * x)
        for k, parts in enumerate((a, c)):
            inner = lateral(parts, tri[...])
            south, north = geo[0, k, lines, :], geo[1, k, lines, :]
            for j, x in enumerate(parts):
                around = near(x, inner[j], south[j : j + 1], north[j : j + 1], turned(1 + k, j))
                bc[v, 16 * k + first + j] = step_from(x, around, 0.2)

    @pl.loop(0, 24, unroll=3)
    def _(n):
        v = n // 6
        at = pl.multiple_of(lax.rem(n, 6) * 8, 8)
        mixed = dot3(ko[0], ko[1], bc[v, :, pl.ds(at, 8), :].reshape(256, 256)).reshape(16, 8, 256)
        wet = mask[pl.ds(at, 8), :] > 0
        ss[v, :, pl.ds(at, 8), :] = jnp.where(wet[None], mixed, oce[v, :, pl.ds(at, 8), :])

    def atm_group(i):
        v = i // 2
        first = pl.multiple_of(lax.rem(i, 2) * 8, 8)
        lines = pl.ds(pl.multiple_of(i * 8, 8), 8)
        turned = lambda k, j: pltpu.roll(gsa[k], (128 - 2 * (i * 8 + j)) & 127, 1)
        parts = [atm[v, first + j] for j in range(8)]
        ends = ((rrf[0, 1, lines, :], rrf[1, 0, lines, :]), (gea[0, lines, :], gea[1, lines, :]))
        for k in range(2):
            inner = lateral(parts, tri[...])
            south, north = ends[k]
            parts = [
                step_from(x, near(x, inner[j], south[j : j + 1], north[j : j + 1], turned(k, j)), 0.15)
                for j, x in enumerate(parts)
            ]
        for j, y in enumerate(parts):
            stepped[v, first + j] = y

    @pl.loop(0, FIRST)
    def _(i):
        atm_group(i)

    for dl in range(3):
        arrive(has_outer, ro.at[dl], 19 + dl)
    for n in range(2):
        arrive(always, rl.at[n], 22 + n)

    @pl.loop(0, 8)
    def _(f):
        parts = [send[4, f], pr[1, f], rl[0, f], rl[1, f], ro[0, f], ro[1, f], ro[2, f]]
        total = functools.reduce(lambda x, y: x + y, [p.astype(F32) for p in parts])
        fs[pl.ds(pl.multiple_of(f * 96, 8), 96), :] = total

    flux = []
    for f in range(8):
        value = sea * jnp.concatenate([fs[pl.ds(f * 96 + h, 48, stride=2), :] for h in range(2)], axis=1)
        f_out[f] = value
        flux.append(value)
    forcing = [
        0.2 * sea * (flux[5] - flux[2] - flux[3] - flux[4]),
        0.2 * sea * (flux[3] - flux[6]),
        sea * (0.3 * flux[0] - 0.1 * flux[7] * oce[2, 0]),
        sea * (0.3 * flux[1] - 0.1 * flux[7] * oce[3, 0]),
    ]

    left = jnp.zeros((48, 128), F32)
    right = jnp.zeros((48, 128), F32)
    edge = [[jnp.zeros((16, 256), F32) for _ in range(2)] for _ in range(2)]
    row_16 = lax.broadcasted_iota(jnp.int32, (16, 256), 0)
    for f, d in enumerate(forcing):
        left = jnp.where((lane_m >> 1) == f, pltpu.roll(d[:, 0:128], 2 * f, 1) if f else d[:, 0:128], left)
        right = jnp.where((lane_m >> 1) == f, pltpu.roll(d[:, 128:256], 2 * f + 2, 1), right)
        for b in range(2):
            for e in range(2):
                r = 46 * b + e
                edge[b][e] = jnp.where(row_16 == f, d[r : r + 1, :], edge[b][e])
    dc_s[0] = left.astype(BF)
    dc_s[1] = right.astype(BF)
    for b in range(2):
        for e in range(2):
            dr_s[b, 16 * e : 16 * e + 16, :] = edge[b][e].astype(BF)
    rows_r = lambda b: dr_r.at[b]
    cols_r = lambda a: dc_r.at[a]
    corn_r = lambda a, b: dk_r.at[2 * a + b]
    halo(24, lambda b: dr_s.at[b], rows_r, lambda a: dc_s.at[a], cols_r,
         lambda a, b: dc_s.at[a, pl.ds(32 * b, 16)], corn_r)
    ring(32, dr_s.at[1], fd)

    @pl.when(top)
    def _():
        fd[lon] = dr_s[1]

    @pl.loop(FIRST, 8)
    def _(i):
        atm_group(i)

    halo_arrive(24, rows_r, cols_r, corn_r)
    for b in range(2):
        drf[b] = dr_r[b].astype(F32)
    for a in range(2):
        ced[a, 0:8, :] = dk_r[2 * a].astype(F32)[8:16]
        ced[a, 8:56, :] = dc_r[a].astype(F32)
        ced[a, 56:64, :] = dk_r[2 * a + 1].astype(F32)[0:8]

    @pl.when(top)
    def _():
        ring_arrive(32, fd)
        total = jnp.zeros((32, 384), F32)
        for j in range(8):
            total += jnp.dot(fd[j], fold[j * 256 : (j + 1) * 256, :], preferred_element_type=F32)
        n = lax.broadcasted_iota(jnp.int32, (16, 384), 0)
        sign = jnp.where(n >= 2, -1.0, 1.0)
        for e in range(2):
            gd[e] = total[16 * (1 - e) : 16 * (2 - e)] * sign
            drf[1, 16 * e : 16 * e + 16, :] = gd[e][:, 0:256]

    @pl.when(jnp.logical_not(top))
    def _():
        gd[...] = jnp.zeros_like(gd)

    m = mext[...]
    for f, d in enumerate(forcing):
        third = unpacked(ced[0], ced[1], f)
        north = jnp.where(top, two_rows(0, gd[0, f : f + 1, 256:384], gd[1, f : f + 1, 256:384]), third[56:64])
        x = framed(
            d,
            two_rows(6, drf[0, f : f + 1, :], drf[0, 16 + f : 17 + f, :]),
            two_rows(0, drf[1, f : f + 1, :], drf[1, 16 + f : 17 + f, :]),
            jnp.concatenate([third[0:56], north], axis=0),
        )
        q = sea * step(m * step(x, 0.2), 0.2)[8:56, 0:256]
        q_out[f] = q
        if f == 0:
            c00 = jnp.concatenate([coef[0:1, :], coef[0:1, :]], axis=1)
            heat = sea * (ss[0, 0] + c00 * q)
            for h in range(2):
                fs[pl.ds(h, 48, stride=2), :] = heat[:, 128 * h : 128 * h + 128]
            sst_s[...] = fs[0:96, :].astype(BF)
            for dl, dn in around:
                n = 40 + direction[(dl, dn)]
                back = 40 + direction[(-dl, -dn)]
                slot = (1 - dl) * 3 + 1 - dn
                send_to(lat_ok(dn), sst_s, sst_r.at[slot], n, back, lon_at(dl), lat + dn)
    @pl.loop(0, 16, unroll=4)
    def _(n):
        v = n // 4
        at = pl.multiple_of(lax.rem(n, 4) * 16, 16)
        mixed = dot3(ka[0], ka[1], stepped[v, :, pl.ds(at, 16), :].reshape(256, 256))
        stepped[v, :, pl.ds(at, 16), :] = mixed.reshape(16, 16, 256)

    sst_r[4] = sst_s[...]
    for dl, dn in around:
        arrive(lat_ok(dn), sst_r.at[(1 + dl) * 3 + 1 + dn], 40 + direction[(dl, dn)])
    sst_out[...] = sst_r[...]
    for finish in pending:
        finish()


def exchange(atm, oce, ts, sw, w, dd, dt, mask, seam, mix_a, mix_o):
    far = [pltpu.with_memory_space_constraint(x, pltpu.HBM) for x in (atm, oce, ts, sw, dd, dt, mask, w)]
    return pl.pallas_call(
        exchange_kernel,
        in_specs=[AWAY] * 8 + [HERE] * 3,
        out_specs=[HERE] * 7,
        out_shape=[
            pltpu.VMEM((128, 3, 128, 128), BF),
            pltpu.VMEM((4, 16, 64, 256), F32),
            pltpu.VMEM((4, 16, 48, 256), F32),
            pltpu.VMEM((4, 48, 256), F32),
            pltpu.VMEM((8, 48, 256), F32),
            pltpu.VMEM((9, 96, 128), BF),
            pltpu.VMEM((16, 128), F32),
        ],
        scratch_shapes=[
            pltpu.VMEM((4, 16, 64, 256), F32),
            pltpu.VMEM((4, 16, 48, 256), F32),
            pltpu.VMEM((4, 64, 256), F32),
            pltpu.VMEM((64, 256), F32),
            pltpu.VMEM((64, 256), F32),
            pltpu.VMEM((3, 128), jnp.int32),
            pltpu.VMEM((3, 128), jnp.int32),
            pltpu.VMEM((48, 256), jnp.int32),
            pltpu.VMEM((1024, 128), F32),
            pltpu.VMEM((3072, 128), F32),
            pltpu.VMEM((864, 384), BF),
            pltpu.VMEM((384, 1024), BF),
            pltpu.VMEM((4, 144, 256), F32),
            pltpu.VMEM((4, 144, 256), BF),
            pltpu.VMEM((2, 160, 128), BF),
            pltpu.VMEM((4, 32, 128), BF),
            pltpu.VMEM((9, 8, 96, 128), BF),
            pltpu.VMEM((4, 32, 48, 256), F32),
            pltpu.VMEM((3, 8, 96, 128), BF),
            pltpu.VMEM((3, 8, 96, 128), BF),
            pltpu.VMEM((2, 8, 96, 128), BF),
            pltpu.VMEM((2, 8, 96, 128), BF),
            pltpu.VMEM((2, 2, 144, 256), BF),
            pltpu.VMEM((2, 160, 128), BF),
            pltpu.VMEM((4, 32, 128), BF),
            pltpu.VMEM((8, 2, 80, 256), BF),
            pltpu.VMEM((2, 2, 144, 256), F32),
            pltpu.VMEM((2, 80, 128), F32),
            pltpu.VMEM((2, 64, 128), F32),
            pltpu.VMEM((64, 384), F32),
            pltpu.VMEM((2048, 384), BF),
            pltpu.VMEM((2, 64, 128), F32),
            pltpu.VMEM((3, 48, 128), F32),
            pltpu.VMEM((2, 64, 256), F32),
            pltpu.VMEM((2, 2, 64, 256), F32),
            pltpu.VMEM((256, 256), BF),
            pltpu.VMEM((2, 256, 256), BF),
            pltpu.VMEM((2, 128, 256), BF),
            pltpu.VMEM((768, 128), F32),
            pltpu.VMEM((2, 32, 256), BF),
            pltpu.VMEM((2, 32, 256), BF),
            pltpu.VMEM((2, 48, 128), BF),
            pltpu.VMEM((2, 48, 128), BF),
            pltpu.VMEM((4, 16, 128), BF),
            pltpu.VMEM((8, 32, 256), BF),
            pltpu.VMEM((2, 32, 256), F32),
            pltpu.VMEM((2, 64, 128), F32),
            pltpu.VMEM((2, 16, 384), F32),
            pltpu.VMEM((96, 128), BF),
            pltpu.VMEM((9, 96, 128), BF),
            pltpu.SemaphoreType.DMA((8 + CHUNKS,)),
            pltpu.SemaphoreType.DMA((1,)),
            pltpu.SemaphoreType.DMA((48,)),
            pltpu.SemaphoreType.DMA((48,)),
        ],
        compiler_params=pltpu.CompilerParams(collective_id=0, has_side_effects=True, vmem_limit_bytes=36 * MIB),
        name="exchange",
    )(*far, seam, mix_a, mix_o)


def back_kernel(sst, dd, dt, q, coef, w, stepped, ss, flux, atm, ex, oce, f_out, sel, exs, exd, warm, sea, sem):
    plain = [
        pltpu.make_async_copy(flux, f_out, sem.at[0]),
        pltpu.make_async_copy(stepped.at[pl.ds(0, 2)], atm.at[pl.ds(0, 2)], sem.at[1]),
        pltpu.make_async_copy(stepped.at[2, pl.ds(0, 15)], atm.at[2, pl.ds(0, 15)], sem.at[2]),
        pltpu.make_async_copy(stepped.at[3], atm.at[3], sem.at[3]),
    ]
    for copy in plain:
        copy.start()
    heat = sst[...].reshape(864, 128)
    for k in range(3):
        picked = lax.dot_general(one_hot_slots(dd, dt, k), heat, TN, preferred_element_type=F32)
        sel[k * 128 : (k + 1) * 128, :] = picked.astype(BF)

    row = lax.broadcasted_iota(jnp.int32, (16, 128), 0)
    even = (row & 1) == 0
    ocean_out = lambda g: pltpu.make_async_copy(sea.at[pl.ds(g * 8, 8)], oce.at[pl.ds(g * 8, 8)], sem.at[6 + g])

    @pl.loop(0, 8)
    def _(g):
        v = g // 2
        for j in range(8):
            l = lax.rem(g, 2) * 8 + j
            c = coef[pl.ds(l, 1), :]
            sea[g * 8 + j] = ss[v, l] + jnp.concatenate([c, c], axis=1) * q[v]
        ocean_out(g).start()
        acc = jnp.zeros((16, 128), F32)
        t0 = pl.multiple_of(g * 16, 16)
        part = [sel[pl.ds(pl.multiple_of(k * 128 + t0, 16), 16), :] for k in range(3)]
        lhs = jnp.concatenate(part[:2], axis=1)
        last = part[2].astype(F32)
        split = jnp.concatenate([jnp.where(even, last, 0.0), jnp.where(even, 0.0, last)], axis=1).astype(BF)
        for j in range(0, 16, 4):
            quad = [[w[t0 + j + n, k] for k in range(3)] for n in range(4)]
            for h in range(2):
                p0, p1 = quad[2 * h], quad[2 * h + 1]
                block = jnp.concatenate([jnp.concatenate(p0[:2], axis=1), jnp.concatenate(p1[:2], axis=1)], axis=0)
                r = lax.dot_general(lhs, block, NT, preferred_element_type=F32)
                acc += jnp.where(row == j + 2 * h, r[:, :128], 0.0) + jnp.where(row == j + 2 * h + 1, r[:, 128:], 0.0)
            block = jnp.concatenate(
                [
                    jnp.concatenate([quad[0][2], quad[1][2]], axis=1),
                    jnp.concatenate([quad[2][2], quad[3][2]], axis=1),
                ],
                axis=0,
            )
            r = lax.dot_general(split, block, NT, preferred_element_type=F32)
            acc += jnp.where((row == j) | (row == j + 1), r[:, :128], 0.0)
            acc += jnp.where((row == j + 2) | (row == j + 3), r[:, 128:], 0.0)
        exs[pl.ds(t0, 16), :] = acc

    for h in range(2):
        at = slice(128 * h, 128 * h + 128)
        heat = exs[pl.ds(h, 64, stride=2), :]
        exd[:, at] = heat
        cold = stepped[2, 15, :, at]
        warm[:, at] = cold + 0.5 * (heat - cold)
    late = [
        pltpu.make_async_copy(exd, ex, sem.at[4]),
        pltpu.make_async_copy(warm, atm.at[2, 15], sem.at[5]),
    ]
    for copy in late:
        copy.start()
    for copy in plain + late:
        copy.wait()
    for g in range(8):
        ocean_out(g).wait()


def remap_back(sst, dd, dt, q, coef, w, stepped, ss, flux):
    return pl.pallas_call(
        back_kernel,
        in_specs=[HERE] * 9,
        out_specs=[AWAY] * 4,
        out_shape=[
            jax.ShapeDtypeStruct((4, 16, 64, 256), F32),
            jax.ShapeDtypeStruct((64, 256), F32),
            jax.ShapeDtypeStruct((64, 48, 256), F32),
            jax.ShapeDtypeStruct((8, 48, 256), F32),
        ],
        scratch_shapes=[
            pltpu.VMEM((384, 128), BF),
            pltpu.VMEM((128, 128), F32),
            pltpu.VMEM((64, 256), F32),
            pltpu.VMEM((64, 256), F32),
            pltpu.VMEM((64, 48, 256), F32),
            pltpu.SemaphoreType.DMA((14,)),
        ],
        compiler_params=pltpu.CompilerParams(vmem_limit_bytes=16 * MIB),
        name="remap_back",
    )(sst, dd, dt, q, coef, w, stepped, ss, flux)


def per_device(atmos, ts, sw, w, dd, dt, mix_a, ocean, mask, seam, mix_o):
    dd, dt = dd.T, dt.T
    w, stepped, ss, q, flux, sst, coef = exchange(
        atmos, ocean, ts, sw, w, dd, dt, mask, seam.reshape(1, 256), mix_a, mix_o
    )
    atm, ex, oce, flux = remap_back(sst, dd, dt, q, coef, w, stepped, ss, flux)
    return atm, ex, oce.reshape(ocean.shape), flux


def solution(mesh):
    field = P(None, None, "lat", "lon")
    plane = P("lat", "lon")
    tiles = P(("lon", "lat"), None)
    return jax.shard_map(
        per_device,
        mesh=mesh,
        in_specs=(field, plane, plane, P(("lon", "lat"), None, None, None), tiles, tiles, P(), field, plane, P("lon"), P()),
        out_specs=(field, plane, field, P(None, "lat", "lon")),
        check_vma=False,
    )
```

```python
import functools

import jax
import jax.numpy as jnp
from jax import lax
from jax.experimental import pallas as pl
from jax.experimental.pallas import tpu as pltpu
from jax.sharding import PartitionSpec as P

F32 = jnp.float32
BF = jnp.bfloat16
MESH = pl.DeviceIdType.MESH
HIGHEST = lax.Precision.HIGHEST
NT = (((1,), (1,)), ((), ()))
TN = (((0,), (0,)), ((), ()))
N_LON = 8
N_LAT = 16
CHUNKS = 8
FIRST = 4
MIXED = 8
DETOUR = 2
MIB = 2**20


def flux_fields(u, v, ta, qa, ts, sw):
    speed = jnp.sqrt(u * u + v * v + 1.0)
    soft = jnp.maximum(qa, 0.0) + jnp.log1p(jnp.exp(-jnp.abs(qa)))
    return [
        0.8 * speed * u,
        0.8 * speed * v,
        0.6 * speed * (ts - ta),
        0.5 * speed * (0.4 * jnp.exp(0.5 * ts) - qa),
        0.3 * (ta - ts) * (2.0 + jnp.tanh(ta)),
        sw * (0.9 - 0.1 * jnp.tanh(qa)),
        soft,
        0.3 * speed * speed,
    ]


def slot_rows(owner, tile):
    lon = lax.axis_index("lon")
    lat = lax.axis_index("lat")
    lon_offset = ((owner >> 4) - lon + 1) & 7
    lat_offset = (owner & 15) - lat + 1
    return (lon_offset * 3 + lat_offset) * 96 + tile


def one_hot_slots(dd, dt, k):
    slot = slot_rows(dd[k : k + 1, :], dt[k : k + 1, :])
    rows = lax.broadcasted_iota(jnp.int32, (864, 128), 0)
    return jnp.where(slot == rows, 1.0, 0.0).astype(BF)


HERE = pl.BlockSpec(memory_space=pltpu.VMEM)
AWAY = pl.BlockSpec(memory_space=pltpu.HBM)


def step(x, rate):
    rows, lanes = x.shape
    around = pltpu.roll(x, 1, 0) + pltpu.roll(x, rows - 1, 0) + pltpu.roll(x, 1, 1) + pltpu.roll(x, lanes - 1, 1)
    return (1.0 - 4.0 * rate) * x + rate * around


def step_from(x, around, rate):
    return (1.0 - 4.0 * rate) * x + rate * around


def unpacked(from_left, from_right, n):
    lane = lax.broadcasted_iota(jnp.int32, from_left.shape, 1)
    right = pltpu.roll(from_right, (128 - 2 * n) & 127, 1)
    left = pltpu.roll(from_left, 126 - 2 * n, 1)
    return jnp.where(lane < 2, right, jnp.where(lane >= 126, left, 0.0))


def two_rows(at, first, second):
    rows = lax.broadcasted_iota(jnp.int32, (8, first.shape[1]), 0)
    return jnp.where(rows == at, first, jnp.where(rows == at + 1, second, 0.0))


def framed(x, south, north, third):
    return jnp.concatenate([jnp.concatenate([south, x, north], axis=0), third], axis=1)


def lateral(parts, tri):
    rows = parts[0].shape[0]
    total = jnp.dot(jnp.concatenate(parts, axis=0).astype(BF), tri, preferred_element_type=F32)
    return [total[n * rows : (n + 1) * rows] for n in range(len(parts))]


def near(x, inner, above, below, ghost):
    rows = x.shape[0]
    lane = lax.broadcasted_iota(jnp.int32, (rows, 128), 1)
    row = lax.broadcasted_iota(jnp.int32, (8, 256), 0)
    up = pltpu.roll(x, 1, 0)
    down = pltpu.roll(x, rows - 1, 0)
    up = jnp.concatenate([jnp.where(row == 0, above, up[0:8]), up[8:]], axis=0)
    down = jnp.concatenate([down[: rows - 8], jnp.where(row == 7, below, down[rows - 8 :])], axis=0)
    edges = jnp.concatenate([jnp.where(lane == 0, ghost, 0.0), jnp.where(lane == 127, ghost, 0.0)], axis=1)
    return up + down + inner + edges


def beside(x, ghost, lane):
    t0, t1 = x[:, 0:128], x[:, 128:256]
    r0, r1 = pltpu.roll(t0, 1, 1), pltpu.roll(t1, 1, 1)
    l0, l1 = pltpu.roll(t0, 127, 1), pltpu.roll(t1, 127, 1)
    first, last = lane == 0, lane == 127
    s0 = jnp.where(first, ghost, r0) + jnp.where(last, l1, l0)
    s1 = jnp.where(first, r0, r1) + jnp.where(last, ghost, l1)
    return jnp.concatenate([s0, s1], axis=1)


def beside_packed(left, right, own_left, own_right, odd):
    centre = jnp.where(odd, left, right)
    outer = jnp.where(odd, pltpu.roll(left, 1, 1), pltpu.roll(right, 127, 1))
    inner = jnp.where(odd, pltpu.roll(own_left, 1, 1), pltpu.roll(own_right, 127, 1))
    return centre, outer + inner


def corner_lanes(centre, row):
    lane = lax.broadcasted_iota(jnp.int32, (64, 128), 1)
    field = lax.broadcasted_iota(jnp.int32, (64, 128), 0)
    line = jnp.broadcast_to(centre[row : row + 1, :], (64, 128))
    left = jnp.sum(jnp.where(lane == 2 * field + 1, line, 0.0), axis=1, keepdims=True)
    right = jnp.sum(jnp.where(lane == 2 * field, line, 0.0), axis=1, keepdims=True)
    return jnp.where(lane == 0, left, jnp.where(lane == 127, right, 0.0))


def spread(mixer, cells):
    size = 16 * cells
    pick = lambda dim: jnp.where(
        lax.broadcasted_iota(jnp.int32, (size, 16) if dim == 0 else (16, size), dim) // cells
        == lax.broadcasted_iota(jnp.int32, (size, 16) if dim == 0 else (16, size), 1 - dim),
        1.0,
        0.0,
    )
    dot = functools.partial(jnp.dot, precision=HIGHEST, preferred_element_type=F32)
    full = dot(dot(pick(0), mixer), pick(1))
    r = lax.broadcasted_iota(jnp.int32, (size, size), 0) % cells
    c = lax.broadcasted_iota(jnp.int32, (size, size), 1) % cells
    return jnp.where(r == c, full, 0.0)


def halves(x):
    high = x.astype(BF)
    return high, (x - high.astype(F32)).astype(BF)


def dot3(lhs_high, lhs_low, x):
    high, low = halves(x)
    dot = functools.partial(jnp.dot, preferred_element_type=F32)
    return dot(lhs_high, high) + dot(lhs_high, low) + dot(lhs_low, high)


def exchange_kernel(
    atm_far, oce_far, ts_far, sw_far, dd_far, dt_far, mask_far, w_far, seam, mix_a, mix_o,
    w_here, stepped, ss, q_out, f_out, sst_out, coef_out,
    atm, oce, surf, heat, sun, dd, dt, mask, ft, terms, oh, tb, rbuf, rows, cols, corn, send,
    bc, pr, ro, rd, rl, sl, rr, cc, kk, fr, rrf, cea, ceo, mext, fold, gsa, gso, gea, geo, tri,
    ka, ko, fs, dr_s, dr_r, dc_s, dc_r, dk_r, fd, drf, ced, gd, sst_s, sst_r,
    sem, lsem, ssem, rsem,
):
    lon = lax.axis_index("lon")
    lat = lax.axis_index("lat")
    side = lax.rem(lat, 2)
    partner = lat + 1 - 2 * side
    outer = lat - 1 + 2 * side
    has_outer = jnp.logical_and(outer >= 0, outer < N_LAT)
    has_south = lat > 0
    has_north = lat < N_LAT - 1
    top = lat == N_LAT - 1
    always = lat >= 0
    lon_at = lambda d: lax.rem(lon + d + N_LON, N_LON)

    def lat_ok(d):
        return always if d == 0 else (has_south if d < 0 else has_north)

    def send_to(cond, src, dst, n, m, dev_lon, dev_lat):
        copy = pltpu.make_async_remote_copy(
            src_ref=src, dst_ref=dst, send_sem=ssem.at[n], recv_sem=rsem.at[m],
            device_id=(dev_lon, dev_lat), device_id_type=MESH,
        )

        @pl.when(cond)
        def _():
            copy.start()

        def finish():
            @pl.when(cond)
            def _():
                copy.wait_send()

        pending.append(finish)

    def arrive(cond, dst, m):
        @pl.when(cond)
        def _():
            pltpu.make_async_remote_copy(
                src_ref=dst, dst_ref=dst, send_sem=ssem.at[0], recv_sem=rsem.at[m],
                device_id=(lon, partner), device_id_type=MESH,
            ).wait_recv()

    pending = []
    barrier = pltpu.get_barrier_semaphore()
    around = [(dl, dn) for dl in (-1, 0, 1) for dn in (-1, 0, 1) if (dl, dn) != (0, 0)]
    for dl, dn in around:

        @pl.when(lat_ok(dn))
        def _(dl=dl, dn=dn):
            pl.semaphore_signal(barrier, inc=1, device_id=(lon_at(dl), lat + dn), device_id_type=MESH)

    @pl.when(top)
    def _():
        for d in range(2, N_LON - 1):
            pl.semaphore_signal(barrier, inc=1, device_id=(lon_at(d), lat), device_id_type=MESH)

    chunk = 128 // CHUNKS
    copies = [
        pltpu.make_async_copy(atm_far.at[:, 15], surf, sem.at[0]),
        pltpu.make_async_copy(ts_far, heat, sem.at[1]),
        pltpu.make_async_copy(sw_far, sun, sem.at[2]),
        pltpu.make_async_copy(mask_far, mask, sem.at[5 + CHUNKS]),
    ]
    targets = [
        pltpu.make_async_copy(dd_far, dd, sem.at[6 + CHUNKS]),
        pltpu.make_async_copy(dt_far, dt, sem.at[7 + CHUNKS]),
    ]
    for copy in targets:
        copy.start()
    weights = lambda i: pltpu.make_async_copy(
        w_far.at[pl.ds(i * chunk, chunk)], w_here.at[pl.ds(i * chunk, chunk)], sem.at[3 + i]
    )
    fields = [
        pltpu.make_async_copy(atm_far, atm, sem.at[3 + CHUNKS]),
        pltpu.make_async_copy(oce_far, oce, sem.at[4 + CHUNKS]),
    ]
    for copy in copies:
        copy.start()
    for copy in fields:
        copy.start()
    for i in range(CHUNKS):
        weights(i).start()

    for copy in targets:
        copy.wait()
    for k in range(3):
        oh[:, k * 128 : (k + 1) * 128] = one_hot_slots(dd, dt, k)
    for copy in copies:
        copy.wait()
    for f, val in enumerate(flux_fields(surf[0], surf[1], surf[2], surf[3], heat[...], sun[...])):
        val = val.astype(BF).astype(F32)
        ft[pl.ds(f, 64, stride=16), :] = val[:, :128]
        ft[pl.ds(8 + f, 64, stride=16), :] = val[:, 128:]

    group = lax.broadcasted_iota(jnp.int32, (32, 128), 0)
    even = (group & 8) == 0

    def remap_chunk(i):
        weights(i).wait()
        for j in range(0, chunk, 4):
            t = i * chunk + j
            a = ft[pl.ds(pl.multiple_of(t * 8, 32), 32), :]
            lhs = jnp.concatenate([jnp.where(even, a, 0.0), jnp.where(even, 0.0, a)], axis=1).astype(BF)
            quad = [[w_here[t + q, k] for k in range(3)] for q in range(4)]
            for h in range(2):
                p, q = quad[2 * h], quad[2 * h + 1]
                block = jnp.concatenate([jnp.concatenate(p[:2], axis=1), jnp.concatenate(q[:2], axis=1)], axis=0)
                r = jnp.dot(lhs[16 * h : 16 * h + 16], block, preferred_element_type=F32)
                for k in range(2):
                    terms[pl.ds(pl.multiple_of((k * 128 + t + 2 * h) * 8, 16), 16), :] = r[:, k * 128 : (k + 1) * 128]
            block = jnp.concatenate(
                [
                    jnp.concatenate([quad[0][2], quad[2][2]], axis=1),
                    jnp.concatenate([quad[1][2], quad[3][2]], axis=1),
                ],
                axis=0,
            )
            r = jnp.dot(lhs, block, preferred_element_type=F32)
            at = pl.multiple_of((256 + t) * 8, 32)
            terms[pl.ds(at, 16), :] = r[:16, :128]
            terms[pl.ds(at + 16, 16), :] = r[16:, 128:]

    for copy in fields:
        copy.wait()
    lane_a = lax.broadcasted_iota(jnp.int32, (64, 128), 1) >> 1
    lane_o = lax.broadcasted_iota(jnp.int32, (48, 128), 1) >> 1
    za = jnp.zeros((64, 128), F32)
    zo = jnp.zeros((48, 128), F32)

    @pl.loop(0, 16, init_carry=(za, za, zo, zo))
    def packed(l, carry):
        left_a, right_a, left_o, right_o = carry
        for v in range(4):
            n = v * 16 + l
            ahead = 2 * n
            back = (2 * n + 2) & 127
            left_a = jnp.where(lane_a == n, pltpu.roll(atm[v, l, :, 0:128], ahead, 1), left_a)
            right_a = jnp.where(lane_a == n, pltpu.roll(atm[v, l, :, 128:256], back, 1), right_a)
            left_o = jnp.where(lane_o == n, pltpu.roll(oce[v, l, :, 0:128], ahead, 1), left_o)
            right_o = jnp.where(lane_o == n, pltpu.roll(oce[v, l, :, 128:256], back, 1), right_o)
            for e in range(2):
                rbuf[e, pl.ds(n, 1), :] = atm[v, l, e : e + 1, :]
                rbuf[2 + e, pl.ds(n, 1), :] = atm[v, l, 62 + e : 63 + e, :]
                rbuf[e, pl.ds(64 + n, 1), :] = oce[v, l, e : e + 1, :]
                rbuf[2 + e, pl.ds(64 + n, 1), :] = oce[v, l, 46 + e : 47 + e, :]
        return left_a, right_a, left_o, right_o

    sea = mask[...].astype(F32)
    for a in range(2):
        cols_a, cols_o = packed[a], packed[2 + a]
        cols[a, 0:64, :] = cols_a.astype(BF)
        cols[a, 64:112, :] = cols_o.astype(BF)
        cols[a, 112:160, :] = sea[:, 128 * a : 128 * a + 128].astype(BF)
        corn[2 * a, 0:16, :] = cols_a[0:16].astype(BF)
        corn[2 * a, 16:32, :] = cols_o[0:16].astype(BF)
        corn[2 * a + 1, 0:16, :] = cols_a[48:64].astype(BF)
        corn[2 * a + 1, 16:32, :] = cols_o[32:48].astype(BF)
    for e in range(2):
        for b in range(2):
            r = 46 * b + e
            rbuf[2 * b + e, 128:144, :] = jnp.broadcast_to(sea[r : r + 1, :], (16, 256))
    rows[...] = rbuf[...].astype(BF)

    @pl.when(top)
    def _():
        pl.semaphore_wait(barrier, 5 + 5)

    @pl.when(lat == 0)
    def _():
        pl.semaphore_wait(barrier, 5)

    @pl.when(jnp.logical_and(has_south, has_north))
    def _():
        pl.semaphore_wait(barrier, 8)

    direction = {pair: n for n, pair in enumerate(around)}

    def halo(first, rows_s, rows_r, cols_s, cols_r, corn_s, corn_r):
        for dl, dn in around:
            n = first + direction[(dl, dn)]
            back = first + direction[(-dl, -dn)]
            if dl == 0:
                src, dst = rows_s(max(dn, 0)), rows_r(max(-dn, 0))
            elif dn == 0:
                src, dst = cols_s(max(dl, 0)), cols_r(max(-dl, 0))
            else:
                src, dst = corn_s(max(dl, 0), max(dn, 0)), corn_r(max(-dl, 0), max(-dn, 0))
            send_to(lat_ok(dn), src, dst, n, back, lon_at(dl), lat + dn)

    def halo_arrive(first, rows_r, cols_r, corn_r):
        for dl, dn in around:
            n = first + direction[(dl, dn)]
            if dl == 0:
                dst = rows_r(max(dn, 0))
            elif dn == 0:
                dst = cols_r(max(dl, 0))
            else:
                dst = corn_r(max(dl, 0), max(dn, 0))
            arrive(lat_ok(dn), dst, n)

    def ring(first, src, landing):
        for d in range(1, N_LON):
            send_to(top, src, landing.at[lon], first + d, first + lon, lon_at(d), lat)

    def ring_arrive(first, landing):
        for d in range(1, N_LON):
            arrive(top, landing.at[lon_at(d)], first + lon_at(d))

    rows_r = lambda b: rr.at[b]
    cols_r = lambda a: cc.at[a]
    corn_r = lambda a, b: kk.at[2 * a + b]
    halo(0, lambda b: rows.at[pl.ds(2 * b, 2)], rows_r, lambda a: cols.at[a], cols_r, lambda a, b: corn.at[2 * a + b], corn_r)
    fold_src = rows.at[pl.ds(2, 2), pl.ds(64, 80)]
    ring(8, fold_src, fr)
    own_fold = pltpu.make_async_copy(fold_src, fr.at[lon], lsem.at[0])

    @pl.when(top)
    def _():
        own_fold.start()

    @pl.loop(0, CHUNKS)
    def _(i):
        remap_chunk(i)

    for f in range(8):
        tb[:, f * 128 : (f + 1) * 128] = terms[pl.ds(f, 384, stride=8), :].astype(BF)
    for g in range(4):
        res = jnp.dot(oh[...], tb[:, g * 256 : (g + 1) * 256], preferred_element_type=F32)
        for o in range(9):
            for b in range(2):
                send[o, 2 * g + b] = res[o * 96 : (o + 1) * 96, b * 128 : (b + 1) * 128].astype(BF)


    for dl in (0, 2, 1):
        send_to(always, send.at[dl * 3 + 2 - 2 * side], pr.at[dl], 16 + dl, 16 + dl, lon, partner)
    straight = pl.ds(DETOUR, 8 - DETOUR)
    for n, dl in enumerate((0, 2)):
        block = dl * 3 + 2 * side
        send_to(has_outer, send.at[block, pl.ds(0, DETOUR)], rd.at[n], 48 + n, 48 + n, lon, outer)
        send_to(has_outer, send.at[block, straight], ro.at[dl, straight], 19 + dl, 19 + dl, lon_at(dl - 1), outer)
    send_to(has_outer, send.at[3 + 2 * side], ro.at[1], 20, 20, lon, outer)

    @pl.when(jnp.logical_not(has_outer))
    def _():
        ro[...] = jnp.zeros_like(ro)
        rd[...] = jnp.zeros_like(rd)

    for dl in (0, 2):
        ro[dl, 0:DETOUR] = jnp.zeros((DETOUR,) + ro.shape[2:], BF)

    for b, cond in ((0, has_south), (1, has_north)):

        @pl.when(jnp.logical_not(cond))
        def _(b=b):
            rr[b] = jnp.zeros(rr.shape[1:], BF)
            dr_r[b] = jnp.zeros(dr_r.shape[1:], BF)
            for a in range(2):
                kk[2 * a + b] = jnp.zeros(kk.shape[1:], BF)
                dk_r[2 * a + b] = jnp.zeros(dk_r.shape[1:], BF)
            for dl in range(3):
                sst_r[dl * 3 + 2 * b] = jnp.zeros(sst_r.shape[1:], BF)

    ma = mix_a[...]
    mo = mix_o[...]
    dot = functools.partial(jnp.dot, precision=HIGHEST, preferred_element_type=F32)
    ma2 = dot(ma, ma)
    mo2 = dot(mo, mo)
    ka[0], ka[1] = halves(spread(ma2, 16))
    ko[0, :, 0:128], ko[1, :, 0:128] = halves(spread(mo2, 8))
    ko[0, :, 128:256], ko[1, :, 128:256] = halves(spread(mo, 8))
    coef = jnp.broadcast_to(mo2[:, 0:1], (16, 128))
    coef_out[...] = coef

    @pl.when(top)
    def _():
        lane = lax.broadcasted_iota(jnp.int32, (1, 384), 1)
        column = lon * 256 + jnp.where(lane < 320, lane, lane - 384)
        pole = seam[0:1, 0:1] + lon * 256
        source = (pole - column) & 2047
        for j in range(8):
            fold[j * 256 : (j + 1) * 256, :] = jnp.where(
                lax.broadcasted_iota(jnp.int32, (256, 384), 0) + j * 256 == source, 1.0, 0.0
            ).astype(BF)

    halo_arrive(0, rows_r, cols_r, corn_r)
    for b in range(2):
        for e in range(2):
            rrf[b, e] = rr[b, e].astype(F32)
    for a in range(2):
        side_cols = cc[a].astype(F32)
        ks = kk[2 * a].astype(F32)
        kn = kk[2 * a + 1].astype(F32)
        cea[a, 0:8, :] = ks[8:16]
        cea[a, 8:72, :] = side_cols[0:64]
        cea[a, 72:80, :] = kn[0:8]
        ceo[a, 0:8, :] = ks[24:32]
        ceo[a, 8:56, :] = side_cols[64:112]
        ceo[a, 56:64, :] = kn[16:24]

    @pl.when(top)
    def _():
        own_fold.wait()
        ring_arrive(8, fr)
        total = jnp.zeros((160, 384), F32)
        for j in range(8):
            total += jnp.dot(fr[j].reshape(160, 256), fold[j * 256 : (j + 1) * 256, :], preferred_element_type=F32)
        n = lax.broadcasted_iota(jnp.int32, (80, 384), 0)
        sign = jnp.where(jnp.logical_and(n >= 32, n < 64), -1.0, 1.0)
        for e in range(2):
            ghost = total[80 * (1 - e) : 80 * (2 - e)] * sign
            if e == 0:
                beyond = ghost[0:64, 256:384]
            rrf[1, e, 64:144, :] = ghost[:, 0:256]
        lane = lax.broadcasted_iota(jnp.int32, (64, 128), 1)
        field = lax.broadcasted_iota(jnp.int32, (64, 128), 0)
        both = jnp.where(lane == 2 * field + 1, beyond[:, 127:128], jnp.where(lane == 2 * field, beyond[:, 0:1], 0.0))
        both = jnp.sum(both, axis=0, keepdims=True)
        ceo[0, 56:57, :] = both
        ceo[1, 56:57, :] = both

    lane_m = lax.broadcasted_iota(jnp.int32, (48, 128), 1)
    sea = mask[...].astype(F32)
    sea_left = cc[0, 112:160, :].astype(F32)
    sea_right = cc[1, 112:160, :].astype(F32)
    third = jnp.where(lane_m < 2, sea_right, jnp.where(lane_m >= 126, sea_left, 0.0))
    none = jnp.zeros((8, 128), F32)
    mext[...] = framed(
        sea,
        two_rows(6, rrf[0, 0, 128:129, :], rrf[0, 1, 128:129, :]),
        two_rows(0, rrf[1, 0, 128:129, :], rrf[1, 1, 128:129, :]),
        jnp.concatenate([none, third, none], axis=0),
    )
    lane_f = lax.broadcasted_iota(jnp.int32, (64, 128), 1)

    def outside(ce, own_at, rows, at, rate, sea_side, sea_rows):
        odd = (lax.broadcasted_iota(jnp.int32, (rows + 16, 128), 1) & 1) == 1
        own = [
            jnp.concatenate([none, cols[a, own_at : own_at + rows, :].astype(F32), none], axis=0)
            for a in range(2)
        ]
        centre, lateral = beside_packed(ce[0], ce[1], own[0], own[1], odd)
        y = step_from(centre, pltpu.roll(centre, 1, 0) + pltpu.roll(centre, rows + 15, 0) + lateral, rate)
        x_side, y_side = centre[8 : 8 + rows], y[8 : 8 + rows]
        pack = lambda x: pltpu.roll(x, 127, 1)
        sides = [pack(x_side), pack(y_side if sea_side is None else y_side * sea_side)]
        if sea_side is not None:
            sides.append(pack(x_side - x_side * sea_side))
        ends = []
        for b in range(2):
            near_row = rrf[b, 1 - b, at : at + 64, :]
            far_row = rrf[b, b, at : at + 64, :]
            own_row = rows_in[2 * b + b, at : at + 64, :].astype(F32)
            ghost = corner_lanes(centre, 7 if b == 0 else rows + 8)
            z = step_from(near_row, far_row + own_row + beside(near_row, ghost, lane_f), rate)
            if sea_side is None:
                ends.append([jnp.where(has_south if b == 0 else has_north, z, 0.0)])
            else:
                ends.append([z * sea_rows[b], near_row - near_row * sea_rows[b]])
        return sides, ends

    rows_in = rows
    odd_m = (lane_m & 1) == 1
    sea_side = jnp.where(odd_m, jnp.broadcast_to(sea_left[:, 127:128], (48, 128)), jnp.broadcast_to(sea_right[:, 0:1], (48, 128)))
    sides, ends = outside(ceo, 64, 48, 64, 0.2, sea_side, [rrf[0, 1, 128:129, :], rrf[1, 0, 128:129, :]])
    for n in range(3):
        gso[n] = sides[n]
    for b in range(2):
        for n in range(2):
            geo[b, n] = ends[b][n]
    sides, ends = outside(cea, 0, 64, 0, 0.15, None, None)
    for n in range(2):
        gsa[n] = sides[n]
    for b in range(2):
        gea[b] = ends[b][0]

    r256 = lax.broadcasted_iota(jnp.int32, (256, 256), 0)
    c256 = lax.broadcasted_iota(jnp.int32, (256, 256), 1)
    tri[...] = jnp.where(jnp.logical_or(r256 == c256 + 1, r256 + 1 == c256), 1.0, 0.0).astype(BF)

    for dl in (0, 2, 1):
        arrive(always, pr.at[dl], 16 + dl)
    for n, dl in enumerate((0, 2)):

        @pl.loop(DETOUR, 8)
        def _(f, n=n, dl=dl):
            sl[n, f] = (send[3 * dl + 1, f].astype(F32) + pr[dl, f].astype(F32)).astype(BF)

        send_to(always, sl.at[n, straight], rl.at[n, straight], 22 + n, 22 + n, lon_at(dl - 1), lat)
    for n, dl in enumerate((0, 2)):
        arrive(has_outer, rd.at[n], 48 + n)
        for f in range(DETOUR):
            total = send[3 * dl + 1, f].astype(F32) + pr[dl, f].astype(F32) + rd[n, f].astype(F32)
            sl[n, f] = total.astype(BF)
        bent = pl.ds(0, DETOUR)
        send_to(always, sl.at[n, bent], rl.at[n, bent], 50 + n, 50 + n, lon_at(dl - 1), lat)

    @pl.loop(0, 8)
    def _(i):
        v = i // 2
        first = pl.multiple_of(lax.rem(i, 2) * 8, 8)
        lines = pl.ds(pl.multiple_of(i * 8, 8), 8)
        far = pl.ds(pl.multiple_of(64 + i * 8, 8), 8)
        turned = lambda k, j: pltpu.roll(gso[k], (128 - 2 * (i * 8 + j)) & 127, 1)
        wet_here = mext[8:56, 0:256]
        south, north = rrf[0, 1, far, :], rrf[1, 0, far, :]
        xs = [oce[v, first + j] for j in range(8)]
        inner = lateral(xs, tri[...])
        a, c = [], []
        for j, x in enumerate(xs):
            around = near(x, inner[j], south[j : j + 1], north[j : j + 1], turned(0, j))
            a.append(wet_here * step_from(x, around, 0.2))
            c.append(x - wet_here * x)
        for k, parts in enumerate((a, c)):
            inner = lateral(parts, tri[...])
            south, north = geo[0, k, lines, :], geo[1, k, lines, :]
            for j, x in enumerate(parts):
                around = near(x, inner[j], south[j : j + 1], north[j : j + 1], turned(1 + k, j))
                bc[v, 16 * k + first + j] = step_from(x, around, 0.2)

    @pl.loop(0, 24, unroll=3)
    def _(n):
        v = n // 6
        at = pl.multiple_of(lax.rem(n, 6) * 8, 8)
        mixed = dot3(ko[0], ko[1], bc[v, :, pl.ds(at, 8), :].reshape(256, 256)).reshape(16, 8, 256)
        wet = mask[pl.ds(at, 8), :] > 0
        ss[v, :, pl.ds(at, 8), :] = jnp.where(wet[None], mixed, oce[v, :, pl.ds(at, 8), :])

    def atm_group(i):
        v = i // 2
        first = pl.multiple_of(lax.rem(i, 2) * 8, 8)
        lines = pl.ds(pl.multiple_of(i * 8, 8), 8)
        turned = lambda k, j: pltpu.roll(gsa[k], (128 - 2 * (i * 8 + j)) & 127, 1)
        parts = [atm[v, first + j] for j in range(8)]
        ends = ((rrf[0, 1, lines, :], rrf[1, 0, lines, :]), (gea[0, lines, :], gea[1, lines, :]))
        for k in range(2):
            inner = lateral(parts, tri[...])
            south, north = ends[k]
            parts = [
                step_from(x, near(x, inner[j], south[j : j + 1], north[j : j + 1], turned(k, j)), 0.15)
                for j, x in enumerate(parts)
            ]
        for j, y in enumerate(parts):
            stepped[v, first + j] = y

    def atm_mix(n):
        v = n // 4
        at = pl.multiple_of(lax.rem(n, 4) * 16, 16)
        mixed = dot3(ka[0], ka[1], stepped[v, :, pl.ds(at, 16), :].reshape(256, 256))
        stepped[v, :, pl.ds(at, 16), :] = mixed.reshape(16, 16, 256)

    @pl.loop(0, FIRST)
    def _(i):
        atm_group(i)

    @pl.loop(0, MIXED, unroll=4)
    def _(n):
        atm_mix(n)

    for dl in (0, 2):
        arrive(has_outer, ro.at[dl, straight], 19 + dl)
    arrive(has_outer, ro.at[1], 20)
    for n in range(2):
        arrive(always, rl.at[n, straight], 22 + n)
        arrive(always, rl.at[n, pl.ds(0, DETOUR)], 50 + n)

    @pl.loop(0, 8)
    def _(f):
        parts = [send[4, f], pr[1, f], rl[0, f], rl[1, f], ro[0, f], ro[1, f], ro[2, f]]
        total = functools.reduce(lambda x, y: x + y, [p.astype(F32) for p in parts])
        fs[pl.ds(pl.multiple_of(f * 96, 8), 96), :] = total

    flux = []
    for f in range(8):
        value = sea * jnp.concatenate([fs[pl.ds(f * 96 + h, 48, stride=2), :] for h in range(2)], axis=1)
        f_out[f] = value
        flux.append(value)
    forcing = [
        0.2 * sea * (flux[5] - flux[2] - flux[3] - flux[4]),
        0.2 * sea * (flux[3] - flux[6]),
        sea * (0.3 * flux[0] - 0.1 * flux[7] * oce[2, 0]),
        sea * (0.3 * flux[1] - 0.1 * flux[7] * oce[3, 0]),
    ]

    left = jnp.zeros((48, 128), F32)
    right = jnp.zeros((48, 128), F32)
    edge = [[jnp.zeros((16, 256), F32) for _ in range(2)] for _ in range(2)]
    row_16 = lax.broadcasted_iota(jnp.int32, (16, 256), 0)
    for f, d in enumerate(forcing):
        left = jnp.where((lane_m >> 1) == f, pltpu.roll(d[:, 0:128], 2 * f, 1) if f else d[:, 0:128], left)
        right = jnp.where((lane_m >> 1) == f, pltpu.roll(d[:, 128:256], 2 * f + 2, 1), right)
        for b in range(2):
            for e in range(2):
                r = 46 * b + e
                edge[b][e] = jnp.where(row_16 == f, d[r : r + 1, :], edge[b][e])
    dc_s[0] = left.astype(BF)
    dc_s[1] = right.astype(BF)
    for b in range(2):
        for e in range(2):
            dr_s[b, 16 * e : 16 * e + 16, :] = edge[b][e].astype(BF)
    rows_r = lambda b: dr_r.at[b]
    cols_r = lambda a: dc_r.at[a]
    corn_r = lambda a, b: dk_r.at[2 * a + b]
    halo(24, lambda b: dr_s.at[b], rows_r, lambda a: dc_s.at[a], cols_r,
         lambda a, b: dc_s.at[a, pl.ds(32 * b, 16)], corn_r)
    ring(32, dr_s.at[1], fd)

    @pl.when(top)
    def _():
        fd[lon] = dr_s[1]

    @pl.loop(FIRST, 8)
    def _(i):
        atm_group(i)

    halo_arrive(24, rows_r, cols_r, corn_r)
    for b in range(2):
        drf[b] = dr_r[b].astype(F32)
    for a in range(2):
        ced[a, 0:8, :] = dk_r[2 * a].astype(F32)[8:16]
        ced[a, 8:56, :] = dc_r[a].astype(F32)
        ced[a, 56:64, :] = dk_r[2 * a + 1].astype(F32)[0:8]

    @pl.when(top)
    def _():
        ring_arrive(32, fd)
        total = jnp.zeros((32, 384), F32)
        for j in range(8):
            total += jnp.dot(fd[j], fold[j * 256 : (j + 1) * 256, :], preferred_element_type=F32)
        n = lax.broadcasted_iota(jnp.int32, (16, 384), 0)
        sign = jnp.where(n >= 2, -1.0, 1.0)
        for e in range(2):
            gd[e] = total[16 * (1 - e) : 16 * (2 - e)] * sign
            drf[1, 16 * e : 16 * e + 16, :] = gd[e][:, 0:256]

    @pl.when(jnp.logical_not(top))
    def _():
        gd[...] = jnp.zeros_like(gd)

    m = mext[...]
    for f, d in enumerate(forcing):
        third = unpacked(ced[0], ced[1], f)
        north = jnp.where(top, two_rows(0, gd[0, f : f + 1, 256:384], gd[1, f : f + 1, 256:384]), third[56:64])
        x = framed(
            d,
            two_rows(6, drf[0, f : f + 1, :], drf[0, 16 + f : 17 + f, :]),
            two_rows(0, drf[1, f : f + 1, :], drf[1, 16 + f : 17 + f, :]),
            jnp.concatenate([third[0:56], north], axis=0),
        )
        q = sea * step(m * step(x, 0.2), 0.2)[8:56, 0:256]
        q_out[f] = q
        if f == 0:
            c00 = jnp.concatenate([coef[0:1, :], coef[0:1, :]], axis=1)
            heat = sea * (ss[0, 0] + c00 * q)
            for h in range(2):
                fs[pl.ds(h, 48, stride=2), :] = heat[:, 128 * h : 128 * h + 128]
            sst_s[...] = fs[0:96, :].astype(BF)
            for dl, dn in around:
                n = 40 + direction[(dl, dn)]
                back = 40 + direction[(-dl, -dn)]
                slot = (1 - dl) * 3 + 1 - dn
                send_to(lat_ok(dn), sst_s, sst_r.at[slot], n, back, lon_at(dl), lat + dn)
    @pl.loop(MIXED, 16, unroll=4)
    def _(n):
        atm_mix(n)

    sst_r[4] = sst_s[...]
    for dl, dn in around:
        arrive(lat_ok(dn), sst_r.at[(1 + dl) * 3 + 1 + dn], 40 + direction[(dl, dn)])
    sst_out[...] = sst_r[...]
    for finish in pending:
        finish()


def exchange(atm, oce, ts, sw, w, dd, dt, mask, seam, mix_a, mix_o):
    far = [pltpu.with_memory_space_constraint(x, pltpu.HBM) for x in (atm, oce, ts, sw, dd, dt, mask, w)]
    return pl.pallas_call(
        exchange_kernel,
        in_specs=[AWAY] * 8 + [HERE] * 3,
        out_specs=[HERE] * 7,
        out_shape=[
            pltpu.VMEM((128, 3, 128, 128), BF),
            pltpu.VMEM((4, 16, 64, 256), F32),
            pltpu.VMEM((4, 16, 48, 256), F32),
            pltpu.VMEM((4, 48, 256), F32),
            pltpu.VMEM((8, 48, 256), F32),
            pltpu.VMEM((9, 96, 128), BF),
            pltpu.VMEM((16, 128), F32),
        ],
        scratch_shapes=[
            pltpu.VMEM((4, 16, 64, 256), F32),
            pltpu.VMEM((4, 16, 48, 256), F32),
            pltpu.VMEM((4, 64, 256), F32),
            pltpu.VMEM((64, 256), F32),
            pltpu.VMEM((64, 256), F32),
            pltpu.VMEM((3, 128), jnp.int32),
            pltpu.VMEM((3, 128), jnp.int32),
            pltpu.VMEM((48, 256), jnp.int32),
            pltpu.VMEM((1024, 128), F32),
            pltpu.VMEM((3072, 128), F32),
            pltpu.VMEM((864, 384), BF),
            pltpu.VMEM((384, 1024), BF),
            pltpu.VMEM((4, 144, 256), F32),
            pltpu.VMEM((4, 144, 256), BF),
            pltpu.VMEM((2, 160, 128), BF),
            pltpu.VMEM((4, 32, 128), BF),
            pltpu.VMEM((9, 8, 96, 128), BF),
            pltpu.VMEM((4, 32, 48, 256), F32),
            pltpu.VMEM((3, 8, 96, 128), BF),
            pltpu.VMEM((3, 8, 96, 128), BF),
            pltpu.VMEM((2, DETOUR, 96, 128), BF),
            pltpu.VMEM((2, 8, 96, 128), BF),
            pltpu.VMEM((2, 8, 96, 128), BF),
            pltpu.VMEM((2, 2, 144, 256), BF),
            pltpu.VMEM((2, 160, 128), BF),
            pltpu.VMEM((4, 32, 128), BF),
            pltpu.VMEM((8, 2, 80, 256), BF),
            pltpu.VMEM((2, 2, 144, 256), F32),
            pltpu.VMEM((2, 80, 128), F32),
            pltpu.VMEM((2, 64, 128), F32),
            pltpu.VMEM((64, 384), F32),
            pltpu.VMEM((2048, 384), BF),
            pltpu.VMEM((2, 64, 128), F32),
            pltpu.VMEM((3, 48, 128), F32),
            pltpu.VMEM((2, 64, 256), F32),
            pltpu.VMEM((2, 2, 64, 256), F32),
            pltpu.VMEM((256, 256), BF),
            pltpu.VMEM((2, 256, 256), BF),
            pltpu.VMEM((2, 128, 256), BF),
            pltpu.VMEM((768, 128), F32),
            pltpu.VMEM((2, 32, 256), BF),
            pltpu.VMEM((2, 32, 256), BF),
            pltpu.VMEM((2, 48, 128), BF),
            pltpu.VMEM((2, 48, 128), BF),
            pltpu.VMEM((4, 16, 128), BF),
            pltpu.VMEM((8, 32, 256), BF),
            pltpu.VMEM((2, 32, 256), F32),
            pltpu.VMEM((2, 64, 128), F32),
            pltpu.VMEM((2, 16, 384), F32),
            pltpu.VMEM((96, 128), BF),
            pltpu.VMEM((9, 96, 128), BF),
            pltpu.SemaphoreType.DMA((8 + CHUNKS,)),
            pltpu.SemaphoreType.DMA((1,)),
            pltpu.SemaphoreType.DMA((52,)),
            pltpu.SemaphoreType.DMA((52,)),
        ],
        compiler_params=pltpu.CompilerParams(collective_id=0, has_side_effects=True, vmem_limit_bytes=36 * MIB),
        name="exchange",
    )(*far, seam, mix_a, mix_o)


def back_kernel(sst, dd, dt, q, coef, w, stepped, ss, flux, atm, ex, oce, f_out, sel, exs, exd, warm, sea, sem):
    plain = [
        pltpu.make_async_copy(flux, f_out, sem.at[0]),
        pltpu.make_async_copy(stepped.at[pl.ds(0, 2)], atm.at[pl.ds(0, 2)], sem.at[1]),
        pltpu.make_async_copy(stepped.at[2, pl.ds(0, 15)], atm.at[2, pl.ds(0, 15)], sem.at[2]),
        pltpu.make_async_copy(stepped.at[3], atm.at[3], sem.at[3]),
    ]
    for copy in plain:
        copy.start()
    heat = sst[...].reshape(864, 128)
    for k in range(3):
        picked = lax.dot_general(one_hot_slots(dd, dt, k), heat, TN, preferred_element_type=F32)
        sel[k * 128 : (k + 1) * 128, :] = picked.astype(BF)

    row = lax.broadcasted_iota(jnp.int32, (16, 128), 0)
    even = (row & 1) == 0
    ocean_out = lambda g: pltpu.make_async_copy(sea.at[pl.ds(g * 8, 8)], oce.at[pl.ds(g * 8, 8)], sem.at[6 + g])

    @pl.loop(0, 8, unroll=2)
    def _(g):
        v = g // 2
        for j in range(8):
            l = lax.rem(g, 2) * 8 + j
            c = coef[pl.ds(l, 1), :]
            sea[g * 8 + j] = ss[v, l] + jnp.concatenate([c, c], axis=1) * q[v]
        ocean_out(g).start()
        acc = jnp.zeros((16, 128), F32)
        t0 = pl.multiple_of(g * 16, 16)
        part = [sel[pl.ds(pl.multiple_of(k * 128 + t0, 16), 16), :] for k in range(3)]
        lhs = jnp.concatenate(part[:2], axis=1)
        last = part[2].astype(F32)
        split = jnp.concatenate([jnp.where(even, last, 0.0), jnp.where(even, 0.0, last)], axis=1).astype(BF)
        for j in range(0, 16, 4):
            quad = [[w[t0 + j + n, k] for k in range(3)] for n in range(4)]
            for h in range(2):
                p0, p1 = quad[2 * h], quad[2 * h + 1]
                block = jnp.concatenate([jnp.concatenate(p0[:2], axis=1), jnp.concatenate(p1[:2], axis=1)], axis=0)
                r = lax.dot_general(lhs, block, NT, preferred_element_type=F32)
                acc += jnp.where(row == j + 2 * h, r[:, :128], 0.0) + jnp.where(row == j + 2 * h + 1, r[:, 128:], 0.0)
            block = jnp.concatenate(
                [
                    jnp.concatenate([quad[0][2], quad[1][2]], axis=1),
                    jnp.concatenate([quad[2][2], quad[3][2]], axis=1),
                ],
                axis=0,
            )
            r = lax.dot_general(split, block, NT, preferred_element_type=F32)
            acc += jnp.where((row == j) | (row == j + 1), r[:, :128], 0.0)
            acc += jnp.where((row == j + 2) | (row == j + 3), r[:, 128:], 0.0)
        exs[pl.ds(t0, 16), :] = acc

    for h in range(2):
        at = slice(128 * h, 128 * h + 128)
        heat = exs[pl.ds(h, 64, stride=2), :]
        exd[:, at] = heat
        cold = stepped[2, 15, :, at]
        warm[:, at] = cold + 0.5 * (heat - cold)
    late = [
        pltpu.make_async_copy(exd, ex, sem.at[4]),
        pltpu.make_async_copy(warm, atm.at[2, 15], sem.at[5]),
    ]
    for copy in late:
        copy.start()
    for copy in plain + late:
        copy.wait()
    for g in range(8):
        ocean_out(g).wait()


def remap_back(sst, dd, dt, q, coef, w, stepped, ss, flux):
    return pl.pallas_call(
        back_kernel,
        in_specs=[HERE] * 9,
        out_specs=[AWAY] * 4,
        out_shape=[
            jax.ShapeDtypeStruct((4, 16, 64, 256), F32),
            jax.ShapeDtypeStruct((64, 256), F32),
            jax.ShapeDtypeStruct((64, 48, 256), F32),
            jax.ShapeDtypeStruct((8, 48, 256), F32),
        ],
        scratch_shapes=[
            pltpu.VMEM((384, 128), BF),
            pltpu.VMEM((128, 128), F32),
            pltpu.VMEM((64, 256), F32),
            pltpu.VMEM((64, 256), F32),
            pltpu.VMEM((64, 48, 256), F32),
            pltpu.SemaphoreType.DMA((14,)),
        ],
        compiler_params=pltpu.CompilerParams(vmem_limit_bytes=16 * MIB),
        name="remap_back",
    )(sst, dd, dt, q, coef, w, stepped, ss, flux)


def per_device(atmos, ts, sw, w, dd, dt, mix_a, ocean, mask, seam, mix_o):
    dd, dt = dd.T, dt.T
    w, stepped, ss, q, flux, sst, coef = exchange(
        atmos, ocean, ts, sw, w, dd, dt, mask, seam.reshape(1, 256), mix_a, mix_o
    )
    atm, ex, oce, flux = remap_back(sst, dd, dt, q, coef, w, stepped, ss, flux)
    return atm, ex, oce.reshape(ocean.shape), flux


def solution(mesh):
    field = P(None, None, "lat", "lon")
    plane = P("lat", "lon")
    tiles = P(("lon", "lat"), None)
    return jax.shard_map(
        per_device,
        mesh=mesh,
        in_specs=(field, plane, plane, P(("lon", "lat"), None, None, None), tiles, tiles, P(), field, plane, P("lon"), P()),
        out_specs=(field, plane, field, P(None, "lat", "lon")),
        check_vma=False,
    )
```

```python
import functools

import jax
import jax.numpy as jnp
from jax import lax
from jax.experimental import pallas as pl
from jax.experimental.pallas import tpu as pltpu
from jax.sharding import PartitionSpec as P

F32 = jnp.float32
BF = jnp.bfloat16
MESH = pl.DeviceIdType.MESH
HIGHEST = lax.Precision.HIGHEST
NT = (((1,), (1,)), ((), ()))
TN = (((0,), (0,)), ((), ()))
N_LON = 8
N_LAT = 16
CHUNKS = 8
FIRST = 4
MIXED = 4
DETOUR = 2
MIB = 2**20


def flux_fields(u, v, ta, qa, ts, sw):
    speed = jnp.sqrt(u * u + v * v + 1.0)
    soft = jnp.maximum(qa, 0.0) + jnp.log1p(jnp.exp(-jnp.abs(qa)))
    return [
        0.8 * speed * u,
        0.8 * speed * v,
        0.6 * speed * (ts - ta),
        0.5 * speed * (0.4 * jnp.exp(0.5 * ts) - qa),
        0.3 * (ta - ts) * (2.0 + jnp.tanh(ta)),
        sw * (0.9 - 0.1 * jnp.tanh(qa)),
        soft,
        0.3 * speed * speed,
    ]


def slot_rows(owner, tile):
    lon = lax.axis_index("lon")
    lat = lax.axis_index("lat")
    lon_offset = ((owner >> 4) - lon + 1) & 7
    lat_offset = (owner & 15) - lat + 1
    return (lon_offset * 3 + lat_offset) * 96 + tile


def one_hot_slots(dd, dt, k):
    slot = slot_rows(dd[k : k + 1, :], dt[k : k + 1, :])
    rows = lax.broadcasted_iota(jnp.int32, (864, 128), 0)
    return jnp.where(slot == rows, 1.0, 0.0).astype(BF)


HERE = pl.BlockSpec(memory_space=pltpu.VMEM)
AWAY = pl.BlockSpec(memory_space=pltpu.HBM)


def step(x, rate):
    rows, lanes = x.shape
    around = pltpu.roll(x, 1, 0) + pltpu.roll(x, rows - 1, 0) + pltpu.roll(x, 1, 1) + pltpu.roll(x, lanes - 1, 1)
    return (1.0 - 4.0 * rate) * x + rate * around


def step_from(x, around, rate):
    return (1.0 - 4.0 * rate) * x + rate * around


def unpacked(from_left, from_right, n):
    lane = lax.broadcasted_iota(jnp.int32, from_left.shape, 1)
    right = pltpu.roll(from_right, (128 - 2 * n) & 127, 1)
    left = pltpu.roll(from_left, 126 - 2 * n, 1)
    return jnp.where(lane < 2, right, jnp.where(lane >= 126, left, 0.0))


def two_rows(at, first, second):
    rows = lax.broadcasted_iota(jnp.int32, (8, first.shape[1]), 0)
    return jnp.where(rows == at, first, jnp.where(rows == at + 1, second, 0.0))


def framed(x, south, north, third):
    return jnp.concatenate([jnp.concatenate([south, x, north], axis=0), third], axis=1)


def lateral(parts, tri):
    rows = parts[0].shape[0]
    total = jnp.dot(jnp.concatenate(parts, axis=0).astype(BF), tri, preferred_element_type=F32)
    return [total[n * rows : (n + 1) * rows] for n in range(len(parts))]


def near(x, inner, above, below, ghost):
    rows = x.shape[0]
    lane = lax.broadcasted_iota(jnp.int32, (rows, 128), 1)
    row = lax.broadcasted_iota(jnp.int32, (8, 256), 0)
    up = pltpu.roll(x, 1, 0)
    down = pltpu.roll(x, rows - 1, 0)
    up = jnp.concatenate([jnp.where(row == 0, above, up[0:8]), up[8:]], axis=0)
    down = jnp.concatenate([down[: rows - 8], jnp.where(row == 7, below, down[rows - 8 :])], axis=0)
    edges = jnp.concatenate([jnp.where(lane == 0, ghost, 0.0), jnp.where(lane == 127, ghost, 0.0)], axis=1)
    return up + down + inner + edges


def beside(x, ghost, lane):
    t0, t1 = x[:, 0:128], x[:, 128:256]
    r0, r1 = pltpu.roll(t0, 1, 1), pltpu.roll(t1, 1, 1)
    l0, l1 = pltpu.roll(t0, 127, 1), pltpu.roll(t1, 127, 1)
    first, last = lane == 0, lane == 127
    s0 = jnp.where(first, ghost, r0) + jnp.where(last, l1, l0)
    s1 = jnp.where(first, r0, r1) + jnp.where(last, ghost, l1)
    return jnp.concatenate([s0, s1], axis=1)


def beside_packed(left, right, own_left, own_right, odd):
    centre = jnp.where(odd, left, right)
    outer = jnp.where(odd, pltpu.roll(left, 1, 1), pltpu.roll(right, 127, 1))
    inner = jnp.where(odd, pltpu.roll(own_left, 1, 1), pltpu.roll(own_right, 127, 1))
    return centre, outer + inner


def corner_lanes(centre, row):
    lane = lax.broadcasted_iota(jnp.int32, (64, 128), 1)
    field = lax.broadcasted_iota(jnp.int32, (64, 128), 0)
    line = jnp.broadcast_to(centre[row : row + 1, :], (64, 128))
    left = jnp.sum(jnp.where(lane == 2 * field + 1, line, 0.0), axis=1, keepdims=True)
    right = jnp.sum(jnp.where(lane == 2 * field, line, 0.0), axis=1, keepdims=True)
    return jnp.where(lane == 0, left, jnp.where(lane == 127, right, 0.0))


def spread(mixer, cells):
    size = 16 * cells
    pick = lambda dim: jnp.where(
        lax.broadcasted_iota(jnp.int32, (size, 16) if dim == 0 else (16, size), dim) // cells
        == lax.broadcasted_iota(jnp.int32, (size, 16) if dim == 0 else (16, size), 1 - dim),
        1.0,
        0.0,
    )
    dot = functools.partial(jnp.dot, precision=HIGHEST, preferred_element_type=F32)
    full = dot(dot(pick(0), mixer), pick(1))
    r = lax.broadcasted_iota(jnp.int32, (size, size), 0) % cells
    c = lax.broadcasted_iota(jnp.int32, (size, size), 1) % cells
    return jnp.where(r == c, full, 0.0)


def halves(x):
    high = x.astype(BF)
    return high, (x - high.astype(F32)).astype(BF)


def dot3(lhs_high, lhs_low, x):
    high, low = halves(x)
    dot = functools.partial(jnp.dot, preferred_element_type=F32)
    return dot(lhs_high, high) + dot(lhs_high, low) + dot(lhs_low, high)


def exchange_kernel(
    atm_far, oce_far, ts_far, sw_far, dd_far, dt_far, mask_far, w_far, seam, mix_a, mix_o,
    w_here, stepped, ss, q_out, f_out, sst_out, coef_out,
    atm, oce, surf, heat, sun, dd, dt, mask, ft, terms, oh, tb, rbuf, rows, cols, corn, send,
    bc, pr, ro, rd, rl, sl, rr, cc, kk, fr, rrf, cea, ceo, mext, fold, gsa, gso, gea, geo, tri,
    ka, ko, fs, dr_s, dr_r, dc_s, dc_r, dk_r, fd, drf, ced, gd, sst_s, sst_r,
    sem, lsem, ssem, rsem,
):
    lon = lax.axis_index("lon")
    lat = lax.axis_index("lat")
    side = lax.rem(lat, 2)
    partner = lat + 1 - 2 * side
    outer = lat - 1 + 2 * side
    has_outer = jnp.logical_and(outer >= 0, outer < N_LAT)
    has_south = lat > 0
    has_north = lat < N_LAT - 1
    top = lat == N_LAT - 1
    always = lat >= 0
    lon_at = lambda d: lax.rem(lon + d + N_LON, N_LON)

    def lat_ok(d):
        return always if d == 0 else (has_south if d < 0 else has_north)

    def send_to(cond, src, dst, n, m, dev_lon, dev_lat):
        copy = pltpu.make_async_remote_copy(
            src_ref=src, dst_ref=dst, send_sem=ssem.at[n], recv_sem=rsem.at[m],
            device_id=(dev_lon, dev_lat), device_id_type=MESH,
        )

        @pl.when(cond)
        def _():
            copy.start()

        def finish():
            @pl.when(cond)
            def _():
                copy.wait_send()

        pending.append(finish)

    def arrive(cond, dst, m):
        @pl.when(cond)
        def _():
            pltpu.make_async_remote_copy(
                src_ref=dst, dst_ref=dst, send_sem=ssem.at[0], recv_sem=rsem.at[m],
                device_id=(lon, partner), device_id_type=MESH,
            ).wait_recv()

    pending = []
    barrier = pltpu.get_barrier_semaphore()
    around = [(dl, dn) for dl in (-1, 0, 1) for dn in (-1, 0, 1) if (dl, dn) != (0, 0)]
    for dl, dn in around:

        @pl.when(lat_ok(dn))
        def _(dl=dl, dn=dn):
            pl.semaphore_signal(barrier, inc=1, device_id=(lon_at(dl), lat + dn), device_id_type=MESH)

    @pl.when(top)
    def _():
        for d in range(2, N_LON - 1):
            pl.semaphore_signal(barrier, inc=1, device_id=(lon_at(d), lat), device_id_type=MESH)

    chunk = 128 // CHUNKS
    copies = [
        pltpu.make_async_copy(atm_far.at[:, 15], surf, sem.at[0]),
        pltpu.make_async_copy(ts_far, heat, sem.at[1]),
        pltpu.make_async_copy(sw_far, sun, sem.at[2]),
        pltpu.make_async_copy(mask_far, mask, sem.at[5 + CHUNKS]),
    ]
    targets = [
        pltpu.make_async_copy(dd_far, dd, sem.at[6 + CHUNKS]),
        pltpu.make_async_copy(dt_far, dt, sem.at[7 + CHUNKS]),
    ]
    for copy in targets:
        copy.start()
    weights = lambda i: pltpu.make_async_copy(
        w_far.at[pl.ds(i * chunk, chunk)], w_here.at[pl.ds(i * chunk, chunk)], sem.at[3 + i]
    )
    fields = [
        pltpu.make_async_copy(atm_far, atm, sem.at[3 + CHUNKS]),
        pltpu.make_async_copy(oce_far, oce, sem.at[4 + CHUNKS]),
    ]
    for copy in copies:
        copy.start()
    for copy in fields:
        copy.start()
    for i in range(CHUNKS):
        weights(i).start()

    for copy in targets:
        copy.wait()
    for k in range(3):
        oh[:, k * 128 : (k + 1) * 128] = one_hot_slots(dd, dt, k)
    for copy in copies:
        copy.wait()
    for f, val in enumerate(flux_fields(surf[0], surf[1], surf[2], surf[3], heat[...], sun[...])):
        val = val.astype(BF).astype(F32)
        ft[pl.ds(f, 64, stride=16), :] = val[:, :128]
        ft[pl.ds(8 + f, 64, stride=16), :] = val[:, 128:]

    group = lax.broadcasted_iota(jnp.int32, (32, 128), 0)
    even = (group & 8) == 0

    def remap_chunk(i):
        weights(i).wait()
        for j in range(0, chunk, 4):
            t = i * chunk + j
            a = ft[pl.ds(pl.multiple_of(t * 8, 32), 32), :]
            lhs = jnp.concatenate([jnp.where(even, a, 0.0), jnp.where(even, 0.0, a)], axis=1).astype(BF)
            quad = [[w_here[t + q, k] for k in range(3)] for q in range(4)]
            for h in range(2):
                p, q = quad[2 * h], quad[2 * h + 1]
                block = jnp.concatenate([jnp.concatenate(p[:2], axis=1), jnp.concatenate(q[:2], axis=1)], axis=0)
                r = jnp.dot(lhs[16 * h : 16 * h + 16], block, preferred_element_type=F32)
                for k in range(2):
                    terms[pl.ds(pl.multiple_of((k * 128 + t + 2 * h) * 8, 16), 16), :] = r[:, k * 128 : (k + 1) * 128]
            block = jnp.concatenate(
                [
                    jnp.concatenate([quad[0][2], quad[2][2]], axis=1),
                    jnp.concatenate([quad[1][2], quad[3][2]], axis=1),
                ],
                axis=0,
            )
            r = jnp.dot(lhs, block, preferred_element_type=F32)
            at = pl.multiple_of((256 + t) * 8, 32)
            terms[pl.ds(at, 16), :] = r[:16, :128]
            terms[pl.ds(at + 16, 16), :] = r[16:, 128:]

    for copy in fields:
        copy.wait()
    lane_a = lax.broadcasted_iota(jnp.int32, (64, 128), 1) >> 1
    lane_o = lax.broadcasted_iota(jnp.int32, (48, 128), 1) >> 1
    za = jnp.zeros((64, 128), F32)
    zo = jnp.zeros((48, 128), F32)

    @pl.loop(0, 16, init_carry=(za, za, zo, zo))
    def packed(l, carry):
        left_a, right_a, left_o, right_o = carry
        for v in range(4):
            n = v * 16 + l
            ahead = 2 * n
            back = (2 * n + 2) & 127
            left_a = jnp.where(lane_a == n, pltpu.roll(atm[v, l, :, 0:128], ahead, 1), left_a)
            right_a = jnp.where(lane_a == n, pltpu.roll(atm[v, l, :, 128:256], back, 1), right_a)
            left_o = jnp.where(lane_o == n, pltpu.roll(oce[v, l, :, 0:128], ahead, 1), left_o)
            right_o = jnp.where(lane_o == n, pltpu.roll(oce[v, l, :, 128:256], back, 1), right_o)
            for e in range(2):
                rbuf[e, pl.ds(n, 1), :] = atm[v, l, e : e + 1, :]
                rbuf[2 + e, pl.ds(n, 1), :] = atm[v, l, 62 + e : 63 + e, :]
                rbuf[e, pl.ds(64 + n, 1), :] = oce[v, l, e : e + 1, :]
                rbuf[2 + e, pl.ds(64 + n, 1), :] = oce[v, l, 46 + e : 47 + e, :]
        return left_a, right_a, left_o, right_o

    sea = mask[...].astype(F32)
    for a in range(2):
        cols_a, cols_o = packed[a], packed[2 + a]
        cols[a, 0:64, :] = cols_a.astype(BF)
        cols[a, 64:112, :] = cols_o.astype(BF)
        cols[a, 112:160, :] = sea[:, 128 * a : 128 * a + 128].astype(BF)
        corn[2 * a, 0:16, :] = cols_a[0:16].astype(BF)
        corn[2 * a, 16:32, :] = cols_o[0:16].astype(BF)
        corn[2 * a + 1, 0:16, :] = cols_a[48:64].astype(BF)
        corn[2 * a + 1, 16:32, :] = cols_o[32:48].astype(BF)
    for e in range(2):
        for b in range(2):
            r = 46 * b + e
            rbuf[2 * b + e, 128:144, :] = jnp.broadcast_to(sea[r : r + 1, :], (16, 256))
    rows[...] = rbuf[...].astype(BF)

    @pl.when(top)
    def _():
        pl.semaphore_wait(barrier, 5 + 5)

    @pl.when(lat == 0)
    def _():
        pl.semaphore_wait(barrier, 5)

    @pl.when(jnp.logical_and(has_south, has_north))
    def _():
        pl.semaphore_wait(barrier, 8)

    direction = {pair: n for n, pair in enumerate(around)}

    def halo(first, rows_s, rows_r, cols_s, cols_r, corn_s, corn_r):
        for dl, dn in around:
            n = first + direction[(dl, dn)]
            back = first + direction[(-dl, -dn)]
            if dl == 0:
                src, dst = rows_s(max(dn, 0)), rows_r(max(-dn, 0))
            elif dn == 0:
                src, dst = cols_s(max(dl, 0)), cols_r(max(-dl, 0))
            else:
                src, dst = corn_s(max(dl, 0), max(dn, 0)), corn_r(max(-dl, 0), max(-dn, 0))
            send_to(lat_ok(dn), src, dst, n, back, lon_at(dl), lat + dn)

    def halo_arrive(first, rows_r, cols_r, corn_r):
        for dl, dn in around:
            n = first + direction[(dl, dn)]
            if dl == 0:
                dst = rows_r(max(dn, 0))
            elif dn == 0:
                dst = cols_r(max(dl, 0))
            else:
                dst = corn_r(max(dl, 0), max(dn, 0))
            arrive(lat_ok(dn), dst, n)

    def ring(first, src, landing):
        for d in range(1, N_LON):
            send_to(top, src, landing.at[lon], first + d, first + lon, lon_at(d), lat)

    def ring_arrive(first, landing):
        for d in range(1, N_LON):
            arrive(top, landing.at[lon_at(d)], first + lon_at(d))

    rows_r = lambda b: rr.at[b]
    cols_r = lambda a: cc.at[a]
    corn_r = lambda a, b: kk.at[2 * a + b]
    halo(0, lambda b: rows.at[pl.ds(2 * b, 2)], rows_r, lambda a: cols.at[a], cols_r, lambda a, b: corn.at[2 * a + b], corn_r)
    fold_src = rows.at[pl.ds(2, 2), pl.ds(64, 80)]
    ring(8, fold_src, fr)
    own_fold = pltpu.make_async_copy(fold_src, fr.at[lon], lsem.at[0])

    @pl.when(top)
    def _():
        own_fold.start()

    @pl.loop(0, CHUNKS)
    def _(i):
        remap_chunk(i)

    for f in range(8):
        tb[:, f * 128 : (f + 1) * 128] = terms[pl.ds(f, 384, stride=8), :].astype(BF)
    for g in range(4):
        res = jnp.dot(oh[...], tb[:, g * 256 : (g + 1) * 256], preferred_element_type=F32)
        for o in range(9):
            for b in range(2):
                send[o, 2 * g + b] = res[o * 96 : (o + 1) * 96, b * 128 : (b + 1) * 128].astype(BF)


    for dl in (0, 2, 1):
        send_to(always, send.at[dl * 3 + 2 - 2 * side], pr.at[dl], 16 + dl, 16 + dl, lon, partner)
    straight = pl.ds(DETOUR, 8 - DETOUR)
    for n, dl in enumerate((0, 2)):
        block = dl * 3 + 2 * side
        send_to(has_outer, send.at[block, pl.ds(0, DETOUR)], rd.at[n], 48 + n, 48 + n, lon, outer)
        send_to(has_outer, send.at[block, straight], ro.at[dl, straight], 19 + dl, 19 + dl, lon_at(dl - 1), outer)
    send_to(has_outer, send.at[3 + 2 * side], ro.at[1], 20, 20, lon, outer)

    @pl.when(jnp.logical_not(has_outer))
    def _():
        ro[...] = jnp.zeros_like(ro)
        rd[...] = jnp.zeros_like(rd)

    for dl in (0, 2):
        ro[dl, 0:DETOUR] = jnp.zeros((DETOUR,) + ro.shape[2:], BF)

    for b, cond in ((0, has_south), (1, has_north)):

        @pl.when(jnp.logical_not(cond))
        def _(b=b):
            rr[b] = jnp.zeros(rr.shape[1:], BF)
            dr_r[b] = jnp.zeros(dr_r.shape[1:], BF)
            for a in range(2):
                kk[2 * a + b] = jnp.zeros(kk.shape[1:], BF)
                dk_r[2 * a + b] = jnp.zeros(dk_r.shape[1:], BF)
            for dl in range(3):
                sst_r[dl * 3 + 2 * b] = jnp.zeros(sst_r.shape[1:], BF)

    ma = mix_a[...]
    mo = mix_o[...]
    dot = functools.partial(jnp.dot, precision=HIGHEST, preferred_element_type=F32)
    ma2 = dot(ma, ma)
    mo2 = dot(mo, mo)
    ka[0], ka[1] = halves(spread(ma2, 16))
    ko[0, :, 0:128], ko[1, :, 0:128] = halves(spread(mo2, 8))
    ko[0, :, 128:256], ko[1, :, 128:256] = halves(spread(mo, 8))
    coef = jnp.broadcast_to(mo2[:, 0:1], (16, 128))
    coef_out[...] = coef

    @pl.when(top)
    def _():
        lane = lax.broadcasted_iota(jnp.int32, (1, 384), 1)
        column = lon * 256 + jnp.where(lane < 320, lane, lane - 384)
        pole = seam[0:1, 0:1] + lon * 256
        source = (pole - column) & 2047
        for j in range(8):
            fold[j * 256 : (j + 1) * 256, :] = jnp.where(
                lax.broadcasted_iota(jnp.int32, (256, 384), 0) + j * 256 == source, 1.0, 0.0
            ).astype(BF)

    halo_arrive(0, rows_r, cols_r, corn_r)
    for b in range(2):
        for e in range(2):
            rrf[b, e] = rr[b, e].astype(F32)
    for a in range(2):
        side_cols = cc[a].astype(F32)
        ks = kk[2 * a].astype(F32)
        kn = kk[2 * a + 1].astype(F32)
        cea[a, 0:8, :] = ks[8:16]
        cea[a, 8:72, :] = side_cols[0:64]
        cea[a, 72:80, :] = kn[0:8]
        ceo[a, 0:8, :] = ks[24:32]
        ceo[a, 8:56, :] = side_cols[64:112]
        ceo[a, 56:64, :] = kn[16:24]

    @pl.when(top)
    def _():
        own_fold.wait()
        ring_arrive(8, fr)
        total = jnp.zeros((160, 384), F32)
        for j in range(8):
            total += jnp.dot(fr[j].reshape(160, 256), fold[j * 256 : (j + 1) * 256, :], preferred_element_type=F32)
        n = lax.broadcasted_iota(jnp.int32, (80, 384), 0)
        sign = jnp.where(jnp.logical_and(n >= 32, n < 64), -1.0, 1.0)
        for e in range(2):
            ghost = total[80 * (1 - e) : 80 * (2 - e)] * sign
            if e == 0:
                beyond = ghost[0:64, 256:384]
            rrf[1, e, 64:144, :] = ghost[:, 0:256]
        lane = lax.broadcasted_iota(jnp.int32, (64, 128), 1)
        field = lax.broadcasted_iota(jnp.int32, (64, 128), 0)
        both = jnp.where(lane == 2 * field + 1, beyond[:, 127:128], jnp.where(lane == 2 * field, beyond[:, 0:1], 0.0))
        both = jnp.sum(both, axis=0, keepdims=True)
        ceo[0, 56:57, :] = both
        ceo[1, 56:57, :] = both

    lane_m = lax.broadcasted_iota(jnp.int32, (48, 128), 1)
    sea = mask[...].astype(F32)
    sea_left = cc[0, 112:160, :].astype(F32)
    sea_right = cc[1, 112:160, :].astype(F32)
    third = jnp.where(lane_m < 2, sea_right, jnp.where(lane_m >= 126, sea_left, 0.0))
    none = jnp.zeros((8, 128), F32)
    mext[...] = framed(
        sea,
        two_rows(6, rrf[0, 0, 128:129, :], rrf[0, 1, 128:129, :]),
        two_rows(0, rrf[1, 0, 128:129, :], rrf[1, 1, 128:129, :]),
        jnp.concatenate([none, third, none], axis=0),
    )
    lane_f = lax.broadcasted_iota(jnp.int32, (64, 128), 1)

    def outside(ce, own_at, rows, at, rate, sea_side, sea_rows):
        odd = (lax.broadcasted_iota(jnp.int32, (rows + 16, 128), 1) & 1) == 1
        own = [
            jnp.concatenate([none, cols[a, own_at : own_at + rows, :].astype(F32), none], axis=0)
            for a in range(2)
        ]
        centre, lateral = beside_packed(ce[0], ce[1], own[0], own[1], odd)
        y = step_from(centre, pltpu.roll(centre, 1, 0) + pltpu.roll(centre, rows + 15, 0) + lateral, rate)
        x_side, y_side = centre[8 : 8 + rows], y[8 : 8 + rows]
        pack = lambda x: pltpu.roll(x, 127, 1)
        sides = [pack(x_side), pack(y_side if sea_side is None else y_side * sea_side)]
        if sea_side is not None:
            sides.append(pack(x_side - x_side * sea_side))
        ends = []
        for b in range(2):
            near_row = rrf[b, 1 - b, at : at + 64, :]
            far_row = rrf[b, b, at : at + 64, :]
            own_row = rows_in[2 * b + b, at : at + 64, :].astype(F32)
            ghost = corner_lanes(centre, 7 if b == 0 else rows + 8)
            z = step_from(near_row, far_row + own_row + beside(near_row, ghost, lane_f), rate)
            if sea_side is None:
                ends.append([jnp.where(has_south if b == 0 else has_north, z, 0.0)])
            else:
                ends.append([z * sea_rows[b], near_row - near_row * sea_rows[b]])
        return sides, ends

    rows_in = rows
    odd_m = (lane_m & 1) == 1
    sea_side = jnp.where(odd_m, jnp.broadcast_to(sea_left[:, 127:128], (48, 128)), jnp.broadcast_to(sea_right[:, 0:1], (48, 128)))
    sides, ends = outside(ceo, 64, 48, 64, 0.2, sea_side, [rrf[0, 1, 128:129, :], rrf[1, 0, 128:129, :]])
    for n in range(3):
        gso[n] = sides[n]
    for b in range(2):
        for n in range(2):
            geo[b, n] = ends[b][n]
    sides, ends = outside(cea, 0, 64, 0, 0.15, None, None)
    for n in range(2):
        gsa[n] = sides[n]
    for b in range(2):
        gea[b] = ends[b][0]

    r256 = lax.broadcasted_iota(jnp.int32, (256, 256), 0)
    c256 = lax.broadcasted_iota(jnp.int32, (256, 256), 1)
    tri[...] = jnp.where(jnp.logical_or(r256 == c256 + 1, r256 + 1 == c256), 1.0, 0.0).astype(BF)

    for dl in (0, 2, 1):
        arrive(always, pr.at[dl], 16 + dl)
    for n, dl in enumerate((0, 2)):

        @pl.loop(DETOUR, 8, unroll=3)
        def _(f, n=n, dl=dl):
            sl[n, f] = (send[3 * dl + 1, f].astype(F32) + pr[dl, f].astype(F32)).astype(BF)

        send_to(always, sl.at[n, straight], rl.at[n, straight], 22 + n, 22 + n, lon_at(dl - 1), lat)
    for n, dl in enumerate((0, 2)):
        arrive(has_outer, rd.at[n], 48 + n)
        for f in range(DETOUR):
            total = send[3 * dl + 1, f].astype(F32) + pr[dl, f].astype(F32) + rd[n, f].astype(F32)
            sl[n, f] = total.astype(BF)
        bent = pl.ds(0, DETOUR)
        send_to(always, sl.at[n, bent], rl.at[n, bent], 50 + n, 50 + n, lon_at(dl - 1), lat)

    @pl.loop(0, 8)
    def _(i):
        v = i // 2
        first = pl.multiple_of(lax.rem(i, 2) * 8, 8)
        lines = pl.ds(pl.multiple_of(i * 8, 8), 8)
        far = pl.ds(pl.multiple_of(64 + i * 8, 8), 8)
        turned = lambda k, j: pltpu.roll(gso[k], (128 - 2 * (i * 8 + j)) & 127, 1)
        wet_here = mext[8:56, 0:256]
        south, north = rrf[0, 1, far, :], rrf[1, 0, far, :]
        xs = [oce[v, first + j] for j in range(8)]
        inner = lateral(xs, tri[...])
        a, c = [], []
        for j, x in enumerate(xs):
            around = near(x, inner[j], south[j : j + 1], north[j : j + 1], turned(0, j))
            a.append(wet_here * step_from(x, around, 0.2))
            c.append(x - wet_here * x)
        for k, parts in enumerate((a, c)):
            inner = lateral(parts, tri[...])
            south, north = geo[0, k, lines, :], geo[1, k, lines, :]
            for j, x in enumerate(parts):
                around = near(x, inner[j], south[j : j + 1], north[j : j + 1], turned(1 + k, j))
                bc[v, 16 * k + first + j] = step_from(x, around, 0.2)

    @pl.loop(0, 24, unroll=6)
    def _(n):
        v = n // 6
        at = pl.multiple_of(lax.rem(n, 6) * 8, 8)
        mixed = dot3(ko[0], ko[1], bc[v, :, pl.ds(at, 8), :].reshape(256, 256)).reshape(16, 8, 256)
        wet = mask[pl.ds(at, 8), :] > 0
        ss[v, :, pl.ds(at, 8), :] = jnp.where(wet[None], mixed, oce[v, :, pl.ds(at, 8), :])

    def atm_group(i):
        v = i // 2
        first = pl.multiple_of(lax.rem(i, 2) * 8, 8)
        lines = pl.ds(pl.multiple_of(i * 8, 8), 8)
        turned = lambda k, j: pltpu.roll(gsa[k], (128 - 2 * (i * 8 + j)) & 127, 1)
        parts = [atm[v, first + j] for j in range(8)]
        ends = ((rrf[0, 1, lines, :], rrf[1, 0, lines, :]), (gea[0, lines, :], gea[1, lines, :]))
        for k in range(2):
            inner = lateral(parts, tri[...])
            south, north = ends[k]
            parts = [
                step_from(x, near(x, inner[j], south[j : j + 1], north[j : j + 1], turned(k, j)), 0.15)
                for j, x in enumerate(parts)
            ]
        for j, y in enumerate(parts):
            stepped[v, first + j] = y

    def atm_mix(n):
        v = n // 4
        at = pl.multiple_of(lax.rem(n, 4) * 16, 16)
        mixed = dot3(ka[0], ka[1], stepped[v, :, pl.ds(at, 16), :].reshape(256, 256))
        stepped[v, :, pl.ds(at, 16), :] = mixed.reshape(16, 16, 256)

    @pl.loop(0, FIRST)
    def _(i):
        atm_group(i)

    @pl.loop(0, MIXED, unroll=4)
    def _(n):
        atm_mix(n)

    for dl in (0, 2):
        arrive(has_outer, ro.at[dl, straight], 19 + dl)
    arrive(has_outer, ro.at[1], 20)
    for n in range(2):
        arrive(always, rl.at[n, straight], 22 + n)
        arrive(always, rl.at[n, pl.ds(0, DETOUR)], 50 + n)

    @pl.loop(0, 8, unroll=4)
    def _(f):
        parts = [send[4, f], pr[1, f], rl[0, f], rl[1, f], ro[0, f], ro[1, f], ro[2, f]]
        total = functools.reduce(lambda x, y: x + y, [p.astype(F32) for p in parts])
        fs[pl.ds(pl.multiple_of(f * 96, 8), 96), :] = total

    flux = []
    for f in range(8):
        value = sea * jnp.concatenate([fs[pl.ds(f * 96 + h, 48, stride=2), :] for h in range(2)], axis=1)
        f_out[f] = value
        flux.append(value)
    forcing = [
        0.2 * sea * (flux[5] - flux[2] - flux[3] - flux[4]),
        0.2 * sea * (flux[3] - flux[6]),
        sea * (0.3 * flux[0] - 0.1 * flux[7] * oce[2, 0]),
        sea * (0.3 * flux[1] - 0.1 * flux[7] * oce[3, 0]),
    ]

    left = jnp.zeros((48, 128), F32)
    right = jnp.zeros((48, 128), F32)
    edge = [[jnp.zeros((16, 256), F32) for _ in range(2)] for _ in range(2)]
    row_16 = lax.broadcasted_iota(jnp.int32, (16, 256), 0)
    for f, d in enumerate(forcing):
        left = jnp.where((lane_m >> 1) == f, pltpu.roll(d[:, 0:128], 2 * f, 1) if f else d[:, 0:128], left)
        right = jnp.where((lane_m >> 1) == f, pltpu.roll(d[:, 128:256], 2 * f + 2, 1), right)
        for b in range(2):
            for e in range(2):
                r = 46 * b + e
                edge[b][e] = jnp.where(row_16 == f, d[r : r + 1, :], edge[b][e])
    dc_s[0] = left.astype(BF)
    dc_s[1] = right.astype(BF)
    for b in range(2):
        for e in range(2):
            dr_s[b, 16 * e : 16 * e + 16, :] = edge[b][e].astype(BF)
    rows_r = lambda b: dr_r.at[b]
    cols_r = lambda a: dc_r.at[a]
    corn_r = lambda a, b: dk_r.at[2 * a + b]
    halo(24, lambda b: dr_s.at[b], rows_r, lambda a: dc_s.at[a], cols_r,
         lambda a, b: dc_s.at[a, pl.ds(32 * b, 16)], corn_r)
    ring(32, dr_s.at[1], fd)

    @pl.when(top)
    def _():
        fd[lon] = dr_s[1]

    @pl.loop(FIRST, 8)
    def _(i):
        atm_group(i)

    halo_arrive(24, rows_r, cols_r, corn_r)
    for b in range(2):
        drf[b] = dr_r[b].astype(F32)
    for a in range(2):
        ced[a, 0:8, :] = dk_r[2 * a].astype(F32)[8:16]
        ced[a, 8:56, :] = dc_r[a].astype(F32)
        ced[a, 56:64, :] = dk_r[2 * a + 1].astype(F32)[0:8]

    @pl.when(top)
    def _():
        ring_arrive(32, fd)
        total = jnp.zeros((32, 384), F32)
        for j in range(8):
            total += jnp.dot(fd[j], fold[j * 256 : (j + 1) * 256, :], preferred_element_type=F32)
        n = lax.broadcasted_iota(jnp.int32, (16, 384), 0)
        sign = jnp.where(n >= 2, -1.0, 1.0)
        for e in range(2):
            gd[e] = total[16 * (1 - e) : 16 * (2 - e)] * sign
            drf[1, 16 * e : 16 * e + 16, :] = gd[e][:, 0:256]

    @pl.when(jnp.logical_not(top))
    def _():
        gd[...] = jnp.zeros_like(gd)

    m = mext[...]
    for f, d in enumerate(forcing):
        third = unpacked(ced[0], ced[1], f)
        north = jnp.where(top, two_rows(0, gd[0, f : f + 1, 256:384], gd[1, f : f + 1, 256:384]), third[56:64])
        x = framed(
            d,
            two_rows(6, drf[0, f : f + 1, :], drf[0, 16 + f : 17 + f, :]),
            two_rows(0, drf[1, f : f + 1, :], drf[1, 16 + f : 17 + f, :]),
            jnp.concatenate([third[0:56], north], axis=0),
        )
        q = sea * step(m * step(x, 0.2), 0.2)[8:56, 0:256]
        q_out[f] = q
        if f == 0:
            c00 = jnp.concatenate([coef[0:1, :], coef[0:1, :]], axis=1)
            heat = sea * (ss[0, 0] + c00 * q)
            for h in range(2):
                fs[pl.ds(h, 48, stride=2), :] = heat[:, 128 * h : 128 * h + 128]
            sst_s[...] = fs[0:96, :].astype(BF)
            for dl, dn in around:
                n = 40 + direction[(dl, dn)]
                back = 40 + direction[(-dl, -dn)]
                slot = (1 - dl) * 3 + 1 - dn
                send_to(lat_ok(dn), sst_s, sst_r.at[slot], n, back, lon_at(dl), lat + dn)
    @pl.loop(MIXED, 16, unroll=4)
    def _(n):
        atm_mix(n)

    sst_r[4] = sst_s[...]
    for dl, dn in around:
        arrive(lat_ok(dn), sst_r.at[(1 + dl) * 3 + 1 + dn], 40 + direction[(dl, dn)])
    sst_out[...] = sst_r[...]
    for finish in pending:
        finish()


def exchange(atm, oce, ts, sw, w, dd, dt, mask, seam, mix_a, mix_o):
    far = [pltpu.with_memory_space_constraint(x, pltpu.HBM) for x in (atm, oce, ts, sw, dd, dt, mask, w)]
    return pl.pallas_call(
        exchange_kernel,
        in_specs=[AWAY] * 8 + [HERE] * 3,
        out_specs=[HERE] * 7,
        out_shape=[
            pltpu.VMEM((128, 3, 128, 128), BF),
            pltpu.VMEM((4, 16, 64, 256), F32),
            pltpu.VMEM((4, 16, 48, 256), F32),
            pltpu.VMEM((4, 48, 256), F32),
            pltpu.VMEM((8, 48, 256), F32),
            pltpu.VMEM((9, 96, 128), BF),
            pltpu.VMEM((16, 128), F32),
        ],
        scratch_shapes=[
            pltpu.VMEM((4, 16, 64, 256), F32),
            pltpu.VMEM((4, 16, 48, 256), F32),
            pltpu.VMEM((4, 64, 256), F32),
            pltpu.VMEM((64, 256), F32),
            pltpu.VMEM((64, 256), F32),
            pltpu.VMEM((3, 128), jnp.int32),
            pltpu.VMEM((3, 128), jnp.int32),
            pltpu.VMEM((48, 256), jnp.int32),
            pltpu.VMEM((1024, 128), F32),
            pltpu.VMEM((3072, 128), F32),
            pltpu.VMEM((864, 384), BF),
            pltpu.VMEM((384, 1024), BF),
            pltpu.VMEM((4, 144, 256), F32),
            pltpu.VMEM((4, 144, 256), BF),
            pltpu.VMEM((2, 160, 128), BF),
            pltpu.VMEM((4, 32, 128), BF),
            pltpu.VMEM((9, 8, 96, 128), BF),
            pltpu.VMEM((4, 32, 48, 256), F32),
            pltpu.VMEM((3, 8, 96, 128), BF),
            pltpu.VMEM((3, 8, 96, 128), BF),
            pltpu.VMEM((2, DETOUR, 96, 128), BF),
            pltpu.VMEM((2, 8, 96, 128), BF),
            pltpu.VMEM((2, 8, 96, 128), BF),
            pltpu.VMEM((2, 2, 144, 256), BF),
            pltpu.VMEM((2, 160, 128), BF),
            pltpu.VMEM((4, 32, 128), BF),
            pltpu.VMEM((8, 2, 80, 256), BF),
            pltpu.VMEM((2, 2, 144, 256), F32),
            pltpu.VMEM((2, 80, 128), F32),
            pltpu.VMEM((2, 64, 128), F32),
            pltpu.VMEM((64, 384), F32),
            pltpu.VMEM((2048, 384), BF),
            pltpu.VMEM((2, 64, 128), F32),
            pltpu.VMEM((3, 48, 128), F32),
            pltpu.VMEM((2, 64, 256), F32),
            pltpu.VMEM((2, 2, 64, 256), F32),
            pltpu.VMEM((256, 256), BF),
            pltpu.VMEM((2, 256, 256), BF),
            pltpu.VMEM((2, 128, 256), BF),
            pltpu.VMEM((768, 128), F32),
            pltpu.VMEM((2, 32, 256), BF),
            pltpu.VMEM((2, 32, 256), BF),
            pltpu.VMEM((2, 48, 128), BF),
            pltpu.VMEM((2, 48, 128), BF),
            pltpu.VMEM((4, 16, 128), BF),
            pltpu.VMEM((8, 32, 256), BF),
            pltpu.VMEM((2, 32, 256), F32),
            pltpu.VMEM((2, 64, 128), F32),
            pltpu.VMEM((2, 16, 384), F32),
            pltpu.VMEM((96, 128), BF),
            pltpu.VMEM((9, 96, 128), BF),
            pltpu.SemaphoreType.DMA((8 + CHUNKS,)),
            pltpu.SemaphoreType.DMA((1,)),
            pltpu.SemaphoreType.DMA((52,)),
            pltpu.SemaphoreType.DMA((52,)),
        ],
        compiler_params=pltpu.CompilerParams(collective_id=0, has_side_effects=True, vmem_limit_bytes=36 * MIB),
        name="exchange",
    )(*far, seam, mix_a, mix_o)


def back_kernel(sst, dd, dt, q, coef, w, stepped, ss, flux, atm, ex, oce, f_out, sel, exs, exd, warm, sea, sem):
    plain = [
        pltpu.make_async_copy(flux, f_out, sem.at[0]),
        pltpu.make_async_copy(stepped.at[pl.ds(0, 2)], atm.at[pl.ds(0, 2)], sem.at[1]),
        pltpu.make_async_copy(stepped.at[2, pl.ds(0, 15)], atm.at[2, pl.ds(0, 15)], sem.at[2]),
        pltpu.make_async_copy(stepped.at[3], atm.at[3], sem.at[3]),
    ]
    for copy in plain:
        copy.start()
    heat = sst[...].reshape(864, 128)
    for k in range(3):
        picked = lax.dot_general(one_hot_slots(dd, dt, k), heat, TN, preferred_element_type=F32)
        sel[k * 128 : (k + 1) * 128, :] = picked.astype(BF)

    row = lax.broadcasted_iota(jnp.int32, (16, 128), 0)
    even = (row & 1) == 0
    ocean_out = lambda g: pltpu.make_async_copy(sea.at[pl.ds(g * 8, 8)], oce.at[pl.ds(g * 8, 8)], sem.at[6 + g])

    @pl.loop(0, 8, unroll=2)
    def _(g):
        v = g // 2
        for j in range(8):
            l = lax.rem(g, 2) * 8 + j
            c = coef[pl.ds(l, 1), :]
            sea[g * 8 + j] = ss[v, l] + jnp.concatenate([c, c], axis=1) * q[v]
        ocean_out(g).start()
        acc = jnp.zeros((16, 128), F32)
        t0 = pl.multiple_of(g * 16, 16)
        part = [sel[pl.ds(pl.multiple_of(k * 128 + t0, 16), 16), :] for k in range(3)]
        lhs = jnp.concatenate(part[:2], axis=1)
        last = part[2].astype(F32)
        split = jnp.concatenate([jnp.where(even, last, 0.0), jnp.where(even, 0.0, last)], axis=1).astype(BF)
        for j in range(0, 16, 4):
            quad = [[w[t0 + j + n, k] for k in range(3)] for n in range(4)]
            for h in range(2):
                p0, p1 = quad[2 * h], quad[2 * h + 1]
                block = jnp.concatenate([jnp.concatenate(p0[:2], axis=1), jnp.concatenate(p1[:2], axis=1)], axis=0)
                r = lax.dot_general(lhs, block, NT, preferred_element_type=F32)
                acc += jnp.where(row == j + 2 * h, r[:, :128], 0.0) + jnp.where(row == j + 2 * h + 1, r[:, 128:], 0.0)
            block = jnp.concatenate(
                [
                    jnp.concatenate([quad[0][2], quad[1][2]], axis=1),
                    jnp.concatenate([quad[2][2], quad[3][2]], axis=1),
                ],
                axis=0,
            )
            r = lax.dot_general(split, block, NT, preferred_element_type=F32)
            acc += jnp.where((row == j) | (row == j + 1), r[:, :128], 0.0)
            acc += jnp.where((row == j + 2) | (row == j + 3), r[:, 128:], 0.0)
        exs[pl.ds(t0, 16), :] = acc

    for h in range(2):
        at = slice(128 * h, 128 * h + 128)
        heat = exs[pl.ds(h, 64, stride=2), :]
        exd[:, at] = heat
        cold = stepped[2, 15, :, at]
        warm[:, at] = cold + 0.5 * (heat - cold)
    late = [
        pltpu.make_async_copy(exd, ex, sem.at[4]),
        pltpu.make_async_copy(warm, atm.at[2, 15], sem.at[5]),
    ]
    for copy in late:
        copy.start()
    for copy in plain + late:
        copy.wait()
    for g in range(8):
        ocean_out(g).wait()


def remap_back(sst, dd, dt, q, coef, w, stepped, ss, flux):
    return pl.pallas_call(
        back_kernel,
        in_specs=[HERE] * 9,
        out_specs=[AWAY] * 4,
        out_shape=[
            jax.ShapeDtypeStruct((4, 16, 64, 256), F32),
            jax.ShapeDtypeStruct((64, 256), F32),
            jax.ShapeDtypeStruct((64, 48, 256), F32),
            jax.ShapeDtypeStruct((8, 48, 256), F32),
        ],
        scratch_shapes=[
            pltpu.VMEM((384, 128), BF),
            pltpu.VMEM((128, 128), F32),
            pltpu.VMEM((64, 256), F32),
            pltpu.VMEM((64, 256), F32),
            pltpu.VMEM((64, 48, 256), F32),
            pltpu.SemaphoreType.DMA((14,)),
        ],
        compiler_params=pltpu.CompilerParams(vmem_limit_bytes=16 * MIB),
        name="remap_back",
    )(sst, dd, dt, q, coef, w, stepped, ss, flux)


def per_device(atmos, ts, sw, w, dd, dt, mix_a, ocean, mask, seam, mix_o):
    dd, dt = dd.T, dt.T
    w, stepped, ss, q, flux, sst, coef = exchange(
        atmos, ocean, ts, sw, w, dd, dt, mask, seam.reshape(1, 256), mix_a, mix_o
    )
    atm, ex, oce, flux = remap_back(sst, dd, dt, q, coef, w, stepped, ss, flux)
    return atm, ex, oce.reshape(ocean.shape), flux


def solution(mesh):
    field = P(None, None, "lat", "lon")
    plane = P("lat", "lon")
    tiles = P(("lon", "lat"), None)
    return jax.shard_map(
        per_device,
        mesh=mesh,
        in_specs=(field, plane, plane, P(("lon", "lat"), None, None, None), tiles, tiles, P(), field, plane, P("lon"), P()),
        out_specs=(field, plane, field, P(None, "lat", "lon")),
        check_vma=False,
    )
```

```python
import functools

import jax
import jax.numpy as jnp
from jax import lax
from jax.experimental import pallas as pl
from jax.experimental.pallas import tpu as pltpu
from jax.sharding import PartitionSpec as P

F32 = jnp.float32
BF = jnp.bfloat16
MESH = pl.DeviceIdType.MESH
HIGHEST = lax.Precision.HIGHEST
NT = (((1,), (1,)), ((), ()))
TN = (((0,), (0,)), ((), ()))
N_LON = 8
N_LAT = 16
CHUNKS = 8
FIRST = 4
MIXED = 4
DETOUR = 2
MIB = 2**20


def flux_fields(u, v, ta, qa, ts, sw):
    speed = jnp.sqrt(u * u + v * v + 1.0)
    soft = jnp.maximum(qa, 0.0) + jnp.log1p(jnp.exp(-jnp.abs(qa)))
    return [
        0.8 * speed * u,
        0.8 * speed * v,
        0.6 * speed * (ts - ta),
        0.5 * speed * (0.4 * jnp.exp(0.5 * ts) - qa),
        0.3 * (ta - ts) * (2.0 + jnp.tanh(ta)),
        sw * (0.9 - 0.1 * jnp.tanh(qa)),
        soft,
        0.3 * speed * speed,
    ]


def slot_rows(owner, tile):
    lon = lax.axis_index("lon")
    lat = lax.axis_index("lat")
    lon_offset = ((owner >> 4) - lon + 1) & 7
    lat_offset = (owner & 15) - lat + 1
    return (lon_offset * 3 + lat_offset) * 96 + tile


def one_hot_slots(dd, dt, k):
    slot = slot_rows(dd[k : k + 1, :], dt[k : k + 1, :])
    rows = lax.broadcasted_iota(jnp.int32, (864, 128), 0)
    return jnp.where(slot == rows, 1.0, 0.0).astype(BF)


HERE = pl.BlockSpec(memory_space=pltpu.VMEM)
AWAY = pl.BlockSpec(memory_space=pltpu.HBM)


def step(x, rate):
    rows, lanes = x.shape
    around = pltpu.roll(x, 1, 0) + pltpu.roll(x, rows - 1, 0) + pltpu.roll(x, 1, 1) + pltpu.roll(x, lanes - 1, 1)
    return (1.0 - 4.0 * rate) * x + rate * around


def step_from(x, around, rate):
    return (1.0 - 4.0 * rate) * x + rate * around


def unpacked(from_left, from_right, n):
    lane = lax.broadcasted_iota(jnp.int32, from_left.shape, 1)
    right = pltpu.roll(from_right, (128 - 2 * n) & 127, 1)
    left = pltpu.roll(from_left, 126 - 2 * n, 1)
    return jnp.where(lane < 2, right, jnp.where(lane >= 126, left, 0.0))


def two_rows(at, first, second):
    rows = lax.broadcasted_iota(jnp.int32, (8, first.shape[1]), 0)
    return jnp.where(rows == at, first, jnp.where(rows == at + 1, second, 0.0))


def framed(x, south, north, third):
    return jnp.concatenate([jnp.concatenate([south, x, north], axis=0), third], axis=1)


def lateral(parts, tri):
    rows = parts[0].shape[0]
    total = jnp.dot(jnp.concatenate(parts, axis=0).astype(BF), tri, preferred_element_type=F32)
    return [total[n * rows : (n + 1) * rows] for n in range(len(parts))]


def near(x, inner, above, below, ghost):
    rows = x.shape[0]
    lane = lax.broadcasted_iota(jnp.int32, (rows, 128), 1)
    row = lax.broadcasted_iota(jnp.int32, (8, 256), 0)
    up = pltpu.roll(x, 1, 0)
    down = pltpu.roll(x, rows - 1, 0)
    up = jnp.concatenate([jnp.where(row == 0, above, up[0:8]), up[8:]], axis=0)
    down = jnp.concatenate([down[: rows - 8], jnp.where(row == 7, below, down[rows - 8 :])], axis=0)
    edges = jnp.concatenate([jnp.where(lane == 0, ghost, 0.0), jnp.where(lane == 127, ghost, 0.0)], axis=1)
    return up + down + inner + edges


def beside(x, ghost, lane):
    t0, t1 = x[:, 0:128], x[:, 128:256]
    r0, r1 = pltpu.roll(t0, 1, 1), pltpu.roll(t1, 1, 1)
    l0, l1 = pltpu.roll(t0, 127, 1), pltpu.roll(t1, 127, 1)
    first, last = lane == 0, lane == 127
    s0 = jnp.where(first, ghost, r0) + jnp.where(last, l1, l0)
    s1 = jnp.where(first, r0, r1) + jnp.where(last, ghost, l1)
    return jnp.concatenate([s0, s1], axis=1)


def beside_packed(left, right, own_left, own_right, odd):
    centre = jnp.where(odd, left, right)
    outer = jnp.where(odd, pltpu.roll(left, 1, 1), pltpu.roll(right, 127, 1))
    inner = jnp.where(odd, pltpu.roll(own_left, 1, 1), pltpu.roll(own_right, 127, 1))
    return centre, outer + inner


def corner_lanes(centre, row):
    lane = lax.broadcasted_iota(jnp.int32, (64, 128), 1)
    field = lax.broadcasted_iota(jnp.int32, (64, 128), 0)
    line = jnp.broadcast_to(centre[row : row + 1, :], (64, 128))
    left = jnp.sum(jnp.where(lane == 2 * field + 1, line, 0.0), axis=1, keepdims=True)
    right = jnp.sum(jnp.where(lane == 2 * field, line, 0.0), axis=1, keepdims=True)
    return jnp.where(lane == 0, left, jnp.where(lane == 127, right, 0.0))


def spread(mixer, cells):
    size = 16 * cells
    pick = lambda dim: jnp.where(
        lax.broadcasted_iota(jnp.int32, (size, 16) if dim == 0 else (16, size), dim) // cells
        == lax.broadcasted_iota(jnp.int32, (size, 16) if dim == 0 else (16, size), 1 - dim),
        1.0,
        0.0,
    )
    dot = functools.partial(jnp.dot, precision=HIGHEST, preferred_element_type=F32)
    full = dot(dot(pick(0), mixer), pick(1))
    r = lax.broadcasted_iota(jnp.int32, (size, size), 0) % cells
    c = lax.broadcasted_iota(jnp.int32, (size, size), 1) % cells
    return jnp.where(r == c, full, 0.0)


def halves(x):
    high = x.astype(BF)
    return high, (x - high.astype(F32)).astype(BF)


def dot3(lhs_high, lhs_low, x):
    high, low = halves(x)
    dot = functools.partial(jnp.dot, preferred_element_type=F32)
    return dot(lhs_high, high) + dot(lhs_high, low) + dot(lhs_low, high)


def exchange_kernel(
    atm_far, oce_far, ts_far, sw_far, dd_far, dt_far, mask_far, w_far, seam, mix_a, mix_o,
    w_here, stepped, ss, q_out, f_out, sst_out, coef_out,
    atm, oce, surf, heat, sun, dd, dt, mask, ft, terms, oh, tb, rbuf, rows, cols, corn, send,
    bc, pr, ro, rd, rl, sl, rr, cc, kk, fr, rrf, cea, ceo, mext, fold, gsa, gso, gea, geo, tri,
    ka, ko, fs, dr_s, dr_r, dc_s, dc_r, dk_r, fd, drf, ced, gd, sst_s, sst_r,
    sem, lsem, ssem, rsem,
):
    lon = lax.axis_index("lon")
    lat = lax.axis_index("lat")
    side = lax.rem(lat, 2)
    partner = lat + 1 - 2 * side
    outer = lat - 1 + 2 * side
    has_outer = jnp.logical_and(outer >= 0, outer < N_LAT)
    has_south = lat > 0
    has_north = lat < N_LAT - 1
    top = lat == N_LAT - 1
    always = lat >= 0
    lon_at = lambda d: lax.rem(lon + d + N_LON, N_LON)

    def lat_ok(d):
        return always if d == 0 else (has_south if d < 0 else has_north)

    def send_to(cond, src, dst, n, m, dev_lon, dev_lat):
        copy = pltpu.make_async_remote_copy(
            src_ref=src, dst_ref=dst, send_sem=ssem.at[n], recv_sem=rsem.at[m],
            device_id=(dev_lon, dev_lat), device_id_type=MESH,
        )

        @pl.when(cond)
        def _():
            copy.start()

        def finish():
            @pl.when(cond)
            def _():
                copy.wait_send()

        pending.append(finish)

    def arrive(cond, dst, m):
        @pl.when(cond)
        def _():
            pltpu.make_async_remote_copy(
                src_ref=dst, dst_ref=dst, send_sem=ssem.at[0], recv_sem=rsem.at[m],
                device_id=(lon, partner), device_id_type=MESH,
            ).wait_recv()

    pending = []
    barrier = pltpu.get_barrier_semaphore()
    around = [(dl, dn) for dl in (-1, 0, 1) for dn in (-1, 0, 1) if (dl, dn) != (0, 0)]
    for dl, dn in around:

        @pl.when(lat_ok(dn))
        def _(dl=dl, dn=dn):
            pl.semaphore_signal(barrier, inc=1, device_id=(lon_at(dl), lat + dn), device_id_type=MESH)

    @pl.when(top)
    def _():
        for d in range(2, N_LON - 1):
            pl.semaphore_signal(barrier, inc=1, device_id=(lon_at(d), lat), device_id_type=MESH)

    chunk = 128 // CHUNKS
    copies = [
        pltpu.make_async_copy(atm_far.at[:, 15], surf, sem.at[0]),
        pltpu.make_async_copy(ts_far, heat, sem.at[1]),
        pltpu.make_async_copy(sw_far, sun, sem.at[2]),
        pltpu.make_async_copy(mask_far, mask, sem.at[5 + CHUNKS]),
    ]
    targets = [
        pltpu.make_async_copy(dd_far, dd, sem.at[6 + CHUNKS]),
        pltpu.make_async_copy(dt_far, dt, sem.at[7 + CHUNKS]),
    ]
    for copy in targets:
        copy.start()
    weights = lambda i: pltpu.make_async_copy(
        w_far.at[pl.ds(i * chunk, chunk)], w_here.at[pl.ds(i * chunk, chunk)], sem.at[3 + i]
    )
    fields = [
        pltpu.make_async_copy(atm_far, atm, sem.at[3 + CHUNKS]),
        pltpu.make_async_copy(oce_far, oce, sem.at[4 + CHUNKS]),
    ]
    for copy in copies:
        copy.start()
    for copy in fields:
        copy.start()
    for i in range(CHUNKS):
        weights(i).start()

    for copy in targets:
        copy.wait()
    for k in range(3):
        oh[:, k * 128 : (k + 1) * 128] = one_hot_slots(dd, dt, k)
    for copy in copies:
        copy.wait()
    for f, val in enumerate(flux_fields(surf[0], surf[1], surf[2], surf[3], heat[...], sun[...])):
        val = val.astype(BF).astype(F32)
        ft[pl.ds(f, 64, stride=16), :] = val[:, :128]
        ft[pl.ds(8 + f, 64, stride=16), :] = val[:, 128:]

    group = lax.broadcasted_iota(jnp.int32, (32, 128), 0)
    even = (group & 8) == 0

    def remap_chunk(i):
        weights(i).wait()
        for j in range(0, chunk, 4):
            t = i * chunk + j
            a = ft[pl.ds(pl.multiple_of(t * 8, 32), 32), :]
            lhs = jnp.concatenate([jnp.where(even, a, 0.0), jnp.where(even, 0.0, a)], axis=1).astype(BF)
            quad = [[w_here[t + q, k] for k in range(3)] for q in range(4)]
            for h in range(2):
                p, q = quad[2 * h], quad[2 * h + 1]
                block = jnp.concatenate([jnp.concatenate(p[:2], axis=1), jnp.concatenate(q[:2], axis=1)], axis=0)
                r = jnp.dot(lhs[16 * h : 16 * h + 16], block, preferred_element_type=F32)
                for k in range(2):
                    terms[pl.ds(pl.multiple_of((k * 128 + t + 2 * h) * 8, 16), 16), :] = r[:, k * 128 : (k + 1) * 128]
            block = jnp.concatenate(
                [
                    jnp.concatenate([quad[0][2], quad[2][2]], axis=1),
                    jnp.concatenate([quad[1][2], quad[3][2]], axis=1),
                ],
                axis=0,
            )
            r = jnp.dot(lhs, block, preferred_element_type=F32)
            at = pl.multiple_of((256 + t) * 8, 32)
            terms[pl.ds(at, 16), :] = r[:16, :128]
            terms[pl.ds(at + 16, 16), :] = r[16:, 128:]

    for copy in fields:
        copy.wait()
    lane_a = lax.broadcasted_iota(jnp.int32, (64, 128), 1) >> 1
    lane_o = lax.broadcasted_iota(jnp.int32, (48, 128), 1) >> 1
    za = jnp.zeros((64, 128), F32)
    zo = jnp.zeros((48, 128), F32)

    @pl.loop(0, 16, init_carry=(za, za, zo, zo))
    def packed(l, carry):
        left_a, right_a, left_o, right_o = carry
        for v in range(4):
            n = v * 16 + l
            ahead = 2 * n
            back = (2 * n + 2) & 127
            left_a = jnp.where(lane_a == n, pltpu.roll(atm[v, l, :, 0:128], ahead, 1), left_a)
            right_a = jnp.where(lane_a == n, pltpu.roll(atm[v, l, :, 128:256], back, 1), right_a)
            left_o = jnp.where(lane_o == n, pltpu.roll(oce[v, l, :, 0:128], ahead, 1), left_o)
            right_o = jnp.where(lane_o == n, pltpu.roll(oce[v, l, :, 128:256], back, 1), right_o)
            for e in range(2):
                rbuf[e, pl.ds(n, 1), :] = atm[v, l, e : e + 1, :]
                rbuf[2 + e, pl.ds(n, 1), :] = atm[v, l, 62 + e : 63 + e, :]
                rbuf[e, pl.ds(64 + n, 1), :] = oce[v, l, e : e + 1, :]
                rbuf[2 + e, pl.ds(64 + n, 1), :] = oce[v, l, 46 + e : 47 + e, :]
        return left_a, right_a, left_o, right_o

    sea = mask[...].astype(F32)
    for a in range(2):
        cols_a, cols_o = packed[a], packed[2 + a]
        cols[a, 0:64, :] = cols_a.astype(BF)
        cols[a, 64:112, :] = cols_o.astype(BF)
        cols[a, 112:160, :] = sea[:, 128 * a : 128 * a + 128].astype(BF)
        corn[2 * a, 0:16, :] = cols_a[0:16].astype(BF)
        corn[2 * a, 16:32, :] = cols_o[0:16].astype(BF)
        corn[2 * a + 1, 0:16, :] = cols_a[48:64].astype(BF)
        corn[2 * a + 1, 16:32, :] = cols_o[32:48].astype(BF)
    for e in range(2):
        for b in range(2):
            r = 46 * b + e
            rbuf[2 * b + e, 128:144, :] = jnp.broadcast_to(sea[r : r + 1, :], (16, 256))
    rows[...] = rbuf[...].astype(BF)

    @pl.when(top)
    def _():
        pl.semaphore_wait(barrier, 5 + 5)

    @pl.when(lat == 0)
    def _():
        pl.semaphore_wait(barrier, 5)

    @pl.when(jnp.logical_and(has_south, has_north))
    def _():
        pl.semaphore_wait(barrier, 8)

    direction = {pair: n for n, pair in enumerate(around)}

    def halo(first, rows_s, rows_r, cols_s, cols_r, corn_s, corn_r):
        for dl, dn in around:
            n = first + direction[(dl, dn)]
            back = first + direction[(-dl, -dn)]
            if dl == 0:
                src, dst = rows_s(max(dn, 0)), rows_r(max(-dn, 0))
            elif dn == 0:
                src, dst = cols_s(max(dl, 0)), cols_r(max(-dl, 0))
            else:
                src, dst = corn_s(max(dl, 0), max(dn, 0)), corn_r(max(-dl, 0), max(-dn, 0))
            send_to(lat_ok(dn), src, dst, n, back, lon_at(dl), lat + dn)

    def halo_arrive(first, rows_r, cols_r, corn_r):
        for dl, dn in around:
            n = first + direction[(dl, dn)]
            if dl == 0:
                dst = rows_r(max(dn, 0))
            elif dn == 0:
                dst = cols_r(max(dl, 0))
            else:
                dst = corn_r(max(dl, 0), max(dn, 0))
            arrive(lat_ok(dn), dst, n)

    def ring(first, src, landing):
        for d in range(1, N_LON):
            send_to(top, src, landing.at[lon], first + d, first + lon, lon_at(d), lat)

    def ring_arrive(first, landing):
        for d in range(1, N_LON):
            arrive(top, landing.at[lon_at(d)], first + lon_at(d))

    rows_r = lambda b: rr.at[b]
    cols_r = lambda a: cc.at[a]
    corn_r = lambda a, b: kk.at[2 * a + b]
    halo(0, lambda b: rows.at[pl.ds(2 * b, 2)], rows_r, lambda a: cols.at[a], cols_r, lambda a, b: corn.at[2 * a + b], corn_r)
    fold_src = rows.at[pl.ds(2, 2), pl.ds(64, 80)]
    ring(8, fold_src, fr)
    own_fold = pltpu.make_async_copy(fold_src, fr.at[lon], lsem.at[0])

    @pl.when(top)
    def _():
        own_fold.start()

    @pl.loop(0, CHUNKS)
    def _(i):
        remap_chunk(i)

    for f in range(8):
        tb[:, f * 128 : (f + 1) * 128] = terms[pl.ds(f, 384, stride=8), :].astype(BF)
    for g in range(4):
        res = jnp.dot(oh[...], tb[:, g * 256 : (g + 1) * 256], preferred_element_type=F32)
        for o in range(9):
            for b in range(2):
                send[o, 2 * g + b] = res[o * 96 : (o + 1) * 96, b * 128 : (b + 1) * 128].astype(BF)


    for dl in (0, 2, 1):
        send_to(always, send.at[dl * 3 + 2 - 2 * side], pr.at[dl], 16 + dl, 16 + dl, lon, partner)
    straight = pl.ds(DETOUR, 8 - DETOUR)
    for n, dl in enumerate((0, 2)):
        block = dl * 3 + 2 * side
        send_to(has_outer, send.at[block, pl.ds(0, DETOUR)], rd.at[n], 48 + n, 48 + n, lon, outer)
        send_to(has_outer, send.at[block, straight], ro.at[dl, straight], 19 + dl, 19 + dl, lon_at(dl - 1), outer)
    send_to(has_outer, send.at[3 + 2 * side], ro.at[1], 20, 20, lon, outer)

    @pl.when(jnp.logical_not(has_outer))
    def _():
        ro[...] = jnp.zeros_like(ro)
        rd[...] = jnp.zeros_like(rd)

    for dl in (0, 2):
        ro[dl, 0:DETOUR] = jnp.zeros((DETOUR,) + ro.shape[2:], BF)

    for b, cond in ((0, has_south), (1, has_north)):

        @pl.when(jnp.logical_not(cond))
        def _(b=b):
            rr[b] = jnp.zeros(rr.shape[1:], BF)
            dr_r[b] = jnp.zeros(dr_r.shape[1:], BF)
            for a in range(2):
                kk[2 * a + b] = jnp.zeros(kk.shape[1:], BF)
                dk_r[2 * a + b] = jnp.zeros(dk_r.shape[1:], BF)
            for dl in range(3):
                sst_r[dl * 3 + 2 * b] = jnp.zeros(sst_r.shape[1:], BF)

    ma = mix_a[...]
    mo = mix_o[...]
    dot = functools.partial(jnp.dot, precision=HIGHEST, preferred_element_type=F32)
    ma2 = dot(ma, ma)
    mo2 = dot(mo, mo)
    ka[0], ka[1] = halves(spread(ma2, 16))
    ko[0, :, 0:128], ko[1, :, 0:128] = halves(spread(mo2, 8))
    ko[0, :, 128:256], ko[1, :, 128:256] = halves(spread(mo, 8))
    coef = jnp.broadcast_to(mo2[:, 0:1], (16, 128))
    coef_out[...] = coef

    @pl.when(top)
    def _():
        lane = lax.broadcasted_iota(jnp.int32, (1, 384), 1)
        column = lon * 256 + jnp.where(lane < 320, lane, lane - 384)
        pole = seam[0:1, 0:1] + lon * 256
        source = (pole - column) & 2047
        for j in range(8):
            fold[j * 256 : (j + 1) * 256, :] = jnp.where(
                lax.broadcasted_iota(jnp.int32, (256, 384), 0) + j * 256 == source, 1.0, 0.0
            ).astype(BF)

    halo_arrive(0, rows_r, cols_r, corn_r)
    for b in range(2):
        for e in range(2):
            rrf[b, e] = rr[b, e].astype(F32)
    for a in range(2):
        side_cols = cc[a].astype(F32)
        ks = kk[2 * a].astype(F32)
        kn = kk[2 * a + 1].astype(F32)
        cea[a, 0:8, :] = ks[8:16]
        cea[a, 8:72, :] = side_cols[0:64]
        cea[a, 72:80, :] = kn[0:8]
        ceo[a, 0:8, :] = ks[24:32]
        ceo[a, 8:56, :] = side_cols[64:112]
        ceo[a, 56:64, :] = kn[16:24]

    @pl.when(top)
    def _():
        own_fold.wait()
        ring_arrive(8, fr)
        total = jnp.zeros((160, 384), F32)
        for j in range(8):
            total += jnp.dot(fr[j].reshape(160, 256), fold[j * 256 : (j + 1) * 256, :], preferred_element_type=F32)
        n = lax.broadcasted_iota(jnp.int32, (80, 384), 0)
        sign = jnp.where(jnp.logical_and(n >= 32, n < 64), -1.0, 1.0)
        for e in range(2):
            ghost = total[80 * (1 - e) : 80 * (2 - e)] * sign
            if e == 0:
                beyond = ghost[0:64, 256:384]
            rrf[1, e, 64:144, :] = ghost[:, 0:256]
        lane = lax.broadcasted_iota(jnp.int32, (64, 128), 1)
        field = lax.broadcasted_iota(jnp.int32, (64, 128), 0)
        both = jnp.where(lane == 2 * field + 1, beyond[:, 127:128], jnp.where(lane == 2 * field, beyond[:, 0:1], 0.0))
        both = jnp.sum(both, axis=0, keepdims=True)
        ceo[0, 56:57, :] = both
        ceo[1, 56:57, :] = both

    lane_m = lax.broadcasted_iota(jnp.int32, (48, 128), 1)
    sea = mask[...].astype(F32)
    sea_left = cc[0, 112:160, :].astype(F32)
    sea_right = cc[1, 112:160, :].astype(F32)
    third = jnp.where(lane_m < 2, sea_right, jnp.where(lane_m >= 126, sea_left, 0.0))
    none = jnp.zeros((8, 128), F32)
    mext[...] = framed(
        sea,
        two_rows(6, rrf[0, 0, 128:129, :], rrf[0, 1, 128:129, :]),
        two_rows(0, rrf[1, 0, 128:129, :], rrf[1, 1, 128:129, :]),
        jnp.concatenate([none, third, none], axis=0),
    )
    lane_f = lax.broadcasted_iota(jnp.int32, (64, 128), 1)

    def outside(ce, own_at, rows, at, rate, sea_side, sea_rows):
        odd = (lax.broadcasted_iota(jnp.int32, (rows + 16, 128), 1) & 1) == 1
        own = [
            jnp.concatenate([none, cols[a, own_at : own_at + rows, :].astype(F32), none], axis=0)
            for a in range(2)
        ]
        centre, lateral = beside_packed(ce[0], ce[1], own[0], own[1], odd)
        y = step_from(centre, pltpu.roll(centre, 1, 0) + pltpu.roll(centre, rows + 15, 0) + lateral, rate)
        x_side, y_side = centre[8 : 8 + rows], y[8 : 8 + rows]
        pack = lambda x: pltpu.roll(x, 127, 1)
        sides = [pack(x_side), pack(y_side if sea_side is None else y_side * sea_side)]
        if sea_side is not None:
            sides.append(pack(x_side - x_side * sea_side))
        ends = []
        for b in range(2):
            near_row = rrf[b, 1 - b, at : at + 64, :]
            far_row = rrf[b, b, at : at + 64, :]
            own_row = rows_in[2 * b + b, at : at + 64, :].astype(F32)
            ghost = corner_lanes(centre, 7 if b == 0 else rows + 8)
            z = step_from(near_row, far_row + own_row + beside(near_row, ghost, lane_f), rate)
            if sea_side is None:
                ends.append([jnp.where(has_south if b == 0 else has_north, z, 0.0)])
            else:
                ends.append([z * sea_rows[b], near_row - near_row * sea_rows[b]])
        return sides, ends

    rows_in = rows
    odd_m = (lane_m & 1) == 1
    sea_side = jnp.where(odd_m, jnp.broadcast_to(sea_left[:, 127:128], (48, 128)), jnp.broadcast_to(sea_right[:, 0:1], (48, 128)))
    sides, ends = outside(ceo, 64, 48, 64, 0.2, sea_side, [rrf[0, 1, 128:129, :], rrf[1, 0, 128:129, :]])
    for n in range(3):
        gso[n] = sides[n]
    for b in range(2):
        for n in range(2):
            geo[b, n] = ends[b][n]
    sides, ends = outside(cea, 0, 64, 0, 0.15, None, None)
    for n in range(2):
        gsa[n] = sides[n]
    for b in range(2):
        gea[b] = ends[b][0]

    r256 = lax.broadcasted_iota(jnp.int32, (256, 256), 0)
    c256 = lax.broadcasted_iota(jnp.int32, (256, 256), 1)
    tri[...] = jnp.where(jnp.logical_or(r256 == c256 + 1, r256 + 1 == c256), 1.0, 0.0).astype(BF)

    for dl in (0, 2, 1):
        arrive(always, pr.at[dl], 16 + dl)
    for n, dl in enumerate((0, 2)):

        @pl.loop(DETOUR, 8, unroll=3)
        def _(f, n=n, dl=dl):
            sl[n, f] = (send[3 * dl + 1, f].astype(F32) + pr[dl, f].astype(F32)).astype(BF)

        send_to(always, sl.at[n, straight], rl.at[n, straight], 22 + n, 22 + n, lon_at(dl - 1), lat)
    for n, dl in enumerate((0, 2)):
        arrive(has_outer, rd.at[n], 48 + n)
        for f in range(DETOUR):
            total = send[3 * dl + 1, f].astype(F32) + pr[dl, f].astype(F32) + rd[n, f].astype(F32)
            sl[n, f] = total.astype(BF)
        bent = pl.ds(0, DETOUR)
        send_to(always, sl.at[n, bent], rl.at[n, bent], 50 + n, 50 + n, lon_at(dl - 1), lat)

    @pl.loop(0, 8)
    def _(i):
        v = i // 2
        first = pl.multiple_of(lax.rem(i, 2) * 8, 8)
        lines = pl.ds(pl.multiple_of(i * 8, 8), 8)
        far = pl.ds(pl.multiple_of(64 + i * 8, 8), 8)
        turned = lambda k, j: pltpu.roll(gso[k], (128 - 2 * (i * 8 + j)) & 127, 1)
        wet_here = mext[8:56, 0:256]
        south, north = rrf[0, 1, far, :], rrf[1, 0, far, :]
        xs = [oce[v, first + j] for j in range(8)]
        inner = lateral(xs, tri[...])
        a, c = [], []
        for j, x in enumerate(xs):
            around = near(x, inner[j], south[j : j + 1], north[j : j + 1], turned(0, j))
            a.append(wet_here * step_from(x, around, 0.2))
            c.append(x - wet_here * x)
        for k, parts in enumerate((a, c)):
            inner = lateral(parts, tri[...])
            south, north = geo[0, k, lines, :], geo[1, k, lines, :]
            for j, x in enumerate(parts):
                around = near(x, inner[j], south[j : j + 1], north[j : j + 1], turned(1 + k, j))
                bc[v, 16 * k + first + j] = step_from(x, around, 0.2)

    @pl.loop(0, 24, unroll=6)
    def _(n):
        v = n // 6
        at = pl.multiple_of(lax.rem(n, 6) * 8, 8)
        mixed = dot3(ko[0], ko[1], bc[v, :, pl.ds(at, 8), :].reshape(256, 256)).reshape(16, 8, 256)
        wet = mask[pl.ds(at, 8), :] > 0
        ss[v, :, pl.ds(at, 8), :] = jnp.where(wet[None], mixed, oce[v, :, pl.ds(at, 8), :])

    def atm_group(i):
        v = i // 2
        first = pl.multiple_of(lax.rem(i, 2) * 8, 8)
        lines = pl.ds(pl.multiple_of(i * 8, 8), 8)
        turned = lambda k, j: pltpu.roll(gsa[k], (128 - 2 * (i * 8 + j)) & 127, 1)
        parts = [atm[v, first + j] for j in range(8)]
        ends = ((rrf[0, 1, lines, :], rrf[1, 0, lines, :]), (gea[0, lines, :], gea[1, lines, :]))
        for k in range(2):
            inner = lateral(parts, tri[...])
            south, north = ends[k]
            parts = [
                step_from(x, near(x, inner[j], south[j : j + 1], north[j : j + 1], turned(k, j)), 0.15)
                for j, x in enumerate(parts)
            ]
        for j, y in enumerate(parts):
            stepped[v, first + j] = y

    def atm_mix(n):
        v = n // 4
        at = pl.multiple_of(lax.rem(n, 4) * 16, 16)
        mixed = dot3(ka[0], ka[1], stepped[v, :, pl.ds(at, 16), :].reshape(256, 256))
        stepped[v, :, pl.ds(at, 16), :] = mixed.reshape(16, 16, 256)

    @pl.loop(0, FIRST)
    def _(i):
        atm_group(i)

    @pl.loop(0, MIXED, unroll=4)
    def _(n):
        atm_mix(n)

    for dl in (0, 2):
        arrive(has_outer, ro.at[dl, straight], 19 + dl)
    arrive(has_outer, ro.at[1], 20)
    for n in range(2):
        arrive(always, rl.at[n, straight], 22 + n)
        arrive(always, rl.at[n, pl.ds(0, DETOUR)], 50 + n)

    @pl.loop(0, 8, unroll=4)
    def _(f):
        parts = [send[4, f], pr[1, f], rl[0, f], rl[1, f], ro[0, f], ro[1, f], ro[2, f]]
        total = functools.reduce(lambda x, y: x + y, [p.astype(F32) for p in parts])
        fs[pl.ds(pl.multiple_of(f * 96, 8), 96), :] = total

    flux = []
    for f in range(8):
        value = sea * jnp.concatenate([fs[pl.ds(f * 96 + h, 48, stride=2), :] for h in range(2)], axis=1)
        f_out[f] = value
        flux.append(value)
    forcing = [
        0.2 * sea * (flux[5] - flux[2] - flux[3] - flux[4]),
        0.2 * sea * (flux[3] - flux[6]),
        sea * (0.3 * flux[0] - 0.1 * flux[7] * oce[2, 0]),
        sea * (0.3 * flux[1] - 0.1 * flux[7] * oce[3, 0]),
    ]

    left = jnp.zeros((48, 128), F32)
    right = jnp.zeros((48, 128), F32)
    edge = [[jnp.zeros((16, 256), F32) for _ in range(2)] for _ in range(2)]
    row_16 = lax.broadcasted_iota(jnp.int32, (16, 256), 0)
    for f, d in enumerate(forcing):
        left = jnp.where((lane_m >> 1) == f, pltpu.roll(d[:, 0:128], 2 * f, 1) if f else d[:, 0:128], left)
        right = jnp.where((lane_m >> 1) == f, pltpu.roll(d[:, 128:256], 2 * f + 2, 1), right)
        for b in range(2):
            for e in range(2):
                r = 46 * b + e
                edge[b][e] = jnp.where(row_16 == f, d[r : r + 1, :], edge[b][e])
    dc_s[0] = left.astype(BF)
    dc_s[1] = right.astype(BF)
    for b in range(2):
        for e in range(2):
            dr_s[b, 16 * e : 16 * e + 16, :] = edge[b][e].astype(BF)
    rows_r = lambda b: dr_r.at[b]
    cols_r = lambda a: dc_r.at[a]
    corn_r = lambda a, b: dk_r.at[2 * a + b]
    halo(24, lambda b: dr_s.at[b], rows_r, lambda a: dc_s.at[a], cols_r,
         lambda a, b: dc_s.at[a, pl.ds(32 * b, 16)], corn_r)
    ring(32, dr_s.at[1], fd)

    @pl.when(top)
    def _():
        fd[lon] = dr_s[1]

    @pl.loop(FIRST, 8)
    def _(i):
        atm_group(i)

    halo_arrive(24, rows_r, cols_r, corn_r)
    for b in range(2):
        drf[b] = dr_r[b].astype(F32)
    for a in range(2):
        ced[a, 0:8, :] = dk_r[2 * a].astype(F32)[8:16]
        ced[a, 8:56, :] = dc_r[a].astype(F32)
        ced[a, 56:64, :] = dk_r[2 * a + 1].astype(F32)[0:8]

    @pl.when(top)
    def _():
        ring_arrive(32, fd)
        total = jnp.zeros((32, 384), F32)
        for j in range(8):
            total += jnp.dot(fd[j], fold[j * 256 : (j + 1) * 256, :], preferred_element_type=F32)
        n = lax.broadcasted_iota(jnp.int32, (16, 384), 0)
        sign = jnp.where(n >= 2, -1.0, 1.0)
        for e in range(2):
            gd[e] = total[16 * (1 - e) : 16 * (2 - e)] * sign
            drf[1, 16 * e : 16 * e + 16, :] = gd[e][:, 0:256]

    @pl.when(jnp.logical_not(top))
    def _():
        gd[...] = jnp.zeros_like(gd)

    m = mext[...]
    for f, d in enumerate(forcing):
        third = unpacked(ced[0], ced[1], f)
        north = jnp.where(top, two_rows(0, gd[0, f : f + 1, 256:384], gd[1, f : f + 1, 256:384]), third[56:64])
        x = framed(
            d,
            two_rows(6, drf[0, f : f + 1, :], drf[0, 16 + f : 17 + f, :]),
            two_rows(0, drf[1, f : f + 1, :], drf[1, 16 + f : 17 + f, :]),
            jnp.concatenate([third[0:56], north], axis=0),
        )
        q = sea * step(m * step(x, 0.2), 0.2)[8:56, 0:256]
        q_out[f] = q
        if f == 0:
            c00 = jnp.concatenate([coef[0:1, :], coef[0:1, :]], axis=1)
            heat = sea * (ss[0, 0] + c00 * q)
            for h in range(2):
                fs[pl.ds(h, 48, stride=2), :] = heat[:, 128 * h : 128 * h + 128]
            sst_s[...] = fs[0:96, :].astype(BF)
            for dl, dn in around:
                n = 40 + direction[(dl, dn)]
                back = 40 + direction[(-dl, -dn)]
                slot = (1 - dl) * 3 + 1 - dn
                send_to(lat_ok(dn), sst_s, sst_r.at[slot], n, back, lon_at(dl), lat + dn)
    @pl.loop(MIXED, 16, unroll=4)
    def _(n):
        atm_mix(n)

    for finish in pending[: -len(around)]:
        finish()
    sst_r[4] = sst_s[...]
    for dl, dn in around:
        arrive(lat_ok(dn), sst_r.at[(1 + dl) * 3 + 1 + dn], 40 + direction[(dl, dn)])
    sst_out[...] = sst_r[...]
    for finish in pending[-len(around) :]:
        finish()


def exchange(atm, oce, ts, sw, w, dd, dt, mask, seam, mix_a, mix_o):
    far = [pltpu.with_memory_space_constraint(x, pltpu.HBM) for x in (atm, oce, ts, sw, dd, dt, mask, w)]
    return pl.pallas_call(
        exchange_kernel,
        in_specs=[AWAY] * 8 + [HERE] * 3,
        out_specs=[HERE] * 7,
        out_shape=[
            pltpu.VMEM((128, 3, 128, 128), BF),
            pltpu.VMEM((4, 16, 64, 256), F32),
            pltpu.VMEM((4, 16, 48, 256), F32),
            pltpu.VMEM((4, 48, 256), F32),
            pltpu.VMEM((8, 48, 256), F32),
            pltpu.VMEM((9, 96, 128), BF),
            pltpu.VMEM((16, 128), F32),
        ],
        scratch_shapes=[
            pltpu.VMEM((4, 16, 64, 256), F32),
            pltpu.VMEM((4, 16, 48, 256), F32),
            pltpu.VMEM((4, 64, 256), F32),
            pltpu.VMEM((64, 256), F32),
            pltpu.VMEM((64, 256), F32),
            pltpu.VMEM((3, 128), jnp.int32),
            pltpu.VMEM((3, 128), jnp.int32),
            pltpu.VMEM((48, 256), jnp.int32),
            pltpu.VMEM((1024, 128), F32),
            pltpu.VMEM((3072, 128), F32),
            pltpu.VMEM((864, 384), BF),
            pltpu.VMEM((384, 1024), BF),
            pltpu.VMEM((4, 144, 256), F32),
            pltpu.VMEM((4, 144, 256), BF),
            pltpu.VMEM((2, 160, 128), BF),
            pltpu.VMEM((4, 32, 128), BF),
            pltpu.VMEM((9, 8, 96, 128), BF),
            pltpu.VMEM((4, 32, 48, 256), F32),
            pltpu.VMEM((3, 8, 96, 128), BF),
            pltpu.VMEM((3, 8, 96, 128), BF),
            pltpu.VMEM((2, DETOUR, 96, 128), BF),
            pltpu.VMEM((2, 8, 96, 128), BF),
            pltpu.VMEM((2, 8, 96, 128), BF),
            pltpu.VMEM((2, 2, 144, 256), BF),
            pltpu.VMEM((2, 160, 128), BF),
            pltpu.VMEM((4, 32, 128), BF),
            pltpu.VMEM((8, 2, 80, 256), BF),
            pltpu.VMEM((2, 2, 144, 256), F32),
            pltpu.VMEM((2, 80, 128), F32),
            pltpu.VMEM((2, 64, 128), F32),
            pltpu.VMEM((64, 384), F32),
            pltpu.VMEM((2048, 384), BF),
            pltpu.VMEM((2, 64, 128), F32),
            pltpu.VMEM((3, 48, 128), F32),
            pltpu.VMEM((2, 64, 256), F32),
            pltpu.VMEM((2, 2, 64, 256), F32),
            pltpu.VMEM((256, 256), BF),
            pltpu.VMEM((2, 256, 256), BF),
            pltpu.VMEM((2, 128, 256), BF),
            pltpu.VMEM((768, 128), F32),
            pltpu.VMEM((2, 32, 256), BF),
            pltpu.VMEM((2, 32, 256), BF),
            pltpu.VMEM((2, 48, 128), BF),
            pltpu.VMEM((2, 48, 128), BF),
            pltpu.VMEM((4, 16, 128), BF),
            pltpu.VMEM((8, 32, 256), BF),
            pltpu.VMEM((2, 32, 256), F32),
            pltpu.VMEM((2, 64, 128), F32),
            pltpu.VMEM((2, 16, 384), F32),
            pltpu.VMEM((96, 128), BF),
            pltpu.VMEM((9, 96, 128), BF),
            pltpu.SemaphoreType.DMA((8 + CHUNKS,)),
            pltpu.SemaphoreType.DMA((1,)),
            pltpu.SemaphoreType.DMA((52,)),
            pltpu.SemaphoreType.DMA((52,)),
        ],
        compiler_params=pltpu.CompilerParams(collective_id=0, has_side_effects=True, vmem_limit_bytes=36 * MIB),
        name="exchange",
    )(*far, seam, mix_a, mix_o)


def back_kernel(sst, dd, dt, q, coef, w, stepped, ss, flux, atm, ex, oce, f_out, sel, exs, exd, warm, sea, sem):
    plain = [
        pltpu.make_async_copy(flux, f_out, sem.at[0]),
        pltpu.make_async_copy(stepped.at[pl.ds(0, 2)], atm.at[pl.ds(0, 2)], sem.at[1]),
        pltpu.make_async_copy(stepped.at[2, pl.ds(0, 15)], atm.at[2, pl.ds(0, 15)], sem.at[2]),
        pltpu.make_async_copy(stepped.at[3], atm.at[3], sem.at[3]),
    ]
    for copy in plain:
        copy.start()
    heat = sst[...].reshape(864, 128)
    for k in range(3):
        picked = lax.dot_general(one_hot_slots(dd, dt, k), heat, TN, preferred_element_type=F32)
        sel[k * 128 : (k + 1) * 128, :] = picked.astype(BF)

    row = lax.broadcasted_iota(jnp.int32, (16, 128), 0)
    even = (row & 1) == 0
    ocean_out = lambda g: pltpu.make_async_copy(sea.at[pl.ds(g * 8, 8)], oce.at[pl.ds(g * 8, 8)], sem.at[6 + g])

    @pl.loop(0, 8, unroll=2)
    def _(g):
        v = g // 2
        for j in range(8):
            l = lax.rem(g, 2) * 8 + j
            c = coef[pl.ds(l, 1), :]
            sea[g * 8 + j] = ss[v, l] + jnp.concatenate([c, c], axis=1) * q[v]
        ocean_out(g).start()
        acc = jnp.zeros((16, 128), F32)
        t0 = pl.multiple_of(g * 16, 16)
        part = [sel[pl.ds(pl.multiple_of(k * 128 + t0, 16), 16), :] for k in range(3)]
        lhs = jnp.concatenate(part[:2], axis=1)
        last = part[2].astype(F32)
        split = jnp.concatenate([jnp.where(even, last, 0.0), jnp.where(even, 0.0, last)], axis=1).astype(BF)
        for j in range(0, 16, 4):
            quad = [[w[t0 + j + n, k] for k in range(3)] for n in range(4)]
            for h in range(2):
                p0, p1 = quad[2 * h], quad[2 * h + 1]
                block = jnp.concatenate([jnp.concatenate(p0[:2], axis=1), jnp.concatenate(p1[:2], axis=1)], axis=0)
                r = lax.dot_general(lhs, block, NT, preferred_element_type=F32)
                acc += jnp.where(row == j + 2 * h, r[:, :128], 0.0) + jnp.where(row == j + 2 * h + 1, r[:, 128:], 0.0)
            block = jnp.concatenate(
                [
                    jnp.concatenate([quad[0][2], quad[1][2]], axis=1),
                    jnp.concatenate([quad[2][2], quad[3][2]], axis=1),
                ],
                axis=0,
            )
            r = lax.dot_general(split, block, NT, preferred_element_type=F32)
            acc += jnp.where((row == j) | (row == j + 1), r[:, :128], 0.0)
            acc += jnp.where((row == j + 2) | (row == j + 3), r[:, 128:], 0.0)
        exs[pl.ds(t0, 16), :] = acc

    for h in range(2):
        at = slice(128 * h, 128 * h + 128)
        heat = exs[pl.ds(h, 64, stride=2), :]
        exd[:, at] = heat
        cold = stepped[2, 15, :, at]
        warm[:, at] = cold + 0.5 * (heat - cold)
    late = [
        pltpu.make_async_copy(exd, ex, sem.at[4]),
        pltpu.make_async_copy(warm, atm.at[2, 15], sem.at[5]),
    ]
    for copy in late:
        copy.start()
    for copy in plain + late:
        copy.wait()
    for g in range(8):
        ocean_out(g).wait()


def remap_back(sst, dd, dt, q, coef, w, stepped, ss, flux):
    return pl.pallas_call(
        back_kernel,
        in_specs=[HERE] * 9,
        out_specs=[AWAY] * 4,
        out_shape=[
            jax.ShapeDtypeStruct((4, 16, 64, 256), F32),
            jax.ShapeDtypeStruct((64, 256), F32),
            jax.ShapeDtypeStruct((64, 48, 256), F32),
            jax.ShapeDtypeStruct((8, 48, 256), F32),
        ],
        scratch_shapes=[
            pltpu.VMEM((384, 128), BF),
            pltpu.VMEM((128, 128), F32),
            pltpu.VMEM((64, 256), F32),
            pltpu.VMEM((64, 256), F32),
            pltpu.VMEM((64, 48, 256), F32),
            pltpu.SemaphoreType.DMA((14,)),
        ],
        compiler_params=pltpu.CompilerParams(vmem_limit_bytes=16 * MIB),
        name="remap_back",
    )(sst, dd, dt, q, coef, w, stepped, ss, flux)


def per_device(atmos, ts, sw, w, dd, dt, mix_a, ocean, mask, seam, mix_o):
    dd, dt = dd.T, dt.T
    w, stepped, ss, q, flux, sst, coef = exchange(
        atmos, ocean, ts, sw, w, dd, dt, mask, seam.reshape(1, 256), mix_a, mix_o
    )
    atm, ex, oce, flux = remap_back(sst, dd, dt, q, coef, w, stepped, ss, flux)
    return atm, ex, oce.reshape(ocean.shape), flux


def solution(mesh):
    field = P(None, None, "lat", "lon")
    plane = P("lat", "lon")
    tiles = P(("lon", "lat"), None)
    return jax.shard_map(
        per_device,
        mesh=mesh,
        in_specs=(field, plane, plane, P(("lon", "lat"), None, None, None), tiles, tiles, P(), field, plane, P("lon"), P()),
        out_specs=(field, plane, field, P(None, "lat", "lon")),
        check_vma=False,
    )
```
